32 devices in a mesh: sp: 16 (over z, x, core), tp: 2 (over y).
Axes of the slice: x: 2, y: 2, z: 4, core: 2. Of those that a mesh axis runs over, the one named last changes fastest.
Arguments:
- tokens: bfloat16 [3072, 1024], P('sp'), may hold values from -6 to 6
- segment_ids: int32 [3072], P('sp'), may hold values from 0 to 1, as said below
- lead_hours: float32 [2], replicated, may hold values from 0.06 to 1.68
- qkv_weight: bfloat16 [3, 1024, 1024], P(None, 'sp', 'tp'), may hold values from -0.25 to 0.25
- qv_bias: bfloat16 [2, 16, 64], P(None, 'tp', 'sp'), may hold values from -3 to 3
- proj_weight: bfloat16 [1024, 1024], P('tp', 'sp'), may hold values from -1.5 to 1.5
- proj_bias: bfloat16 [1024], P('sp'), may hold values from -2 to 2
- up_weight: bfloat16 [1024, 4096], P('sp', 'tp'), may hold values from -0.1875 to 0.1875
- up_bias: bfloat16 [64, 64], P('tp', 'sp'), may hold values from -2 to 2
- down_weight: bfloat16 [4096, 1024], P('tp', 'sp'), may hold values from -0.125 to 0.125
- down_bias: bfloat16 [1024], P('sp'), may hold values from -2 to 2
- norm1_gain: bfloat16 [1024], P('sp'), may hold values from 0.5 to 1.5
- norm1_bias: bfloat16 [1024], P('sp'), may hold values from -2 to 2
- norm2_gain: bfloat16 [1024], P('sp'), may hold values from 0.5 to 1.5
- norm2_bias: bfloat16 [1024], P('sp'), may hold values from -2 to 2
- lead_weight: bfloat16 [1024], P('sp'), may hold values from -3 to 3
- lead_bias: bfloat16 [1024], P('sp'), may hold values from -3 to 3
- out_grad: bfloat16 [3072, 1024], P('sp'), may hold values from -6 to 6
Outputs:
- block_out: bfloat16 [3072, 1024], P('sp')
- input_grad: float32 [3072, 1024], P('sp')
- grad_qkv_weight: float32 [3, 1024, 1024], P(None, 'sp', 'tp')
- grad_qv_bias: float32 [2, 16, 64], P(None, 'tp', 'sp')
- grad_proj_weight: float32 [1024, 1024], P('tp', 'sp')
- grad_proj_bias: float32 [1024], P('sp')
- grad_up_weight: float32 [1024, 4096], P('sp', 'tp')
- grad_up_bias: float32 [64, 64], P('tp', 'sp')
- grad_down_weight: float32 [4096, 1024], P('tp', 'sp')
- grad_down_bias: float32 [1024], P('sp')
- grad_norm1_gain: float32 [1024], P('sp')
- grad_norm1_bias: float32 [1024], P('sp')
- grad_norm2_gain: float32 [1024], P('sp')
- grad_norm2_bias: float32 [1024], P('sp')
- grad_lead_weight: float32 [1024], P('sp')
- grad_lead_bias: float32 [1024], P('sp')
The draws below stay inside these ranges and needn't reach their ends.
Inputs may be any that keep to these rules, and one draw needn't show every extreme that they name: `segment_ids`: sample 0 holds the first and the last patch: two runs at the two ends of the sequence. Samples 1 to 1 follow in order in between, each one run of 576 to 1152 patches, one of them exactly 1152; sample 0 holds all other patches.
All inputs are finite; a program needn't handle non-finite values.
Results may differ from the reference program's by a relative error of at most 0.025.
Values may be sent and summed in bfloat16 or wider, within the bound.
No kernel may reach another device: no remote copies, remote signals or barrier semaphores. Data moves between devices by JAX's collectives and lax.ppermute only.
A program may use at most 128 MiB of HBM per device.

```python
import math
import jax
import jax.numpy as jnp
from jax import lax

D = 1024
H = 16
HD = 64
FF = 4096
TOK_DEV = 192
TOKENS = 3072
NSHORT = 1
NSEG = 2


def draw_segment_ids(key, part):
    key = jax.random.fold_in(key, 11)
    key_len, key_pick, key_tail = jax.random.split(key, 3)
    shorts = jax.random.randint(key_len, (NSHORT,), 3 * TOK_DEV, 6 * TOK_DEV + 1)
    picked = jax.random.randint(key_pick, (), 0, NSHORT)
    shorts = jnp.where(jnp.arange(NSHORT) == picked, 6 * TOK_DEV, shorts)
    ends = jnp.cumsum(shorts)
    long_len = TOKENS - ends[NSHORT - 1]
    tail_len = jax.random.randint(key_tail, (), 1, long_len)
    head_len = long_len - tail_len
    position = jnp.arange(TOKENS)
    inner_pos = position - head_len
    sample_ids = 1 + jnp.sum(inner_pos[:, None] >= ends[None, :], axis=1)
    sample_ids = jnp.where((position < head_len) | (position >= TOKENS - tail_len), 0, sample_ids)
    return sample_ids.astype(jnp.int32)


def levels(key, dims, cuts, low, top_value):
    gain = 1.0
    for axis_at, shards_of in cuts:
        heights = jax.random.uniform(jax.random.fold_in(jax.random.fold_in(key, 6), axis_at), (shards_of,), jnp.float32, low / len(cuts), top_value / len(cuts))
        gain = gain * jnp.repeat(jnp.exp(heights), dims[axis_at] // shards_of).reshape((-1,) + (1,) * (len(dims) - 1 - axis_at))
    return gain


def noise(rng, shape, scale, limit, pieces=(), kind=jnp.bfloat16):
    loudness = levels(rng, shape, pieces, -0.22, 0.18) if pieces else 1.0
    drawn = jax.random.normal(rng, shape, jnp.float32) * scale * loudness
    return jnp.minimum(jnp.maximum(drawn, -limit), limit).astype(kind)


def setup_inputs(seed: int = 0) -> dict:
    key_of = jax.random.split(jax.random.key(seed), 19)
    tokens = noise(key_of[0], (TOKENS, D), 1.0, 6.0, ((0, 16),))
    segment_ids = draw_segment_ids(jax.random.fold_in(key_of[18], 71), 0)
    lead_hours = jnp.clip(jnp.exp(jax.random.uniform(key_of[2], (NSEG,), jnp.float32, math.log(0.06), math.log(1.68))), 0.06, 1.68)
    qkv_weight = noise(key_of[3], (3, D, D), (D // 2) ** -0.5, 0.25, ((1, 16), (2, 2)))
    qv_bias = noise(key_of[4], (2, H, HD), 0.5, 3.0, ((1, 2), (2, 16)))
    proj_weight = noise(key_of[5], (D, D), 16 ** -0.5, 1.5, ((0, 2), (1, 16)))
    proj_bias = noise(key_of[6], (D,), 0.3, 2.0, ((0, 16),))
    up_weight = noise(key_of[7], (D, FF), D ** -0.5, 0.1875, ((0, 16), (1, 2)))
    up_bias = noise(key_of[8], (FF // HD, HD), 0.3, 2.0, ((0, 2), (1, 16)))
    down_weight = noise(key_of[9], (FF, D), (FF // 2) ** -0.5, 0.125, ((0, 2), (1, 16)))
    down_bias = noise(key_of[10], (D,), 0.3, 2.0, ((0, 16),))
    norm1_gain = jnp.clip(1.0 + 0.1 * jax.random.normal(key_of[11], (D,), jnp.float32), 0.5, 1.5).astype(jnp.bfloat16)
    norm1_bias = noise(key_of[12], (D,), 0.3, 2.0, ((0, 16),))
    norm2_gain = jnp.clip(1.0 + 0.1 * jax.random.normal(key_of[13], (D,), jnp.float32), 0.5, 1.5).astype(jnp.bfloat16)
    norm2_bias = noise(key_of[14], (D,), 0.3, 2.0, ((0, 16),))
    lead_weight = noise(key_of[15], (D,), 0.5, 3.0, ((0, 16),))
    lead_bias = noise(key_of[16], (D,), 0.5, 3.0, ((0, 16),))
    out_grad = noise(key_of[17], (TOKENS, D), 1.0, 6.0, ((0, 16),))
    return dict(tokens=tokens, segment_ids=segment_ids, lead_hours=lead_hours, qkv_weight=qkv_weight, qv_bias=qv_bias, proj_weight=proj_weight, proj_bias=proj_bias, up_weight=up_weight, up_bias=up_bias, down_weight=down_weight, down_bias=down_bias, norm1_gain=norm1_gain, norm1_bias=norm1_bias, norm2_gain=norm2_gain, norm2_bias=norm2_bias, lead_weight=lead_weight, lead_bias=lead_bias, out_grad=out_grad)


@jax.custom_vjp
def low(v):
    return lax.optimization_barrier(v.astype(jnp.bfloat16)).astype(jnp.float32)

@jax.custom_vjp
def low_back(v):
    return v

def low_keep(v):
    return (low(v), None)

def low_pass(kept, grad):
    return (grad,)

def back_keep(v):
    return (v, None)

def back_low(kept, grad):
    return (low(grad),)
low.defvjp(low_keep, low_pass)
low_back.defvjp(back_keep, back_low)
NEGATIVE = -1e+30
EPSILON = 1e-05

def matmul(left, right):
    return jnp.dot(left, right, precision=lax.Precision.HIGHEST)

def layer_norm(values, gain_vec, shift_vec):
    center = values - lax.optimization_barrier(jnp.mean(values, axis=-1, keepdims=True))
    spread = lax.optimization_barrier(jnp.mean(center * center, axis=-1, keepdims=True))
    return center * lax.rsqrt(spread + EPSILON) * gain_vec + shift_vec

def attention(queries, key_rows, value_rows, segment_ids):
    block_rows = min(512, TOKENS)
    score_scale = HD ** (-0.5)
    query_blocks = queries.reshape(TOKENS // block_rows, block_rows, H, HD)
    seg_blocks = segment_ids.reshape(TOKENS // block_rows, block_rows)
    key_heads = key_rows.reshape(TOKENS, H, HD)
    value_heads = value_rows.reshape(TOKENS, H, HD)

    def one_block(pair_args):
        query_block, seg_block = pair_args
        scores = jnp.einsum('qhd,khd->hqk', query_block, key_heads, precision=lax.Precision.HIGHEST) * score_scale
        scores = low_back(scores)
        same_seg = (seg_block[:, None] == segment_ids[None, :])[None]
        scores = jnp.where(same_seg, scores, NEGATIVE)
        row_top = lax.optimization_barrier(jnp.max(scores, axis=-1, keepdims=True))
        weights_raw = jnp.where(same_seg, jnp.exp(scores - row_top), 0.0)
        totals = lax.optimization_barrier(jnp.sum(weights_raw, axis=-1))
        mixed = jnp.einsum('hqk,khd->qhd', low(weights_raw), value_heads, precision=lax.Precision.HIGHEST)
        return (mixed / jnp.transpose(totals)[:, :, None]).reshape(block_rows, D)
    return lax.map(jax.checkpoint(one_block), (query_blocks, seg_blocks)).reshape(TOKENS, D)

def block_forward(tokens, qkv_weight, qv_bias, proj_weight, proj_bias, up_weight, up_bias, down_weight, down_bias, norm1_gain, norm1_bias, norm2_gain, norm2_bias, lead_weight, lead_bias, segment_ids, lead_time):
    embedded = tokens + lead_time[:, None] * lead_weight + lead_bias
    normed_one = low(layer_norm(embedded, norm1_gain, norm1_bias))
    queries = low(low_back(matmul(normed_one, qkv_weight[0]) + qv_bias[0].reshape(D)))
    key_rows = low(low_back(matmul(normed_one, qkv_weight[1])))
    value_rows = low(low_back(matmul(normed_one, qkv_weight[2]) + qv_bias[1].reshape(D)))
    attn_out = low(low_back(attention(queries, key_rows, value_rows, segment_ids)))
    middle = embedded + low_back(matmul(attn_out, proj_weight) + proj_bias)
    normed_two = low(layer_norm(middle, norm2_gain, norm2_bias))
    hidden = low_back(matmul(normed_two, up_weight) + up_bias.reshape(FF))
    active = low(jax.nn.gelu(hidden, approximate=False))
    return middle + low_back(matmul(active, down_weight) + down_bias)

def reference(tokens, segment_ids, lead_hours, qkv_weight, qv_bias, proj_weight, proj_bias, up_weight, up_bias, down_weight, down_bias, norm1_gain, norm1_bias, norm2_gain, norm2_bias, lead_weight, lead_bias, out_grad):
    choose = segment_ids[:, None] == jnp.arange(NSEG, dtype=jnp.int32)[None, :]
    lead_time = lax.optimization_barrier(jnp.sum(jnp.where(choose, lead_hours[None, :], 0.0), axis=1))
    primals = tuple((item.astype(jnp.float32) for item in (tokens, qkv_weight, qv_bias, proj_weight, proj_bias, up_weight, up_bias, down_weight, down_bias, norm1_gain, norm1_bias, norm2_gain, norm2_bias, lead_weight, lead_bias)))

    def forward(*values):
        return block_forward(*values, segment_ids, lead_time)
    result, pullback = jax.vjp(forward, *primals)
    grads = pullback(out_grad.astype(jnp.float32))
    return (result.astype(jnp.bfloat16), grads[0], grads[1], grads[2], grads[3], grads[4], grads[5], grads[6], grads[7], grads[8], grads[9], grads[10], grads[11], grads[12], grads[13], grads[14])
```

```python
import functools

import jax
import jax.numpy as jnp
from jax import lax
from jax.experimental import pallas as pl
from jax.experimental.pallas import tpu as pltpu
from jax.sharding import PartitionSpec as P

HD = 64
EPSILON = 1e-05
EXCLUDED = -1e30
F32 = jnp.float32
BF16 = jnp.bfloat16
NN = (((1,), (0,)), ((), ()))
NT = (((1,), (1,)), ((), ()))
TN = (((0,), (0,)), ((), ()))


def dot(left, right, dims=NN):
    return lax.dot_general(left, right, dims, preferred_element_type=F32)


class Grid:
    def __init__(self):
        self.sp = lax.axis_size("sp")
        chips = self.sp // 2
        self.nx = 2 if chips <= 8 else 4
        self.nz = chips // self.nx
        self.chips = chips
        me = lax.axis_index("sp")
        self.core = me % 2
        self.x = (me // 2) % self.nx
        self.z = me // (2 * self.nx)

    def _move(self, block, dz, dx, flip):
        pairs = []
        for i in range(self.sp):
            z, x, c = i // (2 * self.nx), (i // 2) % self.nx, i % 2
            to = (((z + dz) % self.nz) * self.nx + (x + dx) % self.nx) * 2 + (1 - c if flip else c)
            pairs.append((i, to))
        return lax.ppermute(block, "sp", pairs)

    def zshift(self, block, k):
        return self._move(block, k, 0, False)

    def xshift(self, block, k):
        return self._move(block, 0, k, False)

    def cswap(self, block):
        return self._move(block, 0, 0, True)

    def yswap(self, block):
        return lax.ppermute(block, "tp", [(0, 1), (1, 0)])

    def gather(self, block):
        columns = [block] + [self.zshift(block, k) for k in range(1, self.nz)]
        return [[b] + [self.xshift(b, j) for j in range(1, self.nx)] for b in columns]

    def scatter(self, pieces):
        total = pieces[:, 0].astype(F32)
        for j in range(1, self.nx):
            total = total + self.xshift(pieces[:, j], -j).astype(F32)
        low = total.astype(pieces.dtype)
        mine = total[0]
        for k in range(1, self.nz):
            mine = mine + self.zshift(low[k], -k).astype(F32)
        return mine


def normalize(values):
    center = values - jnp.mean(values, axis=-1, keepdims=True)
    spread = jnp.mean(center * center, axis=-1, keepdims=True)
    scale = lax.rsqrt(spread + EPSILON)
    return center * scale, scale


def norm_back(normed, scale, gain, grad):
    scaled = grad * gain
    mean_one = jnp.mean(scaled, axis=-1, keepdims=True)
    mean_two = jnp.mean(scaled * normed, axis=-1, keepdims=True)
    return (scaled - mean_one - normed * mean_two) * scale


def lane_in_head(shape, head):
    lanes = lax.broadcasted_iota(jnp.int32, shape, 1)
    return (lanes // HD) == (head % 2)


def pair_lanes(pair):
    return slice(pair * 2 * HD, (pair + 1) * 2 * HD)


def attend_kernel(chips, heads, q_ref, qcode_ref, kcode_ref, *refs):
    kv_refs = refs[:chips]
    out_ref, lse_ref = refs[chips : chips + 2]
    kaug, vturn, qaug, acc, stat = refs[chips + 2 :]
    rows = q_ref.shape[0]
    width = heads * HD
    for i in range(chips):
        code = kcode_ref[pl.ds(i * rows, rows), :]
        for p in range(heads // 2):
            keys = kv_refs[i][:, pair_lanes(p)]
            for h in (2 * p, 2 * p + 1):
                kaug[h, pl.ds(i * rows, rows), :] = jnp.where(lane_in_head(keys.shape, h), keys, code)
        vturn[i] = jnp.transpose(kv_refs[i][:, width:])
    for p in range(heads // 2):
        part = q_ref[:, pair_lanes(p)]
        for h in (2 * p, 2 * p + 1):
            qaug[h] = jnp.where(lane_in_head(part.shape, h), part, qcode_ref[...])
    acc[...] = jnp.zeros_like(acc)
    stat[0] = jnp.full(stat.shape[1:], EXCLUDED, F32)
    stat[1] = jnp.zeros(stat.shape[1:], F32)

    def chunk(i, carry):
        for h in range(heads):
            scores = dot(kaug[h, pl.ds(i * rows, rows), :], qaug[h], NT)
            top = stat[0, h : h + 1, :]
            new_top = jnp.maximum(top, jnp.max(scores, axis=0, keepdims=True))
            weight = jnp.exp(scores - new_top)
            rescale = jnp.exp(top - new_top)
            stat[0, h : h + 1, :] = new_top
            stat[1, h : h + 1, :] = stat[1, h : h + 1, :] * rescale + jnp.sum(weight, axis=0, keepdims=True)
            span = slice(h * HD, (h + 1) * HD)
            acc[span, :] = acc[span, :] * rescale + dot(vturn[i, span, :], weight.astype(BF16))
        return carry

    lax.fori_loop(0, chips, chunk, 0)
    for h in range(heads):
        span = slice(h * HD, (h + 1) * HD)
        acc[span, :] = acc[span, :] / stat[1, h : h + 1, :]
    out_ref[...] = jnp.transpose(acc[...])
    lse_ref[...] = stat[0] + jnp.log(jnp.maximum(stat[1], 1e-37))


def attend(q, qcode, kcode, kv_pieces):
    rows, width = q.shape
    heads = width // HD
    chips = len(kv_pieces)
    return pl.pallas_call(
        functools.partial(attend_kernel, chips, heads),
        out_shape=(jax.ShapeDtypeStruct((rows, width), F32), jax.ShapeDtypeStruct((8, rows), F32)),
        scratch_shapes=[
            pltpu.VMEM((heads, chips * rows, 2 * HD), BF16),
            pltpu.VMEM((chips, width, rows), BF16),
            pltpu.VMEM((heads, rows, 2 * HD), BF16),
            pltpu.VMEM((width, rows), F32),
            pltpu.VMEM((2, 8, rows), F32),
        ],
        compiler_params=pltpu.CompilerParams(vmem_limit_bytes=48 * 1024 * 1024),
        cost_estimate=pl.CostEstimate(
            flops=4 * rows * rows * chips * width, bytes_accessed=4 * rows * width * chips, transcendentals=rows * rows * chips * heads
        ),
        name="attend",
    )(q, qcode, kcode, *kv_pieces)


def attend_back_kernel(chips, heads, q_ref, qcode_ref, kcode_ref, dout_ref, lse_ref, delta_ref, *refs):
    kv_refs = refs[:chips]
    dq_ref, dkv_ref = refs[chips : chips + 2]
    kaug, kturn, vals, qaug, qmask, domask, acc = refs[chips + 2 :]
    rows = q_ref.shape[0]
    width = heads * HD
    for i in range(chips):
        span = pl.ds(i * rows, rows)
        code = kcode_ref[span, :]
        for p in range(heads // 2):
            keys = kv_refs[i][:, pair_lanes(p)]
            for h in (2 * p, 2 * p + 1):
                kaug[h, span, :] = jnp.where(lane_in_head(keys.shape, h), keys, code)
        kturn[i] = jnp.transpose(kv_refs[i][:, :width])
        vals[span, :] = kv_refs[i][:, width:]
    for p in range(heads // 2):
        part = q_ref[:, pair_lanes(p)]
        dpart = dout_ref[:, pair_lanes(p)]
        for h in (2 * p, 2 * p + 1):
            inside = lane_in_head(part.shape, h)
            qaug[h] = jnp.where(inside, part, qcode_ref[...])
            qmask[h] = jnp.where(inside, part, jnp.zeros_like(part))
            domask[h] = jnp.where(inside, dpart, jnp.zeros_like(dpart))
    acc[...] = jnp.zeros_like(acc)

    def chunk(i, carry):
        span = pl.ds(i * rows, rows)
        for p in range(heads // 2):
            dkey = dval = None
            for h in (2 * p, 2 * p + 1):
                scores = dot(kaug[h, span, :], qaug[h], NT)
                prob = jnp.exp(scores - lse_ref[h : h + 1, :])
                dprob = dot(vals[span, pair_lanes(p)], domask[h], NT)
                dscore = (prob * (dprob - delta_ref[h : h + 1, :])).astype(BF16)
                add_val = dot(prob.astype(BF16), domask[h])
                add_key = dot(dscore, qmask[h])
                dval = add_val if dval is None else dval + add_val
                dkey = add_key if dkey is None else dkey + add_key
                turn = slice(h * HD, (h + 1) * HD)
                acc[turn, :] += dot(kturn[i, turn, :], dscore)
            dkv_ref[i, :, pair_lanes(p)] = dkey.astype(BF16)
            dkv_ref[i, :, slice(width + p * 2 * HD, width + (p + 1) * 2 * HD)] = dval.astype(BF16)
        return carry

    lax.fori_loop(0, chips, chunk, 0)
    dq_ref[...] = (jnp.transpose(acc[...]) * (HD ** (-0.5))).astype(BF16)


def attend_back(q, qcode, kcode, dout, lse, delta, kv_pieces):
    rows, width = q.shape
    heads = width // HD
    chips = len(kv_pieces)
    return pl.pallas_call(
        functools.partial(attend_back_kernel, chips, heads),
        out_shape=(
            jax.ShapeDtypeStruct((rows, width), BF16),
            jax.ShapeDtypeStruct((chips, rows, 2 * width), BF16),
        ),
        scratch_shapes=[
            pltpu.VMEM((heads, chips * rows, 2 * HD), BF16),
            pltpu.VMEM((chips, width, rows), BF16),
            pltpu.VMEM((chips * rows, width), BF16),
            pltpu.VMEM((heads, rows, 2 * HD), BF16),
            pltpu.VMEM((heads, rows, 2 * HD), BF16),
            pltpu.VMEM((heads, rows, 2 * HD), BF16),
            pltpu.VMEM((width, rows), F32),
        ],
        compiler_params=pltpu.CompilerParams(vmem_limit_bytes=56 * 1024 * 1024),
        cost_estimate=pl.CostEstimate(
            flops=10 * rows * rows * chips * width, bytes_accessed=8 * rows * width * chips, transcendentals=rows * rows * chips * heads
        ),
        name="attend_back",
    )(q, qcode, kcode, dout, lse, delta, *kv_pieces)


def per_device(
    tokens,
    segment_ids,
    lead_hours,
    qkv_weight,
    qv_bias,
    proj_weight,
    proj_bias,
    up_weight,
    up_bias,
    down_weight,
    down_bias,
    norm1_gain,
    norm1_bias,
    norm2_gain,
    norm2_bias,
    lead_weight,
    lead_bias,
    out_grad,
):
    grid = Grid()
    core, chips = grid.core, grid.chips
    rows, width = tokens.shape
    part = norm1_gain.shape[0]
    low_core = core == 0

    def by_core(own, other):
        return jnp.where(low_core, own, other), jnp.where(low_core, other, own)

    def core_half(array, axis):
        half = array.shape[axis] // 2
        first = lax.slice_in_dim(array, 0, half, axis=axis)
        second = lax.slice_in_dim(array, half, 2 * half, axis=axis)
        return jnp.where(low_core, first, second), jnp.where(low_core, second, first)

    def spread(shard):
        keep, send = core_half(shard, shard.ndim - 1)
        keep = jnp.swapaxes(keep, 0, 1).reshape(part, -1) if keep.ndim == 3 else keep
        send = jnp.swapaxes(send, 0, 1).reshape(part, -1) if send.ndim == 3 else send
        return jnp.concatenate(by_core(keep, grid.cswap(send)), axis=0)

    def collect(block):
        pieces = grid.gather(block)
        return jnp.concatenate([p for line in pieces for p in line], axis=0)

    vectors = [lead_weight, lead_bias, norm1_gain, norm1_bias, proj_bias, norm2_gain, norm2_bias, down_bias]
    n_vec = len(vectors)
    flat = jnp.concatenate(vectors + [qv_bias.reshape(-1), up_bias.reshape(-1), segment_ids.astype(BF16)])
    sizes = (n_vec * part, qv_bias.size, up_bias.size, rows)
    pack = jnp.pad(flat, (0, -flat.size % 1024)).reshape(-1, 128)
    both = jnp.stack(by_core(pack, grid.cswap(pack)))
    table = jnp.stack([p for line in grid.gather(both) for p in line]).reshape(chips, 2, -1)
    order = jnp.arange(chips)
    chip_of = ((grid.z - order // grid.nx) % grid.nz) * grid.nx + (grid.x - order % grid.nx) % grid.nx
    at = 0
    vec_table = table[:, :, : sizes[0]].reshape(chips, 2, n_vec, part)
    vecs = jnp.transpose(vec_table, (2, 0, 1, 3)).reshape(n_vec, width).astype(F32)
    at += sizes[0]
    heads_local = qv_bias.shape[1]
    bias_table = table[:, :, at : at + sizes[1] + sizes[2]].reshape(chips, -1)
    place = (jnp.arange(chips)[:, None] == chip_of[None, :]).astype(BF16)
    bias_abs = dot(place, bias_table).reshape(2 * chips, -1)
    qv_all = jnp.transpose(bias_abs[:, : sizes[1]].reshape(2 * chips, 2, heads_local, -1), (1, 2, 0, 3)).reshape(
        2, heads_local * HD
    )
    up_all = jnp.transpose(bias_abs[:, sizes[1] :].reshape(2 * chips, up_bias.shape[0], -1), (1, 0, 2)).reshape(1, -1)
    qv_full = core_half(qv_all, 1)[0]
    up_full = core_half(up_all, 1)[0]
    at += sizes[1] + sizes[2]
    seg_table = table[:, :, at : at + rows]
    key_seg = jnp.concatenate(core_half(seg_table, 1), axis=1).reshape(-1).astype(jnp.int32)
    query_seg = key_seg[: 2 * rows]
    lanes = jnp.arange(2 * HD, dtype=jnp.int32) % HD
    kcode = jnp.where(key_seg[:, None] == lanes[None, :], 0.0, EXCLUDED).astype(BF16)
    qcode = (query_seg[:, None] == lanes[None, :]).astype(BF16)

    group = 2 * part
    feature = jnp.arange(width)
    source = jnp.sum(
        jnp.where((feature // group)[:, None] == order[None, :], chip_of[None, :], 0), axis=1
    ) * group + feature % group
    turn = (feature[:, None] == source[None, :]).astype(BF16)

    w_qkv = collect(spread(qkv_weight))
    tokens_two = jnp.concatenate([tokens, grid.cswap(tokens)], axis=0)
    grad_two = jnp.concatenate([out_grad, grid.cswap(out_grad)], axis=0)
    turned = dot(jnp.concatenate([tokens_two, grad_two], axis=0), turn)
    choose = query_seg[:, None] == jnp.arange(lead_hours.shape[0], dtype=jnp.int32)[None, :]
    lead_time = jnp.sum(jnp.where(choose, lead_hours[None, :], 0.0), axis=1)
    embedded_two = turned[: 2 * rows] + lead_time[:, None] * vecs[0] + vecs[1]
    gz = turned[2 * rows :].astype(BF16)
    embedded = embedded_two[:rows]
    n1, s1 = normalize(embedded_two)
    normed_one = (n1 * vecs[2] + vecs[3]).astype(BF16)
    local = qv_full.shape[1]
    qkv = dot(normed_one, w_qkv)
    q = ((qkv[:, :local] + qv_full[0]).astype(BF16) * jnp.asarray(HD ** (-0.5), BF16))
    kv = jnp.concatenate([qkv[:, local : 2 * local], qkv[:, 2 * local :] + qv_full[1]], axis=1).astype(BF16)
    kv_pieces = [p for line in grid.gather(kv) for p in line]

    w_proj = collect(spread(jnp.transpose(proj_weight)))
    w_up = collect(spread(up_weight))
    w_down = collect(spread(jnp.transpose(down_weight)))

    attn_full, lse = attend(q, qcode, kcode, kv_pieces)
    attn_out = attn_full.astype(BF16)

    def pair_sum(partial):
        mine = partial[:rows] + grid.cswap(partial[rows:].astype(BF16)).astype(F32)
        low = mine.astype(BF16)
        return low.astype(F32) + grid.yswap(low).astype(F32)

    def core_pair(block):
        return jnp.concatenate([block, grid.cswap(block)], axis=0)

    middle = embedded + (pair_sum(dot(attn_out, w_proj, NT)) + vecs[4])
    n2, s2 = normalize(middle)
    normed_two = core_pair((n2 * vecs[5] + vecs[6]).astype(BF16))
    hidden = dot(normed_two, w_up) + up_full
    cdf = 0.5 * (1.0 + lax.erf(hidden * (0.5**0.5)))
    active = (hidden * cdf).astype(BF16)
    slope = cdf + hidden * (jnp.exp(-0.5 * hidden * hidden) * ((0.5 / jnp.pi) ** 0.5))
    grad_hidden = (dot(gz, w_down) * slope).astype(BF16)
    grad_n2 = pair_sum(dot(grad_hidden, w_up, NT))
    block_out = middle + (pair_sum(dot(active, w_down, NT)) + vecs[7])
    block_out = dot(block_out.astype(BF16), turn, NT).astype(BF16)

    def give(gradient):
        pieces = gradient.astype(BF16).reshape(grid.nz, grid.nx, 2 * part, -1)
        mine = grid.scatter(pieces)
        keep, send = core_half(mine, 0)
        other = grid.cswap(send.astype(BF16)).astype(F32)
        return by_core(keep, other)

    d_up = give(dot(normed_two, grad_hidden, TN))
    d_down = give(dot(gz, active, TN))

    grad_top = gz[:rows].astype(F32)
    grad_middle = grad_top + norm_back(n2, s2, vecs[5], grad_n2)
    grad_branch = core_pair(grad_middle.astype(BF16))
    d_proj = give(dot(grad_branch, attn_out, TN))
    grad_attn = dot(grad_branch, w_proj).astype(BF16)
    delta = jnp.sum((grad_attn.astype(F32) * attn_full).reshape(2 * rows, -1, HD), axis=2)
    delta = jnp.pad(jnp.transpose(delta), ((0, 8 - delta.shape[1]), (0, 0)))
    grad_q, grad_kv_all = attend_back(q, qcode, kcode, grad_attn, lse, delta, kv_pieces)
    grad_kv = grid.scatter(grad_kv_all.reshape((grid.nz, grid.nx) + grad_kv_all.shape[1:])).astype(BF16)
    grad_stack = jnp.concatenate([grad_q, grad_kv], axis=1)
    d_qkv = give(dot(normed_one, grad_stack, TN))
    grad_n1 = pair_sum(dot(grad_stack, w_qkv, NT))
    input_grad = grad_middle + norm_back(n1[:rows], s1[:rows], vecs[2], grad_n1)

    sums = jnp.stack(
        [
            jnp.sum(input_grad * lead_time[:rows, None], axis=0),
            jnp.sum(input_grad, axis=0),
            jnp.sum(grad_n1 * n1[:rows], axis=0),
            jnp.sum(grad_n1, axis=0),
            jnp.sum(grad_branch[:rows].astype(F32), axis=0),
            jnp.sum(grad_n2 * n2, axis=0),
            jnp.sum(grad_n2, axis=0),
            jnp.sum(grad_top, axis=0),
        ]
    )
    sums = sums + grid.cswap(sums)
    sums = jnp.transpose(sums.reshape(n_vec, grid.nz, grid.nx, group), (1, 2, 0, 3))
    sums = core_half(grid.scatter(sums), 1)[0]
    bias_sums = jnp.concatenate(
        [jnp.sum(grad_hidden.astype(F32), axis=0), jnp.sum(grad_stack.astype(F32), axis=0)]
    ).reshape(1, -1)
    total = bias_sums
    for j in range(1, grid.nx):
        total = total + grid.xshift(bias_sums, j)
    whole = total
    for k in range(1, grid.nz):
        whole = whole + grid.zshift(total, k)
    low_half, high_half = by_core(whole, grid.cswap(whole))
    me = lax.axis_index("sp")
    n_up = grad_hidden.shape[1]

    def piece(low, high, start, size):
        both_halves = jnp.concatenate([low[0, start : start + size], high[0, start : start + size]])
        table_rows = both_halves.reshape(-1, HD)
        return lax.dynamic_slice_in_dim(table_rows, me * (HD // grid.sp), HD // grid.sp, 1)

    g_up_bias = piece(low_half, high_half, 0, n_up)
    g_q_bias = piece(low_half, high_half, n_up, local)
    g_v_bias = piece(low_half, high_half, n_up + 2 * local, local)

    input_grad = lax.dot_general(
        input_grad, turn.astype(F32), NT, precision=lax.Precision.HIGHEST, preferred_element_type=F32
    )
    g_qkv = jnp.concatenate([h.reshape(part, 3, local) for h in d_qkv], axis=2)
    return (
        block_out,
        input_grad,
        jnp.swapaxes(g_qkv, 0, 1),
        jnp.stack([g_q_bias, g_v_bias]),
        jnp.transpose(jnp.concatenate(d_proj, axis=1)),
        sums[4],
        jnp.concatenate(d_up, axis=1),
        g_up_bias,
        jnp.transpose(jnp.concatenate(d_down, axis=1)),
        sums[7],
        sums[2],
        sums[3],
        sums[5],
        sums[6],
        sums[0],
        sums[1],
    )


def solution(mesh):
    placed = (
        P("sp", None),
        P("sp"),
        P(),
        P(None, "sp", "tp"),
        P(None, "tp", "sp"),
        P("tp", "sp"),
        P("sp"),
        P("sp", "tp"),
        P("tp", "sp"),
        P("tp", "sp"),
        P("sp"),
        P("sp"),
        P("sp"),
        P("sp"),
        P("sp"),
        P("sp"),
        P("sp"),
        P("sp", None),
    )
    return jax.shard_map(
        per_device,
        mesh=mesh,
        in_specs=placed,
        out_specs=(
            P("sp", None),
            P("sp", None),
            P(None, "sp", "tp"),
            P(None, "tp", "sp"),
            P("tp", "sp"),
            P("sp"),
            P("sp", "tp"),
            P("tp", "sp"),
            P("tp", "sp"),
            P("sp"),
            P("sp"),
            P("sp"),
            P("sp"),
            P("sp"),
            P("sp"),
            P("sp"),
        ),
        check_vma=False,
    )
```

```python
import functools

import jax
import jax.numpy as jnp
from jax import lax
from jax.experimental import pallas as pl
from jax.experimental.pallas import tpu as pltpu
from jax.sharding import PartitionSpec as P

HD = 64
EPSILON = 1e-05
EXCLUDED = -1e30
F32 = jnp.float32
BF16 = jnp.bfloat16
NN = (((1,), (0,)), ((), ()))
NT = (((1,), (1,)), ((), ()))
TN = (((0,), (0,)), ((), ()))


def dot(left, right, dims=NN):
    return lax.dot_general(left, right, dims, preferred_element_type=F32)


class Grid:
    def __init__(self):
        self.sp = lax.axis_size("sp")
        self.nz = 4
        self.nx = self.sp // (2 * self.nz)
        self.chips = self.nz * self.nx
        me = lax.axis_index("sp")
        self.me = me
        self.core = me % 2
        self.x = (me // 2) % self.nx
        self.z = me // (2 * self.nx)
        self.y = lax.axis_index("tp")

    def _move(self, block, dz, dx, flip):
        pairs = []
        for i in range(self.sp):
            z, x, c = i // (2 * self.nx), (i // 2) % self.nx, i % 2
            to = (((z + dz) % self.nz) * self.nx + (x + dx) % self.nx) * 2 + (1 - c if flip else c)
            pairs.append((i, to))
        return lax.ppermute(block, "sp", pairs)

    def zshift(self, block, k):
        return self._move(block, k, 0, False)

    def xshift(self, block, k):
        return self._move(block, 0, k, False)

    def cswap(self, block):
        return self._move(block, 0, 0, True)

    def yswap(self, block):
        return lax.ppermute(block, "tp", [(0, 1), (1, 0)])

    def _pairs(self, route):
        pairs = []
        for chip in range(self.chips):
            for (c, y), (to_c, to_y) in route:
                pairs.append(((chip * 2 + c) * 2 + y, (chip * 2 + to_c) * 2 + to_y))
        return pairs

    def spin(self, block, back=False):
        route = []
        for b in (0, 1):
            route += [((b, b), (b, 1 - b)), ((1 - b, b), (b, b))]
        if back:
            route = [(to, at) for at, to in route]
        return lax.ppermute(block, ("sp", "tp"), self._pairs(route))

    def cross(self, block):
        route = [((1 - b, b), (b, 1 - b)) for b in (0, 1)]
        return lax.ppermute(block, ("sp", "tp"), self._pairs(route))

    def far_z(self, k):
        return (self.z + k) % self.nz

    def far_x(self, j):
        return (self.x + j) % self.nx

    def gather(self, block):
        columns = [block] + [self.zshift(block, k) for k in range(1, self.nz)]
        return [p for b in columns for p in [b] + [self.xshift(b, j) for j in range(1, self.nx)]]

    def chip_order(self):
        order = jnp.arange(self.chips)
        return self.far_z(-(order // self.nx)) * self.nx + self.far_x(-(order % self.nx))

    def scatter(self, pieces):
        total = pick(pieces, self.x, 1).astype(F32)
        for j in range(1, self.nx):
            total = total + self.xshift(pick(pieces, self.far_x(j), 1), j).astype(F32)
        low = total.astype(pieces.dtype)
        mine = pick(total, self.z, 0)
        for k in range(1, self.nz):
            mine = mine + self.zshift(pick(low, self.far_z(k), 0), k).astype(F32)
        return mine


def pick(array, index, axis):
    return lax.dynamic_index_in_dim(array, index, axis, keepdims=False)


def normalize(values):
    center = values - jnp.mean(values, axis=-1, keepdims=True)
    spread = jnp.mean(center * center, axis=-1, keepdims=True)
    scale = lax.rsqrt(spread + EPSILON)
    return center * scale, scale


def norm_back(normed, scale, gain, grad):
    scaled = grad * gain
    mean_one = jnp.mean(scaled, axis=-1, keepdims=True)
    mean_two = jnp.mean(scaled * normed, axis=-1, keepdims=True)
    return (scaled - mean_one - normed * mean_two) * scale


def place_kernel(axis, starts_ref, *refs):
    pieces, out_ref = refs[:-1], refs[-1]
    for i, piece in enumerate(pieces):
        size = piece.shape[axis]
        span = pl.ds(pl.multiple_of(starts_ref[i], size), size)
        if axis == 0:
            out_ref[span, :] = piece[...]
        else:
            out_ref[:, span] = piece[...]


def place(pieces, starts, axis):
    shape = list(pieces[0].shape)
    shape[axis] *= len(pieces)
    vmem = pl.BlockSpec(memory_space=pltpu.VMEM)
    return pl.pallas_call(
        functools.partial(place_kernel, axis),
        out_shape=jax.ShapeDtypeStruct(tuple(shape), pieces[0].dtype),
        in_specs=[pl.BlockSpec(memory_space=pltpu.SMEM)] + [vmem] * len(pieces),
        out_specs=vmem,
        compiler_params=pltpu.CompilerParams(vmem_limit_bytes=32 * 1024 * 1024),
        name="place",
    )(jnp.stack(starts).astype(jnp.int32), *pieces)


def place_qkv_kernel(starts_ref, *refs):
    pieces, out_ref = refs[:-1], refs[-1]
    for i, piece in enumerate(pieces):
        size = piece.shape[1] // 3
        span = pl.ds(pl.multiple_of(starts_ref[i], size), size)
        for c in range(3):
            out_ref[c, :, span] = piece[:, c * size : (c + 1) * size].astype(F32)


def place_qkv(pieces, starts):
    rows, columns = pieces[0].shape
    vmem = pl.BlockSpec(memory_space=pltpu.VMEM)
    return pl.pallas_call(
        place_qkv_kernel,
        out_shape=jax.ShapeDtypeStruct((3, rows, columns // 3 * len(pieces)), F32),
        in_specs=[pl.BlockSpec(memory_space=pltpu.SMEM)] + [vmem] * len(pieces),
        out_specs=vmem,
        name="place_qkv",
    )(jnp.stack(starts).astype(jnp.int32), *pieces)


def lane_in_head(shape, head):
    lanes = lax.broadcasted_iota(jnp.int32, shape, 1)
    return (lanes // HD) == (head % 2)


def pair_lanes(pair):
    return slice(pair * 2 * HD, (pair + 1) * 2 * HD)


STEP = 384


def attend_kernel(pieces, heads, q_ref, qcode_ref, kcode_ref, *refs):
    kv_refs = refs[:pieces]
    out_ref, lse_ref = refs[pieces : pieces + 2]
    kaug, vturn, qaug, acc, stat = refs[pieces + 2 :]
    width = heads * HD
    steps = kv_refs[0].shape[0] // STEP
    for n in range(pieces * steps):
        block = kv_refs[n // steps]
        rows = pl.ds((n % steps) * STEP, STEP)
        span = pl.ds(n * STEP, STEP)
        code = kcode_ref[span, :]
        for p in range(heads // 2):
            keys = block[rows, pair_lanes(p)]
            for h in (2 * p, 2 * p + 1):
                kaug[h, span, :] = jnp.where(lane_in_head(keys.shape, h), keys, code)
        vturn[n] = jnp.transpose(block[rows, width:])
    for p in range(heads // 2):
        part = q_ref[:, pair_lanes(p)]
        for h in (2 * p, 2 * p + 1):
            qaug[h] = jnp.where(lane_in_head(part.shape, h), part, qcode_ref[...])
    acc[...] = jnp.zeros_like(acc)
    stat[0] = jnp.full(stat.shape[1:], EXCLUDED, F32)
    stat[1] = jnp.zeros(stat.shape[1:], F32)

    def chunk(i, carry):
        for h in range(heads):
            scores = dot(kaug[h, pl.ds(i * STEP, STEP), :], qaug[h], NT)
            top = stat[0, h : h + 1, :]
            new_top = jnp.maximum(top, jnp.max(scores, axis=0, keepdims=True))
            weight = jnp.exp(scores - new_top)
            rescale = jnp.exp(top - new_top)
            stat[0, h : h + 1, :] = new_top
            stat[1, h : h + 1, :] = stat[1, h : h + 1, :] * rescale + jnp.sum(weight, axis=0, keepdims=True)
            span = slice(h * HD, (h + 1) * HD)
            acc[span, :] = acc[span, :] * rescale + dot(vturn[i, span, :], weight.astype(BF16))
        return carry

    lax.fori_loop(0, pieces * steps, chunk, 0)
    for h in range(heads):
        span = slice(h * HD, (h + 1) * HD)
        acc[span, :] = acc[span, :] / stat[1, h : h + 1, :]
    out_ref[...] = jnp.transpose(acc[...])
    lse_ref[...] = stat[0] + jnp.log(jnp.maximum(stat[1], 1e-37))


def attend(q, qcode, kcode, kv_pieces):
    rows, width = q.shape
    heads = width // HD
    keys = kcode.shape[0]
    return pl.pallas_call(
        functools.partial(attend_kernel, len(kv_pieces), heads),
        out_shape=(jax.ShapeDtypeStruct((rows, width), F32), jax.ShapeDtypeStruct((8, rows), F32)),
        scratch_shapes=[
            pltpu.VMEM((heads, keys, 2 * HD), BF16),
            pltpu.VMEM((keys // STEP, width, STEP), BF16),
            pltpu.VMEM((heads, rows, 2 * HD), BF16),
            pltpu.VMEM((width, rows), F32),
            pltpu.VMEM((2, 8, rows), F32),
        ],
        compiler_params=pltpu.CompilerParams(vmem_limit_bytes=48 * 1024 * 1024),
        cost_estimate=pl.CostEstimate(
            flops=4 * rows * keys * width, bytes_accessed=4 * keys * width, transcendentals=rows * keys * heads
        ),
        name="attend",
    )(q, qcode, kcode, *kv_pieces)


def attend_back_kernel(pieces, heads, q_ref, qcode_ref, kcode_ref, dout_ref, lse_ref, delta_ref, *refs):
    kv_refs = refs[:pieces]
    dq_ref, dkv_ref = refs[pieces : pieces + 2]
    kaug, kturn, vals, qaug, qmask, domask, acc = refs[pieces + 2 :]
    width = heads * HD
    steps = kv_refs[0].shape[0] // STEP
    for n in range(pieces * steps):
        block = kv_refs[n // steps]
        rows = pl.ds((n % steps) * STEP, STEP)
        span = pl.ds(n * STEP, STEP)
        code = kcode_ref[span, :]
        for p in range(heads // 2):
            keys = block[rows, pair_lanes(p)]
            for h in (2 * p, 2 * p + 1):
                kaug[h, span, :] = jnp.where(lane_in_head(keys.shape, h), keys, code)
        kturn[n] = jnp.transpose(block[rows, :width])
        vals[span, :] = block[rows, width:]
    for p in range(heads // 2):
        part = q_ref[:, pair_lanes(p)]
        dpart = dout_ref[:, pair_lanes(p)]
        for h in (2 * p, 2 * p + 1):
            inside = lane_in_head(part.shape, h)
            qaug[h] = jnp.where(inside, part, qcode_ref[...])
            qmask[h] = jnp.where(inside, part, jnp.zeros_like(part))
            domask[h] = jnp.where(inside, dpart, jnp.zeros_like(dpart))
    acc[...] = jnp.zeros_like(acc)

    def chunk(i, carry):
        span = pl.ds(i * STEP, STEP)
        for p in range(heads // 2):
            dkey = dval = None
            for h in (2 * p, 2 * p + 1):
                scores = dot(kaug[h, span, :], qaug[h], NT)
                prob = jnp.exp(scores - lse_ref[h : h + 1, :])
                dprob = dot(vals[span, pair_lanes(p)], domask[h], NT)
                dscore = (prob * (dprob - delta_ref[h : h + 1, :])).astype(BF16)
                add_val = dot(prob.astype(BF16), domask[h])
                add_key = dot(dscore, qmask[h])
                dval = add_val if dval is None else dval + add_val
                dkey = add_key if dkey is None else dkey + add_key
                turn = slice(h * HD, (h + 1) * HD)
                acc[turn, :] += dot(kturn[i, turn, :], dscore)
            dkv_ref[i, :, pair_lanes(p)] = dkey.astype(BF16)
            dkv_ref[i, :, slice(width + p * 2 * HD, width + (p + 1) * 2 * HD)] = dval.astype(BF16)
        return carry

    lax.fori_loop(0, pieces * steps, chunk, 0)
    dq_ref[...] = (jnp.transpose(acc[...]) * (HD ** (-0.5))).astype(BF16)


def attend_back(q, qcode, kcode, dout, lse, delta, kv_pieces):
    rows, width = q.shape
    heads = width // HD
    keys = kcode.shape[0]
    return pl.pallas_call(
        functools.partial(attend_back_kernel, len(kv_pieces), heads),
        out_shape=(
            jax.ShapeDtypeStruct((rows, width), BF16),
            jax.ShapeDtypeStruct((keys // STEP, STEP, 2 * width), BF16),
        ),
        scratch_shapes=[
            pltpu.VMEM((heads, keys, 2 * HD), BF16),
            pltpu.VMEM((keys // STEP, width, STEP), BF16),
            pltpu.VMEM((keys, width), BF16),
            pltpu.VMEM((heads, rows, 2 * HD), BF16),
            pltpu.VMEM((heads, rows, 2 * HD), BF16),
            pltpu.VMEM((heads, rows, 2 * HD), BF16),
            pltpu.VMEM((width, rows), F32),
        ],
        compiler_params=pltpu.CompilerParams(vmem_limit_bytes=56 * 1024 * 1024),
        cost_estimate=pl.CostEstimate(
            flops=10 * rows * keys * width, bytes_accessed=8 * keys * width, transcendentals=rows * keys * heads
        ),
        name="attend_back",
    )(q, qcode, kcode, dout, lse, delta, *kv_pieces)


def after(block, *before):
    return lax.optimization_barrier((block,) + before)[0]


def per_device(
    tokens,
    segment_ids,
    lead_hours,
    qkv_weight,
    qv_bias,
    proj_weight,
    proj_bias,
    up_weight,
    up_bias,
    down_weight,
    down_bias,
    norm1_gain,
    norm1_bias,
    norm2_gain,
    norm2_bias,
    lead_weight,
    lead_bias,
    out_grad,
):
    grid = Grid()
    nz, nx, chips, sp = grid.nz, grid.nx, grid.chips, grid.sp
    core, y = grid.core, grid.y
    full_rows, width = tokens.shape
    rows = full_rows // 2
    part = norm1_gain.shape[0]
    at_home = core == y

    def split(array, axis, index):
        half = array.shape[axis] // 2
        first = lax.slice_in_dim(array, 0, half, axis=axis)
        second = lax.slice_in_dim(array, half, 2 * half, axis=axis)
        return jnp.where(index == 0, first, second), jnp.where(index == 0, second, first)

    def in_order(own, other, index):
        return jnp.where(index == 0, own, other), jnp.where(index == 0, other, own)

    vectors = [lead_weight, lead_bias, norm1_gain, norm1_bias, proj_bias, norm2_gain, norm2_bias, down_bias]
    n_vec = len(vectors)
    pack = jnp.concatenate(
        [
            jnp.stack(vectors),
            qv_bias.reshape(-1, part),
            up_bias.reshape(-1, part),
            segment_ids.astype(BF16).reshape(-1, part),
        ],
        axis=0,
    )
    n_qv, n_up = qv_bias.size // part, up_bias.size // part
    both = jnp.stack(in_order(pack, grid.cswap(pack), core))
    table = jnp.stack(grid.gather(both)).reshape(chips, -1)
    chip_of = grid.chip_order()
    in_place = (jnp.arange(chips)[:, None] == chip_of[None, :]).astype(BF16)
    table = dot(in_place, table).reshape(sp, -1, part)
    vecs = jnp.transpose(table[:, :n_vec], (1, 0, 2)).reshape(n_vec, width)
    heads_local = qv_bias.shape[1]
    qv_all = jnp.transpose(
        table[:, n_vec : n_vec + n_qv].reshape(sp, 2, heads_local, -1), (1, 2, 0, 3)
    ).reshape(2, heads_local * HD)
    up_all = jnp.transpose(
        table[:, n_vec + n_qv : n_vec + n_qv + n_up].reshape(sp, up_bias.shape[0], -1), (1, 0, 2)
    ).reshape(1, -1)
    up_full = split(up_all, 1, core)[0]
    qv_far = grid.yswap(qv_all)
    qv_mine = jnp.where(at_home, qv_all, qv_far).reshape(2, nz, -1)
    qv_full = pick(qv_mine, grid.z, 1)
    local = qv_full.shape[1]

    seg_rows = table[:, n_vec + n_qv + n_up :].reshape(sp * 2, rows)
    n_key = nx * 2 * 2 * nz
    n = jnp.arange(n_key)
    k, r, w, j = n % nz, (n // nz) % 2, (n // (2 * nz)) % 2, n // (4 * nz)
    key_at = ((grid.far_z(-k) * nx + grid.far_x(-j)) * 2 + (core + r) % 2) * 2 + (y + w) % 2
    take = (key_at[:, None] == jnp.arange(2 * sp)[None, :]).astype(BF16)
    key_seg = dot(take, seg_rows.astype(BF16)).astype(jnp.int32).reshape(-1)
    query_seg = key_seg[: 2 * nz * rows]
    lanes = jnp.arange(2 * HD, dtype=jnp.int32) % HD
    kcode = jnp.where(key_seg[:, None] == lanes[None, :], 0.0, EXCLUDED).astype(BF16)
    qcode = (query_seg[:, None] == lanes[None, :]).astype(BF16)

    shard = jnp.transpose(qkv_weight.reshape(3, part, nz, -1), (2, 1, 0, 3)).reshape(nz, part, -1)
    wq_z = [pick(shard, grid.z, 0)] + [grid.zshift(pick(shard, grid.far_z(k), 0), k) for k in range(1, nz)]

    own_tokens = split(tokens, 0, y)[0]
    token_z = jnp.concatenate([own_tokens] + [grid.zshift(own_tokens, k) for k in range(1, nz)])
    tokens_all = jnp.concatenate([token_z, grid.cswap(token_z)])

    wq_z = jnp.stack(wq_z)
    wq_x = jnp.stack([wq_z] + [grid.xshift(wq_z, j) for j in range(1, nx)])
    wq_spin, wq_cross = grid.spin(wq_x), grid.cross(wq_x)
    wq_same = jnp.where(at_home, wq_x, wq_spin)
    wq_other = jnp.where(at_home, wq_spin, wq_cross)
    starts, pieces = [], []
    for p, block in ((core, wq_same), (1 - core, wq_other)):
        for j in range(nx):
            for k in range(nz):
                starts.append(((grid.far_z(-k) * nx + grid.far_x(-j)) * 2 + p) * part)
                pieces.append(block[j, k])
    w_qkv = place(pieces, starts, 0)

    choose = query_seg[:, None] == jnp.arange(lead_hours.shape[0], dtype=jnp.int32)[None, :]
    lead_time = jnp.sum(jnp.where(choose, lead_hours[None, :], 0.0), axis=1)
    embedded_all = tokens_all.astype(F32) + lead_time[:, None] * vecs[0] + vecs[1]
    embedded = embedded_all[:rows]
    n1_all, s1_all = normalize(embedded_all)
    n1, s1 = n1_all[:rows], s1_all[:rows]
    normed_one = (n1_all * vecs[2] + vecs[3]).astype(BF16)
    qkv = dot(normed_one, w_qkv)
    q = (qkv[:, :local] + qv_full[0]).astype(BF16) * jnp.asarray(HD ** (-0.5), BF16)
    kv = jnp.concatenate([qkv[:, local : 2 * local], qkv[:, 2 * local :] + qv_full[1]], axis=1).astype(BF16)
    kv_far = grid.yswap(kv)
    kv_pieces = [kv, kv_far]
    for j in range(1, nx):
        kv_pieces += [grid.xshift(kv, j), grid.xshift(kv_far, j)]

    def spread(shard):
        keep, send = split(shard, 1, core)
        return jnp.concatenate(in_order(keep, grid.cswap(send), core), axis=0)

    chip_starts = [chip_of[i] * (2 * part) for i in range(chips)]
    w_up = place(grid.gather(spread(up_weight)), chip_starts, 0)
    w_down = place(grid.gather(spread(jnp.transpose(down_weight))), chip_starts, 0)

    wp = grid.gather(jnp.transpose(proj_weight))
    wp_half = jnp.concatenate(wp)
    wp_rows = jnp.concatenate(in_order(wp_half, grid.yswap(wp_half), y), axis=1)
    wp_far = grid.cswap(wp_rows)
    starts, pieces = [], []
    for p, block in ((core, wp_rows), (1 - core, wp_far)):
        for i in range(chips):
            starts.append((chip_of[i] * 2 + p) * part)
            pieces.append(block[i * part : (i + 1) * part])
    w_proj = place(pieces, starts, 0)

    attn_full, lse = attend(q, qcode, kcode, kv_pieces)
    blocks = attn_full.astype(BF16).reshape(2, nz, rows, local)
    home = jnp.stack([blocks[:, 0]] + [grid.zshift(blocks[:, k], -k) for k in range(1, nz)])
    home_far = grid.cswap(home[:, 1])
    starts, pieces = [], []
    for c, block in ((core, home[:, 0]), (1 - core, home_far)):
        for k in range(nz):
            starts.append((c * nz + grid.far_z(k)) * local)
            pieces.append(block[k])
    attn_out = place(pieces, starts, 1)

    def all_four(block):
        two = jnp.concatenate([block, grid.yswap(block)], axis=0)
        return jnp.concatenate([two, grid.cswap(two)], axis=0)

    def sum_four(partial):
        half = partial[: 2 * rows] + grid.cswap(partial[2 * rows :].astype(BF16)).astype(F32)
        return half[:rows] + grid.yswap(half[rows:].astype(BF16)).astype(F32)

    middle = embedded + (dot(attn_out, w_proj, NT) + vecs[4])
    n2, s2 = normalize(middle)
    normed_two = all_four((n2 * vecs[5] + vecs[6]).astype(BF16))
    gz_own, gz_far = split(out_grad, 0, y)
    gz_two = jnp.concatenate([gz_own, gz_far], axis=0)
    gz = jnp.concatenate([gz_two, grid.cswap(gz_two)], axis=0)
    hidden = dot(normed_two, w_up) + up_full
    cdf = 0.5 * (1.0 + lax.erf(hidden * (0.5**0.5)))
    active = (hidden * cdf).astype(BF16)
    slope = cdf + hidden * (jnp.exp(-0.5 * hidden * hidden) * ((0.5 / jnp.pi) ** 0.5))
    grad_hidden = (dot(gz, w_down) * slope).astype(BF16)
    grad_n2 = sum_four(dot(grad_hidden, w_up, NT))
    block_out = (middle + (sum_four(dot(active, w_down, NT)) + vecs[7])).astype(BF16)
    block_out = jnp.concatenate(in_order(block_out, grid.yswap(block_out), y), axis=0)

    def give(gradient):
        mine = grid.scatter(gradient.astype(BF16).reshape(nz, nx, 2 * part, -1))
        keep, send = split(mine, 0, core)
        other = grid.cswap(send.astype(BF16)).astype(F32)
        return jnp.concatenate(in_order(keep, other, core), axis=1)

    d_up = give(dot(normed_two, grad_hidden, TN))
    d_down = give(dot(gz, active, TN))

    grad_top = gz_own.astype(F32)
    grad_middle = grad_top + norm_back(n2, s2, vecs[5], grad_n2)
    grad_branch = grad_middle.astype(BF16)
    grad_attn = dot(grad_branch, w_proj).astype(BF16)
    near, send = split(grad_attn, 1, core)
    far = grid.cswap(send)
    pair = jnp.stack([near, far]).reshape(2, rows, nz, local)
    d_out = jnp.stack(
        [pick(pair, grid.z, 2)] + [grid.zshift(pick(pair, grid.far_z(k), 2), k) for k in range(1, nz)], axis=1
    ).reshape(2 * nz * rows, local)
    delta = jnp.sum((d_out.astype(F32) * attn_full).reshape(2 * nz * rows, -1, HD), axis=2)
    delta = jnp.pad(jnp.transpose(delta), ((0, 8 - delta.shape[1]), (0, 0)))
    grad_q, grad_kv_all = attend_back(q, qcode, kcode, d_out, lse, delta, kv_pieces)
    grad_kv_all = grad_kv_all.reshape(nx, 2, 2 * nz * rows, 2 * local)
    two = grad_kv_all[0].astype(F32)
    for j in range(1, nx):
        two = two + grid.xshift(grad_kv_all[j], -j).astype(F32)
    grad_kv = (two[0] + grid.yswap(two[1].astype(BF16)).astype(F32)).astype(BF16)
    grad_stack = jnp.concatenate([grad_q, grad_kv], axis=1)

    part_n1 = dot(grad_stack, w_qkv, NT).astype(BF16)
    part_n1 = (part_n1[: nz * rows].astype(F32) + grid.cswap(part_n1[nz * rows :]).astype(F32)).reshape(nz, rows, width)
    low = part_n1.astype(BF16)
    grad_n1 = part_n1[0]
    for k in range(1, nz):
        grad_n1 = grad_n1 + grid.zshift(low[k], -k).astype(F32)

    dp = dot(grad_branch, attn_out, TN).astype(BF16).reshape(chips, 2, part, 2, -1)
    dp = pick(dp, core, 1).astype(F32) + grid.cswap(pick(dp, 1 - core, 1)).astype(F32)
    dp_low = dp.astype(BF16)
    dp = pick(dp, y, 2) + grid.yswap(pick(dp_low, 1 - y, 2)).astype(F32)
    d_proj = grid.scatter(dp.astype(BF16).reshape(nz, nx, part, -1))

    dw = dot(normed_one, grad_stack, TN).astype(BF16).reshape(nz, nx, 2, part, -1)
    dw_same, dw_other = pick(dw, core, 2), pick(dw, 1 - core, 2)
    from_spin = grid.spin(jnp.where(at_home, dw_other, dw_same), back=True)
    from_cross = grid.cross(dw_other)
    dw = from_spin.astype(F32) + jnp.where(at_home, dw_same, from_cross).astype(F32)
    dw_low = dw.astype(BF16)
    dw = pick(dw, grid.x, 1)
    for j in range(1, nx):
        dw = dw + grid.xshift(pick(dw_low, grid.far_x(j), 1), j).astype(F32)
    dw = dw.astype(BF16)
    dw_pieces = [pick(dw, grid.z, 0)] + [grid.zshift(pick(dw, grid.far_z(k), 0), k) for k in range(1, nz)]
    g_qkv = place_qkv(dw_pieces, [grid.far_z(-k) * local for k in range(nz)])

    input_grad = grad_middle + norm_back(n1, s1, vecs[2], grad_n1)
    lead_own = lead_time[:rows, None]
    sums = jnp.stack(
        [
            jnp.sum(input_grad * lead_own, axis=0),
            jnp.sum(input_grad, axis=0),
            jnp.sum(grad_n1 * n1, axis=0),
            jnp.sum(grad_n1, axis=0),
            jnp.sum(grad_branch.astype(F32), axis=0),
            jnp.sum(grad_n2 * n2, axis=0),
            jnp.sum(grad_n2, axis=0),
            jnp.sum(grad_top, axis=0),
        ]
    )
    sums = sums + grid.yswap(sums)
    sums = sums + grid.cswap(sums)
    sums = grid.scatter(jnp.transpose(sums.reshape(n_vec, nz, nx, 2 * part), (1, 2, 0, 3)))
    sums = split(sums, 1, core)[0]

    up_sum = jnp.sum(grad_hidden.astype(F32), axis=0)
    stack_sum = jnp.sum(grad_stack.astype(F32), axis=0)
    qv_sum = jnp.concatenate([stack_sum[:local], stack_sum[2 * local :]])
    qv_sum = qv_sum + grid.yswap(qv_sum)
    bias = jnp.concatenate([up_sum, qv_sum])
    bias_x = bias
    for j in range(1, nx):
        bias_x = bias_x + grid.xshift(bias, j)
    bias_z = jnp.stack([bias_x] + [grid.zshift(bias_x, k) for k in range(1, nz)])
    n_hidden = grad_hidden.shape[1]
    up_sum = jnp.sum(bias_z[:, :n_hidden], axis=0)
    to_z = (jnp.arange(nz)[:, None] == grid.far_z(-jnp.arange(nz))[None, :]).astype(F32)
    qv_sum = jnp.sum(to_z[:, :, None] * bias_z[None, :, n_hidden:], axis=1)
    bias = jnp.concatenate([up_sum, qv_sum.reshape(-1)])
    bias_far = grid.cswap(bias)
    up_sum = jnp.concatenate(in_order(bias[:n_hidden], bias_far[:n_hidden], core)).reshape(-1, HD)
    qv_sum = jnp.where(at_home, bias[n_hidden:], bias_far[n_hidden:]).reshape(nz, 2, -1, HD)
    qv_sum = jnp.transpose(qv_sum, (1, 0, 2, 3)).reshape(2, -1, HD)
    each = HD // sp
    g_up_bias = lax.dynamic_slice_in_dim(up_sum, grid.me * each, each, 1)
    g_qv_bias = lax.dynamic_slice_in_dim(qv_sum, grid.me * each, each, 2)

    input_grad = input_grad.astype(BF16)
    input_grad = jnp.concatenate(in_order(input_grad, grid.yswap(input_grad), y), axis=0).astype(F32)
    return (
        block_out,
        input_grad,
        g_qkv,
        g_qv_bias,
        jnp.transpose(d_proj),
        sums[4],
        d_up,
        g_up_bias,
        jnp.transpose(d_down),
        sums[7],
        sums[2],
        sums[3],
        sums[5],
        sums[6],
        sums[0],
        sums[1],
    )


def solution(mesh):
    placed = (
        P("sp", None),
        P("sp"),
        P(),
        P(None, "sp", "tp"),
        P(None, "tp", "sp"),
        P("tp", "sp"),
        P("sp"),
        P("sp", "tp"),
        P("tp", "sp"),
        P("tp", "sp"),
        P("sp"),
        P("sp"),
        P("sp"),
        P("sp"),
        P("sp"),
        P("sp"),
        P("sp"),
        P("sp", None),
    )
    return jax.shard_map(
        per_device,
        mesh=mesh,
        in_specs=placed,
        out_specs=(
            P("sp", None),
            P("sp", None),
            P(None, "sp", "tp"),
            P(None, "tp", "sp"),
            P("tp", "sp"),
            P("sp"),
            P("sp", "tp"),
            P("tp", "sp"),
            P("tp", "sp"),
            P("sp"),
            P("sp"),
            P("sp"),
            P("sp"),
            P("sp"),
            P("sp"),
            P("sp"),
        ),
        check_vma=False,
    )
```

```python
import functools

import jax
import jax.numpy as jnp
from jax import lax
from jax.experimental import pallas as pl
from jax.experimental.pallas import tpu as pltpu
from jax.sharding import PartitionSpec as P

HD = 64
EPSILON = 1e-05
EXCLUDED = -1e30
F32 = jnp.float32
BF16 = jnp.bfloat16
NN = (((1,), (0,)), ((), ()))
NT = (((1,), (1,)), ((), ()))
TN = (((0,), (0,)), ((), ()))


def dot(left, right, dims=NN):
    return lax.dot_general(left, right, dims, preferred_element_type=F32)


SP = ("z", "x", "core")


class Grid:
    def __init__(self):
        self.nz = lax.axis_size("z")
        self.nx = lax.axis_size("x")
        self.chips = self.nz * self.nx
        self.sp = 2 * self.chips
        me = lax.axis_index(SP)
        self.me = me
        self.core = me % 2
        self.x = (me // 2) % self.nx
        self.z = me // (2 * self.nx)
        self.y = lax.axis_index("tp")

    def _move(self, block, dz, dx, flip):
        pairs = []
        for i in range(self.sp):
            z, x, c = i // (2 * self.nx), (i // 2) % self.nx, i % 2
            to = (((z + dz) % self.nz) * self.nx + (x + dx) % self.nx) * 2 + (1 - c if flip else c)
            pairs.append((i, to))
        return lax.ppermute(block, SP, pairs)

    def zshift(self, block, k):
        return self._move(block, k, 0, False)

    def xshift(self, block, k):
        return self._move(block, 0, k, False)

    def cswap(self, block):
        return self._move(block, 0, 0, True)

    def yswap(self, block):
        return lax.ppermute(block, "tp", [(0, 1), (1, 0)])

    def _pairs(self, route):
        pairs = []
        for chip in range(self.chips):
            for (c, y), (to_c, to_y) in route:
                pairs.append(((chip * 2 + c) * 2 + y, (chip * 2 + to_c) * 2 + to_y))
        return pairs

    def spin(self, block, back=False):
        route = []
        for b in (0, 1):
            route += [((b, b), (b, 1 - b)), ((1 - b, b), (b, b))]
        if back:
            route = [(to, at) for at, to in route]
        return lax.ppermute(block, SP + ("tp",), self._pairs(route))

    def cross(self, block):
        route = [((1 - b, b), (b, 1 - b)) for b in (0, 1)]
        return lax.ppermute(block, SP + ("tp",), self._pairs(route))

    def far_z(self, k):
        return (self.z + k) % self.nz

    def far_x(self, j):
        return (self.x + j) % self.nx

    def gather(self, block):
        columns = [block] + [self.zshift(block, k) for k in range(1, self.nz)]
        return [p for b in columns for p in [b] + [self.xshift(b, j) for j in range(1, self.nx)]]

    def chip_order(self):
        order = jnp.arange(self.chips)
        return self.far_z(-(order // self.nx)) * self.nx + self.far_x(-(order % self.nx))

    def scatter(self, pieces):
        total = pick(pieces, self.x, 1).astype(F32)
        for j in range(1, self.nx):
            total = total + self.xshift(pick(pieces, self.far_x(j), 1), j).astype(F32)
        low = total.astype(pieces.dtype)
        mine = pick(total, self.z, 0)
        for k in range(1, self.nz):
            mine = mine + self.zshift(pick(low, self.far_z(k), 0), k).astype(F32)
        return mine


def pick(array, index, axis):
    return lax.dynamic_index_in_dim(array, index, axis, keepdims=False)


def normalize(values):
    center = values - jnp.mean(values, axis=-1, keepdims=True)
    spread = jnp.mean(center * center, axis=-1, keepdims=True)
    scale = lax.rsqrt(spread + EPSILON)
    return center * scale, scale


def norm_back(normed, scale, gain, grad):
    scaled = grad * gain
    mean_one = jnp.mean(scaled, axis=-1, keepdims=True)
    mean_two = jnp.mean(scaled * normed, axis=-1, keepdims=True)
    return (scaled - mean_one - normed * mean_two) * scale


def place_qkv_kernel(starts_ref, *refs):
    pieces, out_ref = refs[:-1], refs[-1]
    for i, piece in enumerate(pieces):
        size = out_ref.shape[2] // len(pieces)
        span = pl.ds(pl.multiple_of(starts_ref[i], size), size)
        for c in range(3):
            out_ref[c, :, span] = piece[:, c * size : (c + 1) * size].astype(F32)


def place_qkv(pieces, starts, columns):
    rows = pieces[0].shape[0]
    vmem = pl.BlockSpec(memory_space=pltpu.VMEM)
    return pl.pallas_call(
        place_qkv_kernel,
        out_shape=jax.ShapeDtypeStruct((3, rows, columns * len(pieces)), F32),
        in_specs=[pl.BlockSpec(memory_space=pltpu.SMEM)] + [vmem] * len(pieces),
        out_specs=vmem,
        name="place_qkv",
    )(jnp.stack(starts).astype(jnp.int32), *pieces)


def lane_in_head(shape, head):
    lanes = lax.broadcasted_iota(jnp.int32, shape, 1)
    return (lanes // HD) == (head % 2)


def pair_lanes(pair):
    return slice(pair * 2 * HD, (pair + 1) * 2 * HD)


STEP = 384
SMEM = pl.BlockSpec(memory_space=pltpu.SMEM)


def in_vmem(count):
    return [pl.BlockSpec(memory_space=pltpu.VMEM)] * count


def local_kernel(kernel, name, out_shape, operands, scalars=1, scratch=(), flops=0, megabytes=48):
    single = not isinstance(out_shape, tuple)
    return pl.pallas_call(
        kernel,
        out_shape=out_shape,
        in_specs=[SMEM] * scalars + in_vmem(len(operands) - scalars),
        out_specs=in_vmem(1)[0] if single else tuple(in_vmem(len(out_shape))),
        scratch_shapes=list(scratch),
        compiler_params=pltpu.CompilerParams(vmem_limit_bytes=megabytes * 1024 * 1024),
        cost_estimate=pl.CostEstimate(flops=flops, bytes_accessed=1 << 16, transcendentals=0),
        name=name,
    )(*operands)


def shape(dims, kind=BF16):
    return jax.ShapeDtypeStruct(tuple(dims), kind)


def turned(index, size):
    return lax.rem(index + size, size)


def enter_kernel(nz, nx, n_vec, part, at_ref, hour_ref, *refs):
    token_refs, refs = refs[: nz + 1], refs[nz + 1 :]
    pack_refs, refs = refs[: nx - 1], refs[nx - 1 :]
    weight_refs, refs = refs[:2], refs[2:]
    normed_ref, unit_ref, scale_ref, lead_ref, first_ref, vec_ref, weight_ref, q_ref, kv_ref = refs[:9]
    packs = refs[9]
    z, x, c = at_ref[0], at_ref[1], at_ref[2]
    rows, width = first_ref.shape
    tall = packs.shape[3]
    local = q_ref.shape[1]
    aux = slice(width, width + 128)
    for k in range(nz):
        packs[0, 0, k] = token_refs[k][:tall, aux]
        packs[0, 1, k] = token_refs[nz][k, :tall, aux]
    for j in range(1, nx):
        packs[j] = pack_refs[j - 1][...]
    for dev in range(2 * nz * nx):
        dev_z, dev_x, dev_c = dev // (2 * nx), (dev // 2) % nx, dev % 2
        block = packs[turned(x - dev_x, nx), turned(c - dev_c, 2), turned(z - dev_z, nz)]
        vec_ref[:, dev * part : (dev + 1) * part] = block[:n_vec, 64 : 64 + part].astype(F32)
    for n in range(2 * nz):
        ref = token_refs[n] if n < nz else token_refs[nz].at[n - nz]
        span = slice(n * rows, (n + 1) * rows)
        segment = ref[:, aux][:, :1].astype(F32)
        lead = jnp.zeros_like(segment)
        for i in range(hour_ref.shape[0]):
            lead = jnp.where(segment == float(i), hour_ref[i], lead)
        lead_ref[span, :] = lead
        value = ref[:, :width].astype(F32) + lead * vec_ref[0:1, :] + vec_ref[1:2, :]
        if n == 0:
            first_ref[...] = value
        unit, scale = normalize(value)
        scale_ref[span, :] = scale
        unit_ref[span, :] = unit.astype(BF16)
        normed_ref[span, :] = (unit * vec_ref[2:3, :] + vec_ref[3:4, :]).astype(BF16)
    for p, ref in enumerate(weight_refs):
        parity = c if p == 0 else 1 - c
        for j in range(nx):
            for k in range(nz):
                row = ((turned(z - k, nz) * nx + turned(x - j, nx)) * 2 + parity) * part
                weight_ref[pl.ds(pl.multiple_of(row, part), part), :] = ref[j, k]
    made = dot(normed_ref[...], weight_ref[...])
    q_ref[...] = made[:, :local]
    kv_ref[...] = made[:, local:].astype(BF16)


def enter(at, hours, tokens, packs, same, other, n_vec, part):
    nz, nx = len(tokens) - 1, len(packs) + 1
    rows, wide = tokens[0].shape
    width = wide - 128
    count = 2 * nz * rows
    local = same.shape[-1] // 3
    tall = packs[0].shape[2]
    return local_kernel(
        functools.partial(enter_kernel, nz, nx, n_vec, part),
        "enter",
        (
            shape((count, width)),
            shape((count, width)),
            shape((count, 1), F32),
            shape((count, 1), F32),
            shape((rows, width), F32),
            shape((n_vec, width), F32),
            shape((width, 3 * local)),
            shape((count, local), F32),
            shape((count, 2 * local)),
        ),
        (at, hours, *tokens, *packs, same, other),
        scalars=2,
        scratch=[pltpu.VMEM((nx, 2, nz, tall, 128), BF16)],
    )


def attend_kernel(pieces, heads, nz, at_ref, q_ref, bias_ref, qcode_ref, kcode_ref, *refs):
    kv_refs = refs[:pieces]
    out_ref, lse_ref, low_ref, send_ref = refs[pieces : pieces + 4]
    kaug, vturn, qaug, acc, stat = refs[pieces + 4 :]
    width = heads * HD
    count = q_ref.shape[0]
    rows = count // (2 * nz)
    steps = kv_refs[0].shape[0] // STEP
    low_ref[...] = (q_ref[...] + bias_ref[0:1, :]).astype(BF16) * jnp.asarray(HD ** (-0.5), BF16)
    for n in range(pieces * steps):
        block = kv_refs[n // steps]
        span_in = pl.ds((n % steps) * STEP, STEP)
        span = pl.ds(n * STEP, STEP)
        code = kcode_ref[span, :]
        for p in range(heads // 2):
            keys = block[span_in, pair_lanes(p)]
            for h in (2 * p, 2 * p + 1):
                kaug[h, span, :] = jnp.where(lane_in_head(keys.shape, h), keys, code)
        vturn[n] = jnp.transpose(block[span_in, width:])
    for p in range(heads // 2):
        part = low_ref[:, pair_lanes(p)]
        for h in (2 * p, 2 * p + 1):
            qaug[h] = jnp.where(lane_in_head(part.shape, h), part, qcode_ref[...])
    acc[...] = jnp.zeros_like(acc)
    stat[0] = jnp.full(stat.shape[1:], EXCLUDED, F32)
    stat[1] = jnp.zeros(stat.shape[1:], F32)

    def chunk(i, carry):
        for h in range(heads):
            scores = dot(kaug[h, pl.ds(i * STEP, STEP), :], qaug[h], NT)
            top = stat[0, h : h + 1, :]
            new_top = jnp.maximum(top, jnp.max(scores, axis=0, keepdims=True))
            weight = jnp.exp(scores - new_top)
            rescale = jnp.exp(top - new_top)
            stat[0, h : h + 1, :] = new_top
            stat[1, h : h + 1, :] = stat[1, h : h + 1, :] * rescale + jnp.sum(weight, axis=0, keepdims=True)
            span = slice(h * HD, (h + 1) * HD)
            acc[span, :] = acc[span, :] * rescale + dot(vturn[i, span, :], weight.astype(BF16))
        return carry

    lax.fori_loop(0, pieces * steps, chunk, 0)
    for h in range(heads):
        span = slice(h * HD, (h + 1) * HD)
        acc[span, :] = acc[span, :] / stat[1, h : h + 1, :]
    out_ref[...] = jnp.transpose(acc[...])
    lse_ref[...] = stat[0] + jnp.log(jnp.maximum(stat[1], 1e-37))
    z = at_ref[0]
    for r in range(2):
        for k in range(nz):
            span = slice((r * nz + k) * rows, (r * nz + k + 1) * rows)
            send_ref[turned(z - k, nz), r] = (out_ref[span, :] + bias_ref[1:2, :]).astype(BF16)


def attend(at, nz, q, bias, qcode, kcode, kv_pieces):
    count, width = q.shape
    heads = width // HD
    keys = kcode.shape[0]
    return local_kernel(
        functools.partial(attend_kernel, len(kv_pieces), heads, nz),
        "attend",
        (
            shape((count, width), F32),
            shape((8, count), F32),
            shape((count, width)),
            shape((nz, 2, count // (2 * nz), width)),
        ),
        (at, q, bias, qcode, kcode, *kv_pieces),
        scratch=[
            pltpu.VMEM((heads, keys, 2 * HD), BF16),
            pltpu.VMEM((keys // STEP, width, STEP), BF16),
            pltpu.VMEM((heads, count, 2 * HD), BF16),
            pltpu.VMEM((width, count), F32),
            pltpu.VMEM((2, 8, count), F32),
        ],
    )


def attend_back_kernel(
    nx, heads, nz, at_ref, q_ref, qcode_ref, kcode_ref, got_ref, full_ref, lse_ref, *refs
):
    pieces = 2 * nx
    kv_refs = refs[:pieces]
    dq_ref, dkv_refs = refs[pieces], refs[pieces + 1 : pieces + 1 + nx]
    kaug, kturn, vals, qaug, qmask, domask, acc, dout, delta = refs[pieces + 1 + nx :]
    width = heads * HD
    count = q_ref.shape[0]
    rows = count // (2 * nz)
    steps = kv_refs[0].shape[0] // STEP
    z = at_ref[0]
    for r in range(2):
        for k in range(nz):
            span = slice((r * nz + k) * rows, (r * nz + k + 1) * rows)
            dout[span, :] = got_ref[turned(z - k, nz), r]
    product = dout[...].astype(F32) * full_ref[...]
    head_rows = lax.broadcasted_iota(jnp.int32, (8, width), 0)
    head_lanes = lax.broadcasted_iota(jnp.int32, (8, width), 1) // HD
    delta[...] = lax.dot_general(
        (head_rows == head_lanes).astype(F32),
        product,
        NT,
        precision=lax.Precision.HIGHEST,
        preferred_element_type=F32,
    )
    for n in range(pieces * steps):
        block = kv_refs[n // steps]
        span_in = pl.ds((n % steps) * STEP, STEP)
        span = pl.ds(n * STEP, STEP)
        code = kcode_ref[span, :]
        for p in range(heads // 2):
            keys = block[span_in, pair_lanes(p)]
            for h in (2 * p, 2 * p + 1):
                kaug[h, span, :] = jnp.where(lane_in_head(keys.shape, h), keys, code)
        kturn[n] = jnp.transpose(block[span_in, :width])
        vals[span, :] = block[span_in, width:]
    for p in range(heads // 2):
        part = q_ref[:, pair_lanes(p)]
        dpart = dout[:, pair_lanes(p)]
        for h in (2 * p, 2 * p + 1):
            inside = lane_in_head(part.shape, h)
            qaug[h] = jnp.where(inside, part, qcode_ref[...])
            qmask[h] = jnp.where(inside, part, jnp.zeros_like(part))
            domask[h] = jnp.where(inside, dpart, jnp.zeros_like(dpart))
    acc[...] = jnp.zeros_like(acc)
    each = 2 * steps
    for j in range(nx):

        def chunk(n, carry, j=j):
            i = j * each + n
            span = pl.ds(i * STEP, STEP)
            span_out = pl.ds(n * STEP, STEP)
            for p in range(heads // 2):
                dkey = dval = None
                for h in (2 * p, 2 * p + 1):
                    scores = dot(kaug[h, span, :], qaug[h], NT)
                    prob = jnp.exp(scores - lse_ref[h : h + 1, :])
                    dprob = dot(vals[span, pair_lanes(p)], domask[h], NT)
                    dscore = (prob * (dprob - delta[h : h + 1, :])).astype(BF16)
                    add_val = dot(prob.astype(BF16), domask[h])
                    add_key = dot(dscore, qmask[h])
                    dval = add_val if dval is None else dval + add_val
                    dkey = add_key if dkey is None else dkey + add_key
                    turn = slice(h * HD, (h + 1) * HD)
                    acc[turn, :] += dot(kturn[i, turn, :], dscore)
                dkv_refs[j][span_out, pair_lanes(p)] = dkey.astype(BF16)
                dkv_refs[j][span_out, slice(width + p * 2 * HD, width + (p + 1) * 2 * HD)] = dval.astype(BF16)
            return carry

        lax.fori_loop(0, each, chunk, 0)
    dq_ref[...] = (jnp.transpose(acc[...]) * (HD ** (-0.5))).astype(BF16)


def attend_back(at, nz, q, qcode, kcode, got, full, lse, kv_pieces):
    count, width = q.shape
    heads = width // HD
    keys = kcode.shape[0]
    nx = len(kv_pieces) // 2
    return local_kernel(
        functools.partial(attend_back_kernel, nx, heads, nz),
        "attend_back",
        (shape((count, width)),) + (shape((2 * count, 2 * width)),) * nx,
        (at, q, qcode, kcode, got, full, lse, *kv_pieces),
        scratch=[
            pltpu.VMEM((heads, keys, 2 * HD), BF16),
            pltpu.VMEM((keys // STEP, width, STEP), BF16),
            pltpu.VMEM((keys, width), BF16),
            pltpu.VMEM((heads, count, 2 * HD), BF16),
            pltpu.VMEM((heads, count, 2 * HD), BF16),
            pltpu.VMEM((heads, count, 2 * HD), BF16),
            pltpu.VMEM((width, count), F32),
            pltpu.VMEM((count, width), BF16),
            pltpu.VMEM((8, count), F32),
        ],
        megabytes=56,
    )


def whole_proj_kernel(nz, nx, part, at_ref, own_ref, far_ref, out_ref):
    z, x, c, y = at_ref[0], at_ref[1], at_ref[2], at_ref[3]
    half = out_ref.shape[1] // 2
    for p, ref in enumerate((own_ref, far_ref)):
        parity = c if p == 0 else 1 - c
        for w in range(2):
            column = pl.multiple_of(turned(y - w, 2) * half, half)
            for j in range(nx):
                for k in range(nz):
                    row = ((turned(z - k, nz) * nx + turned(x - j, nx)) * 2 + parity) * part
                    out_ref[pl.ds(pl.multiple_of(row, part), part), pl.ds(column, half)] = ref[w, j, k]


def whole_proj(at, own, far):
    _, nx, nz, part, half = own.shape
    return local_kernel(
        functools.partial(whole_proj_kernel, nz, nx, part),
        "whole_proj",
        shape((2 * nx * nz * part, 2 * half)),
        (at, own, far),
    )


def project_kernel(at_ref, got_ref, far_ref, weight_ref, first_ref, vec_ref, *refs):
    attn_ref, unit_ref, scale_ref, normed_ref, middle_ref = refs
    nz, _, _, local = got_ref.shape
    c = at_ref[2]
    for block in range(2):
        base = (c if block == 0 else 1 - c) * nz
        for z in range(nz):
            lane = pl.multiple_of((base + z) * local, local)
            attn_ref[:, pl.ds(lane, local)] = got_ref[z, 0] if block == 0 else far_ref[z]
    middle = first_ref[...] + (dot(attn_ref[...], weight_ref[...], NT) + vec_ref[4:5, :])
    middle_ref[...] = middle
    unit, scale = normalize(middle)
    unit_ref[...] = unit
    scale_ref[...] = scale
    normed_ref[...] = (unit * vec_ref[5:6, :] + vec_ref[6:7, :]).astype(BF16)


def project(at, got, far, weight, first, vecs):
    rows, width = first.shape
    return local_kernel(
        project_kernel,
        "project",
        (
            shape((rows, width)),
            shape((rows, width), F32),
            shape((rows, 1), F32),
            shape((rows, width)),
            shape((rows, width), F32),
        ),
        (at, got, far, weight, first, vecs),
    )


def feed_kernel(bias_ref, own_ref, near_ref, far_ref, gz_ref, weight, *refs):
    normed_ref, act_ref, gh_ref, sum_ref, keep_n_ref, send_n_ref, keep_o_ref, send_o_ref = refs[:8]
    back, out = refs[8:]
    rows = own_ref.shape[0]
    hidden_size = act_ref.shape[1]
    normed_ref[:rows, :] = own_ref[...]
    normed_ref[rows : 2 * rows, :] = near_ref[...]
    normed_ref[2 * rows :, :] = far_ref[...]
    step = 256
    for n in range(hidden_size // step):
        up = slice(n * step, (n + 1) * step)
        down = slice(hidden_size + n * step, hidden_size + (n + 1) * step)
        value = dot(normed_ref[...], weight[:, up]) + bias_ref[:, up]
        cdf = 0.5 * (1.0 + lax.erf(value * (0.5**0.5)))
        act = (value * cdf).astype(BF16)
        slope = cdf + value * (jnp.exp(-0.5 * value * value) * ((0.5 / jnp.pi) ** 0.5))
        low = (dot(gz_ref[...], weight[:, down]) * slope).astype(BF16)
        act_ref[:, up] = act
        gh_ref[:, up] = low
        sum_ref[:, up] = jnp.sum(low.astype(F32), axis=0, keepdims=True)
        add_back = dot(low, weight[:, up], NT)
        add_out = dot(act, weight[:, down], NT)
        if n == 0:
            back[...] = add_back
            out[...] = add_out
        else:
            back[...] += add_back
            out[...] += add_out
    keep_n_ref[...] = back[: 2 * rows, :]
    send_n_ref[...] = back[2 * rows :, :].astype(BF16)
    keep_o_ref[...] = out[: 2 * rows, :]
    send_o_ref[...] = out[2 * rows :, :].astype(BF16)


def feed(bias, own, near, far, gz, weight):
    count, width = gz.shape
    hidden_size = bias.shape[1]
    half = count // 2
    return local_kernel(
        feed_kernel,
        "feed",
        (
            shape((count, width)),
            shape((count, hidden_size)),
            shape((count, hidden_size)),
            shape((1, hidden_size), F32),
            shape((half, width), F32),
            shape((half, width)),
            shape((half, width), F32),
            shape((half, width)),
        ),
        (bias, own, near, far, gz, weight),
        scalars=0,
        scratch=[pltpu.VMEM((count, width), F32), pltpu.VMEM((count, width), F32)],
        megabytes=56,
    )


def outer_kernel(normed_ref, gh_ref, gz_ref, act_ref, out_ref):
    hidden_size = gh_ref.shape[1]
    step = 256
    for base, left_ref, right_ref in ((0, normed_ref, gh_ref), (hidden_size, gz_ref, act_ref)):
        for n in range(hidden_size // step):
            made = dot(left_ref[...], right_ref[:, n * step : (n + 1) * step], TN)
            out_ref[:, base + n * step : base + (n + 1) * step] = made.astype(BF16)


def outer(normed, gh, gz, act):
    return local_kernel(
        outer_kernel, "outer", shape((normed.shape[1], 2 * gh.shape[1])), (normed, gh, gz, act), scalars=0
    )


def branch_kernel(at_ref, half_ref, near_ref, unit_ref, scale_ref, vec_ref, gz_ref, weight_ref, *refs):
    middle_ref, branch_ref, mine_ref, send_ref, sum_ref = refs
    rows = half_ref.shape[0] // 2
    nz, _, local = mine_ref.shape
    c = at_ref[2]
    grad = half_ref[:rows, :] + near_ref[...].astype(F32)
    top = gz_ref[...].astype(F32)
    unit = unit_ref[...]
    middle = top + norm_back(unit, scale_ref[...], vec_ref[5:6, :], grad)
    middle_ref[...] = middle
    low = middle.astype(BF16)
    branch_ref[...] = low
    made = dot(low, weight_ref[...]).astype(BF16)
    for h in range(2):
        for z in range(nz):
            block = made[:, (h * nz + z) * local : (h * nz + z + 1) * local]

            @pl.when(c == h)
            def _():
                mine_ref[z] = block

            @pl.when(c != h)
            def _():
                send_ref[z] = block

    sum_ref[...] = jnp.concatenate(
        [
            jnp.sum(low.astype(F32), axis=0, keepdims=True),
            jnp.sum(grad * unit, axis=0, keepdims=True),
            jnp.sum(grad, axis=0, keepdims=True),
            jnp.sum(top, axis=0, keepdims=True),
        ],
        axis=0,
    )


def branch(at, nz, half, near, unit, scale, vecs, gz, weight):
    rows, width = unit.shape
    local = width // (2 * nz)
    return local_kernel(
        branch_kernel,
        "branch",
        (
            shape((rows, width), F32),
            shape((rows, width)),
            shape((nz, rows, local)),
            shape((nz, rows, local)),
            shape((4, width), F32),
        ),
        (at, half, near, unit, scale, vecs, gz, weight),
    )


def leave_kernel(dq_ref, two_ref, near_ref, weight_ref, stack_ref, full_ref, send_ref):
    count, local = dq_ref.shape
    stack_ref[:, :local] = dq_ref[...]
    stack_ref[:, local:] = (two_ref[:count, :] + near_ref[...].astype(F32)).astype(BF16)
    full_ref[...] = dot(stack_ref[...], weight_ref[...], NT)
    send_ref[...] = full_ref[count // 2 :, :].astype(BF16)


def leave(dq, two, near, weight):
    count, local = dq.shape
    width = weight.shape[0]
    return local_kernel(
        leave_kernel,
        "leave",
        (shape((count, 3 * local)), shape((count, width), F32), shape((count // 2, width))),
        (dq, two, near, weight),
        scalars=0,
    )


def close_kernel(rows, full_ref, unit_ref, scale_ref, lead_ref, vec_ref, middle_ref, normed_ref, stack_ref, *refs):
    sum_ref, bias_ref, out_ref = refs
    count, width = full_ref.shape
    lead_row = jnp.zeros((4, width), F32)
    for n in range(count // rows):
        span = slice(n * rows, (n + 1) * rows)
        grad = full_ref[span, :]
        unit = unit_ref[span, :].astype(F32)
        back = norm_back(unit, scale_ref[span, :], vec_ref[2:3, :], grad)
        if n == 0:
            back = back + middle_ref[...]
        lead_row = lead_row + jnp.concatenate(
            [
                jnp.sum(back * lead_ref[span, :], axis=0, keepdims=True),
                jnp.sum(back, axis=0, keepdims=True),
                jnp.sum(grad * unit, axis=0, keepdims=True),
                jnp.sum(grad, axis=0, keepdims=True),
            ],
            axis=0,
        )
    sum_ref[...] = lead_row
    bias_ref[...] = jnp.sum(stack_ref[...].astype(F32), axis=0, keepdims=True)
    out_ref[...] = dot(normed_ref[...], stack_ref[...], TN).astype(BF16)


def close(rows, full, unit, scale, lead, vecs, middle, normed, stack):
    width = full.shape[1]
    return local_kernel(
        functools.partial(close_kernel, rows),
        "close",
        (shape((4, width), F32), shape((1, stack.shape[1]), F32), shape((width, stack.shape[1]))),
        (full, unit, scale, lead, vecs, middle, normed, stack),
        scalars=0,
    )


def after(block, *before):
    return lax.optimization_barrier((block,) + before)[0]


def per_device(
    tokens,
    segment_ids,
    lead_hours,
    qkv_weight,
    qv_bias,
    proj_weight,
    proj_bias,
    up_weight,
    up_bias,
    down_weight,
    down_bias,
    norm1_gain,
    norm1_bias,
    norm2_gain,
    norm2_bias,
    lead_weight,
    lead_bias,
    out_grad,
):
    grid = Grid()
    nz, nx, chips, sp = grid.nz, grid.nx, grid.chips, grid.sp
    core, y = grid.core, grid.y
    at = jnp.stack([grid.z, grid.x, core, y]).astype(jnp.int32)
    full_rows, width = tokens.shape
    rows = full_rows // 2
    part = norm1_gain.shape[0]
    each = HD // sp
    at_home = core == y

    def split(array, axis, index):
        half = array.shape[axis] // 2
        first = lax.slice_in_dim(array, 0, half, axis=axis)
        second = lax.slice_in_dim(array, half, 2 * half, axis=axis)
        return jnp.where(index == 0, first, second), jnp.where(index == 0, second, first)

    def in_order(own, other, index):
        return jnp.where(index == 0, own, other), jnp.where(index == 0, other, own)

    shard = jnp.transpose(qkv_weight.reshape(3, part, nz, -1), (2, 1, 0, 3)).reshape(nz, part, -1)
    wq_z = [pick(shard, grid.z, 0)] + [grid.zshift(pick(shard, grid.far_z(k), 0), k) for k in range(1, nz)]

    vectors = [lead_weight, lead_bias, norm1_gain, norm1_bias, proj_bias, norm2_gain, norm2_bias, down_bias]
    n_vec = len(vectors)
    n_qv, n_up = qv_bias.size // part, up_bias.size // part
    pack = jnp.concatenate(
        [
            jnp.stack(vectors),
            qv_bias.reshape(-1, part),
            up_bias.reshape(-1, part),
            segment_ids.astype(BF16).reshape(-1, part),
        ],
        axis=0,
    )
    pack_rows = pack.shape[0]
    tall = -(-pack_rows // 16) * 16
    pack = jnp.pad(pack, ((0, rows - pack_rows), (63, 128 - 64 - part)))
    own_segments = split(segment_ids, 0, y)[0]
    beside = jnp.concatenate([own_segments.astype(BF16)[:, None], pack], axis=1)
    own_tokens = jnp.concatenate([split(tokens, 0, y)[0], beside], axis=1)
    token_far = [grid.zshift(own_tokens, k) for k in range(1, nz)]
    token_z = jnp.stack([own_tokens] + token_far)
    token_c = grid.cswap(token_z)
    packs_own = jnp.stack([token_z[:, :tall, width:], token_c[:, :tall, width:]])
    packs_far = [grid.xshift(packs_own, j) for j in range(1, nx)]

    wq_z = jnp.stack(wq_z)
    wq_x = jnp.stack([wq_z] + [grid.xshift(wq_z, j) for j in range(1, nx)])
    wq_spin, wq_cross = grid.spin(wq_x), grid.cross(wq_x)
    wq_same = jnp.where(at_home, wq_x, wq_spin)
    wq_other = jnp.where(at_home, wq_spin, wq_cross)

    normed_one, unit_one, scale_one, lead, embedded, vecs, w_qkv, q_raw, kv = enter(
        at, lead_hours, [own_tokens] + token_far + [token_c], packs_far, wq_same, wq_other, n_vec, part
    )
    local = q_raw.shape[1]
    kv_far = grid.yswap(kv)
    kv_pieces = [kv, kv_far]
    for j in range(1, nx):
        kv_pieces += [grid.xshift(kv, j), grid.xshift(kv_far, j)]

    table = jnp.stack([packs_own] + packs_far)[:, :, :, n_vec:pack_rows, 64 : 64 + part].reshape(sp, -1)
    n = jnp.arange(sp)
    rel_j, rel_r, rel_k = n // (2 * nz), (n // nz) % 2, n % nz
    device = (grid.far_z(-rel_k) * nx + grid.far_x(-rel_j)) * 2 + (core + rel_r) % 2
    in_place = (jnp.arange(sp)[:, None] == device[None, :]).astype(BF16)
    table = dot(in_place, table).reshape(sp, -1, part)
    heads_local = qv_bias.shape[1]
    qv_all = jnp.transpose(table[:, :n_qv].reshape(sp, 2, heads_local, -1), (1, 2, 0, 3)).reshape(2, heads_local * HD)
    qv_far = grid.yswap(qv_all)
    qv_full = pick(jnp.where(at_home, qv_all, qv_far).reshape(2, nz, -1), grid.z, 1)
    seg_rows = table[:, n_qv + n_up :].reshape(sp * 2, rows)
    n = jnp.arange(nx * 2 * 2 * nz)
    k, r, w, j = n % nz, (n // nz) % 2, (n // (2 * nz)) % 2, n // (4 * nz)
    key_at = ((grid.far_z(-k) * nx + grid.far_x(-j)) * 2 + (core + r) % 2) * 2 + (y + w) % 2
    take = (key_at[:, None] == jnp.arange(2 * sp)[None, :]).astype(BF16)
    key_seg = dot(take, seg_rows.astype(BF16)).astype(jnp.int32).reshape(-1)
    query_seg = key_seg[: 2 * nz * rows]
    lanes = jnp.arange(2 * HD, dtype=jnp.int32) % HD
    kcode = jnp.where(key_seg[:, None] == lanes[None, :], 0.0, EXCLUDED).astype(BF16)
    qcode = (query_seg[:, None] == lanes[None, :]).astype(BF16)
    up_all = jnp.transpose(table[:, n_qv : n_qv + n_up].reshape(sp, up_bias.shape[0], -1), (1, 0, 2)).reshape(1, -1)
    up_full = split(up_all, 1, core)[0]

    up_shard, down_shard, _ = lax.optimization_barrier((up_weight, down_weight, wq_z))
    up_keep, up_send = split(up_shard, 1, core)
    down_keep, down_send = split(jnp.transpose(down_shard), 1, core)
    ff_far = grid.cswap(jnp.concatenate([up_send, down_send], axis=1))
    ff = jnp.concatenate(in_order(jnp.concatenate([up_keep, down_keep], axis=1), ff_far, core), axis=0)
    w_ff = lax.all_gather(after(ff, *token_far), ("z", "x"), axis=0, tiled=True)

    gz_own, gz_far = split(after(out_grad, kv), 0, y)
    gz_two = jnp.concatenate([gz_own, gz_far], axis=0)
    gz = jnp.concatenate([gz_two, grid.cswap(gz_two)], axis=0)

    wp = jnp.transpose(after(proj_weight, wq_spin, token_c))
    wp_z = jnp.stack([wp] + [grid.zshift(wp, k) for k in range(1, nz)])
    wp_z = after(wp_z, kv)
    wp_x = jnp.stack([wp_z] + [grid.xshift(wp_z, j) for j in range(1, nx)])
    wp_x = after(wp_x, kv_far)
    wp_own = jnp.stack([wp_x, grid.yswap(wp_x)])
    w_proj = whole_proj(at, wp_own, grid.cswap(wp_own))

    q_raw, up_full, gz = lax.optimization_barrier((q_raw, up_full, gz))
    attn_full, lse, q, attn_send = attend(at, nz, q_raw, qv_full, qcode, kcode, kv_pieces)
    attn_got = lax.all_to_all(attn_send, "z", 0, 0, tiled=True)
    attn_far = grid.cswap(attn_got[:, 1])
    attn_out, n2, s2, normed, middle = project(at, attn_got, attn_far, w_proj, embedded, vecs)
    near = grid.yswap(normed)
    far = grid.cswap(jnp.concatenate([normed, near], axis=0))
    normed_two, active, grad_hidden, up_sum, keep_n, send_n, keep_o, send_o = feed(up_full, normed, near, far, gz, w_ff)

    half_n = keep_n + grid.cswap(send_n).astype(F32)
    near_n = grid.yswap(half_n[rows:].astype(BF16))
    d_ff = lax.psum_scatter(
        outer(normed_two, grad_hidden, gz, active), ("z", "x"), scatter_dimension=0, tiled=True
    )
    grad_middle, grad_branch, mine, send, sums_two = branch(
        at, nz, half_n, near_n, n2, s2, vecs, gz[:rows], w_proj
    )
    theirs = grid.cswap(send)
    got = lax.all_to_all(jnp.stack([mine, theirs], axis=1), "z", 0, 0, tiled=True)

    back = attend_back(at, nz, q, qcode, kcode, got, attn_full, lse, kv_pieces)
    grad_q, grad_kv = back[0], back[1].astype(F32)
    for j in range(1, nx):
        grad_kv = grad_kv + grid.xshift(back[1 + j], -j).astype(F32)
    count = 2 * nz * rows
    near_kv = grid.yswap(grad_kv[count:].astype(BF16))
    grad_stack, part_full, part_send = leave(grad_q, grad_kv, near_kv, w_qkv)

    part_n1 = (part_full[: nz * rows] + grid.cswap(part_send).astype(F32)).reshape(nz, rows, width)
    low = part_n1.astype(BF16)
    n1_far = [grid.zshift(low[k], -k) for k in range(1, nz)]

    sums_one, stack_sum, d_wqkv = close(
        rows, part_full, unit_one, scale_one, lead, vecs, grad_middle, normed_one, grad_stack
    )
    up_column = jnp.transpose(up_sum.reshape(-1, sp, each), (1, 0, 2)).reshape(1, -1)
    sums = jnp.concatenate([sums_one, sums_two, up_column], axis=0)
    sums_far = grid.cswap(sums)
    up_both = jnp.concatenate(in_order(sums[n_vec:], sums_far[n_vec:], core), axis=0)
    sums = jnp.concatenate(
        [sums[:n_vec] + sums_far[:n_vec], jnp.where(y == 0, up_both, 0.0), jnp.where(y == 0, 0.0, up_both)], axis=0
    )
    n_sums = n_vec + 4
    qv_sum = jnp.concatenate([stack_sum[0, :local], stack_sum[0, 2 * local :]]).reshape(-1, sp, each)
    n_bias = qv_sum.shape[0] * each
    qv_column = jnp.pad(jnp.transpose(qv_sum, (1, 0, 2)).reshape(sp, n_bias), ((0, 0), (0, part - n_bias)))
    columns = jnp.concatenate([jnp.transpose(sums), qv_column.reshape(-1, 1)], axis=1).astype(BF16)
    columns = jnp.pad(columns, ((0, 0), (0, 128 - columns.shape[1])))
    dw = jnp.concatenate([d_wqkv, columns], axis=1).reshape(nz, nx, 2, part, -1)
    dw_same, dw_other = pick(dw, core, 2), pick(dw, 1 - core, 2)
    from_spin = grid.spin(jnp.where(at_home, dw_other, dw_same), back=True)
    from_cross = grid.cross(dw_other)
    dw = from_spin.astype(F32) + jnp.where(at_home, dw_same, from_cross).astype(F32)
    dw_low = dw.astype(BF16)
    dw = pick(dw, grid.x, 1)
    for j in range(1, nx):
        dw = dw + grid.xshift(pick(dw_low, grid.far_x(j), 1), j).astype(F32)
    dw = lax.all_to_all(dw.astype(BF16), "z", 0, 0, tiled=True)
    g_qkv = place_qkv([dw[k] for k in range(nz)], [jnp.int32(k * local) for k in range(nz)], local)
    tails = dw[:, :, 3 * local :].astype(F32)
    sums = jnp.transpose(jnp.sum(tails[:, :, :n_sums], axis=0))
    up_rows = jnp.where(y == 0, sums[n_vec : n_vec + 2], sums[n_vec + 2 : n_vec + 4])
    g_up_bias = up_rows.reshape(-1, each)
    qv_tail = tails[:, :n_bias, n_sums].reshape(nz, 2, -1, each)
    g_qv_bias = jnp.transpose(qv_tail, (1, 0, 2, 3)).reshape(2, -1, each)

    grad_n1 = part_n1[0]
    for block in n1_far:
        grad_n1 = grad_n1 + block.astype(F32)
    input_grad = grad_middle + norm_back(unit_one[:rows].astype(F32), scale_one[:rows], vecs[2], grad_n1)
    input_grad = input_grad.astype(BF16)
    input_grad = jnp.concatenate(in_order(input_grad, grid.yswap(input_grad), y), axis=0).astype(F32)

    half_o = keep_o + grid.cswap(after(send_o, grad_branch)).astype(F32)
    block_out = half_o[:rows] + grid.yswap(half_o[rows:].astype(BF16)).astype(F32)
    block_out = (middle + (block_out + vecs[7])).astype(BF16)
    block_out = jnp.concatenate(in_order(block_out, grid.yswap(block_out), y), axis=0)
    dp = dot(grad_branch, after(attn_out, got), TN).astype(BF16).reshape(chips, 2, part, -1)
    dp = pick(dp, core, 1).astype(F32) + grid.cswap(pick(dp, 1 - core, 1)).astype(F32)
    dp_keep, dp_send = split(dp, 2, y)
    dp = dp_keep + grid.yswap(dp_send.astype(BF16)).astype(F32)
    d_proj = grid.scatter(dp.astype(BF16).reshape(nz, nx, part, -1))

    keep, send = split(after(d_ff, grad_n1), 0, core)
    low_cols, high_cols = in_order(keep, grid.cswap(send), core)
    n_hidden = grad_hidden.shape[1]
    d_up = jnp.concatenate([low_cols[:, :n_hidden], high_cols[:, :n_hidden]], axis=1).astype(F32)
    d_down = jnp.concatenate([low_cols[:, n_hidden:], high_cols[:, n_hidden:]], axis=1).astype(F32)
    return (
        block_out,
        input_grad,
        g_qkv,
        g_qv_bias,
        jnp.transpose(d_proj),
        sums[4],
        d_up,
        g_up_bias,
        jnp.transpose(d_down),
        sums[7],
        sums[2],
        sums[3],
        sums[5],
        sums[6],
        sums[0],
        sums[1],
    )


def solution(mesh):
    sp = mesh.shape["sp"]
    nz = 4
    devices = mesh.devices.reshape(nz, sp // (2 * nz), 2, mesh.shape["tp"])
    fine = jax.sharding.Mesh(devices, SP + ("tp",))
    line = P(SP)
    placed = (
        P(SP, None),
        line,
        P(),
        P(None, SP, "tp"),
        P(None, "tp", SP),
        P("tp", SP),
        line,
        P(SP, "tp"),
        P("tp", SP),
        P("tp", SP),
    ) + (line,) * 7 + (P(SP, None),)
    given = (
        P(SP, None),
        P(SP, None),
        P(None, SP, "tp"),
        P(None, "tp", SP),
        P("tp", SP),
        line,
        P(SP, "tp"),
        P("tp", SP),
        P("tp", SP),
    ) + (line,) * 7
    return jax.shard_map(per_device, mesh=fine, in_specs=placed, out_specs=given, check_vma=False)
```

```python
import functools

import jax
import jax.numpy as jnp
from jax import lax
from jax.experimental import pallas as pl
from jax.experimental.pallas import tpu as pltpu
from jax.sharding import PartitionSpec as P

HD = 64
EPSILON = 1e-05
EXCLUDED = -1e30
F32 = jnp.float32
BF16 = jnp.bfloat16
NN = (((1,), (0,)), ((), ()))
NT = (((1,), (1,)), ((), ()))
TN = (((0,), (0,)), ((), ()))


def dot(left, right, dims=NN):
    return lax.dot_general(left, right, dims, preferred_element_type=F32)


SP = ("z", "x", "core")


class Grid:
    def __init__(self):
        self.nz = lax.axis_size("z")
        self.nx = lax.axis_size("x")
        self.chips = self.nz * self.nx
        self.sp = 2 * self.chips
        me = lax.axis_index(SP)
        self.me = me
        self.core = me % 2
        self.x = (me // 2) % self.nx
        self.z = me // (2 * self.nx)
        self.y = lax.axis_index("tp")

    def _move(self, block, dz, dx, flip):
        pairs = []
        for i in range(self.sp):
            z, x, c = i // (2 * self.nx), (i // 2) % self.nx, i % 2
            to = (((z + dz) % self.nz) * self.nx + (x + dx) % self.nx) * 2 + (1 - c if flip else c)
            pairs.append((i, to))
        return lax.ppermute(block, SP, pairs)

    def zshift(self, block, k):
        return self._move(block, k, 0, False)

    def xshift(self, block, k):
        return self._move(block, 0, k, False)

    def cswap(self, block):
        return self._move(block, 0, 0, True)

    def yswap(self, block):
        return lax.ppermute(block, "tp", [(0, 1), (1, 0)])

    def _pairs(self, route):
        pairs = []
        for chip in range(self.chips):
            for (c, y), (to_c, to_y) in route:
                pairs.append(((chip * 2 + c) * 2 + y, (chip * 2 + to_c) * 2 + to_y))
        return pairs

    def spin(self, block, back=False):
        route = []
        for b in (0, 1):
            route += [((b, b), (b, 1 - b)), ((1 - b, b), (b, b))]
        if back:
            route = [(to, at) for at, to in route]
        return lax.ppermute(block, SP + ("tp",), self._pairs(route))

    def cross(self, block):
        route = [((1 - b, b), (b, 1 - b)) for b in (0, 1)]
        return lax.ppermute(block, SP + ("tp",), self._pairs(route))

    def far_z(self, k):
        return (self.z + k) % self.nz

    def far_x(self, j):
        return (self.x + j) % self.nx

    def gather(self, block):
        columns = [block] + [self.zshift(block, k) for k in range(1, self.nz)]
        return [p for b in columns for p in [b] + [self.xshift(b, j) for j in range(1, self.nx)]]

    def chip_order(self):
        order = jnp.arange(self.chips)
        return self.far_z(-(order // self.nx)) * self.nx + self.far_x(-(order % self.nx))

    def scatter(self, pieces):
        total = pick(pieces, self.x, 1).astype(F32)
        for j in range(1, self.nx):
            total = total + self.xshift(pick(pieces, self.far_x(j), 1), j).astype(F32)
        low = total.astype(pieces.dtype)
        mine = pick(total, self.z, 0)
        for k in range(1, self.nz):
            mine = mine + self.zshift(pick(low, self.far_z(k), 0), k).astype(F32)
        return mine


def pick(array, index, axis):
    return lax.dynamic_index_in_dim(array, index, axis, keepdims=False)


def normalize(values):
    center = values - jnp.mean(values, axis=-1, keepdims=True)
    spread = jnp.mean(center * center, axis=-1, keepdims=True)
    scale = lax.rsqrt(spread + EPSILON)
    return center * scale, scale


def norm_back(normed, scale, gain, grad):
    scaled = grad * gain
    mean_one = jnp.mean(scaled, axis=-1, keepdims=True)
    mean_two = jnp.mean(scaled * normed, axis=-1, keepdims=True)
    return (scaled - mean_one - normed * mean_two) * scale


def place_qkv_kernel(starts_ref, *refs):
    pieces, out_ref = refs[:-1], refs[-1]
    for i, piece in enumerate(pieces):
        size = out_ref.shape[2] // len(pieces)
        span = pl.ds(pl.multiple_of(starts_ref[i], size), size)
        for c in range(3):
            out_ref[c, :, span] = piece[:, c * size : (c + 1) * size].astype(F32)


def place_qkv(pieces, starts, columns):
    rows = pieces[0].shape[0]
    vmem = pl.BlockSpec(memory_space=pltpu.VMEM)
    return pl.pallas_call(
        place_qkv_kernel,
        out_shape=jax.ShapeDtypeStruct((3, rows, columns * len(pieces)), F32),
        in_specs=[pl.BlockSpec(memory_space=pltpu.SMEM)] + [vmem] * len(pieces),
        out_specs=vmem,
        name="place_qkv",
    )(jnp.stack(starts).astype(jnp.int32), *pieces)


def lane_in_head(shape, head):
    lanes = lax.broadcasted_iota(jnp.int32, shape, 1)
    return (lanes // HD) == (head % 2)


def pair_lanes(pair):
    return slice(pair * 2 * HD, (pair + 1) * 2 * HD)


STEP = 384
SMEM = pl.BlockSpec(memory_space=pltpu.SMEM)


def in_vmem(count):
    return [pl.BlockSpec(memory_space=pltpu.VMEM)] * count


COSTS = {"enter": 5, "attend": 14, "attend_back": 17, "whole_proj": 1, "project": 2, "branch": 2, "leave": 3, "close": 5, "outer": 5}


def local_kernel(kernel, name, out_shape, operands, scalars=1, scratch=(), flops=0, megabytes=48, before=()):
    if before:
        inner, at_end = kernel, len(operands)

        def kernel(*refs):
            inner(*refs[:at_end], *refs[at_end + len(before) :])

    single = not isinstance(out_shape, tuple)
    return pl.pallas_call(
        kernel,
        out_shape=out_shape,
        in_specs=[SMEM] * scalars + in_vmem(len(operands) - scalars) + [ANY] * len(before),
        out_specs=in_vmem(1)[0] if single else tuple(in_vmem(len(out_shape))),
        scratch_shapes=list(scratch),
        compiler_params=pltpu.CompilerParams(vmem_limit_bytes=megabytes * 1024 * 1024),
        cost_estimate=pl.CostEstimate(flops=COSTS.get(name, 0) * 1000000000, bytes_accessed=1 << 16, transcendentals=0),
        name=name,
    )(*operands, *before)


def turn_kernel(in_ref, out_ref):
    out_ref[...] = jnp.transpose(in_ref[...])


def turn(block, *before):
    return local_kernel(turn_kernel, "turn", shape(block.shape[::-1]), (block,), scalars=0, before=before)


def shape(dims, kind=BF16):
    return jax.ShapeDtypeStruct(tuple(dims), kind)


ANY = pl.BlockSpec(memory_space=pl.ANY)


def gate(block, *before):
    return pl.pallas_call(
        lambda *refs: None,
        out_shape=jax.ShapeDtypeStruct(block.shape, block.dtype),
        in_specs=[ANY] * (1 + len(before)),
        out_specs=ANY,
        input_output_aliases={0: 0},
        cost_estimate=pl.CostEstimate(flops=0, bytes_accessed=0, transcendentals=0),
        name="gate",
    )(block, *before)


def stack_kernel(count, *refs):
    for n in range(count):
        refs[-1][n] = refs[n][...]


def stack(blocks, *before):
    first = blocks[0]
    return pl.pallas_call(
        functools.partial(stack_kernel, len(blocks)),
        out_shape=jax.ShapeDtypeStruct((len(blocks),) + first.shape, first.dtype),
        in_specs=in_vmem(len(blocks)) + [ANY] * len(before),
        out_specs=in_vmem(1)[0],
        cost_estimate=pl.CostEstimate(flops=0, bytes_accessed=1 << 16, transcendentals=0),
        name="stack",
    )(*blocks, *before)


def turned(index, size):
    return lax.rem(index + size, size)


def enter_kernel(nz, nx, n_vec, part, at_ref, hour_ref, *refs):
    token_refs, refs = refs[: nz + 1], refs[nz + 1 :]
    pack_refs, refs = refs[: nx - 1], refs[nx - 1 :]
    weight_refs, refs = refs[:2], refs[2:]
    normed_ref, unit_ref, scale_ref, lead_ref, first_ref, vec_ref, weight_ref, q_ref, kv_ref = refs[:9]
    packs = refs[9]
    z, x, c = at_ref[0], at_ref[1], at_ref[2]
    rows, width = first_ref.shape
    tall = packs.shape[3]
    local = q_ref.shape[1]
    aux = slice(width, width + 128)
    for k in range(nz):
        packs[0, 0, k] = token_refs[k][:tall, aux]
        packs[0, 1, k] = token_refs[nz][k, :tall, aux]
    for j in range(1, nx):
        packs[j] = pack_refs[j - 1][...]
    for dev in range(2 * nz * nx):
        dev_z, dev_x, dev_c = dev // (2 * nx), (dev // 2) % nx, dev % 2
        block = packs[turned(x - dev_x, nx), turned(c - dev_c, 2), turned(z - dev_z, nz)]
        vec_ref[:, dev * part : (dev + 1) * part] = block[:n_vec, 64 : 64 + part].astype(F32)
    for n in range(2 * nz):
        ref = token_refs[n] if n < nz else token_refs[nz].at[n - nz]
        span = slice(n * rows, (n + 1) * rows)
        segment = ref[:, aux][:, :1].astype(F32)
        lead = jnp.zeros_like(segment)
        for i in range(hour_ref.shape[0]):
            lead = jnp.where(segment == float(i), hour_ref[i], lead)
        lead_ref[span, :] = lead
        value = ref[:, :width].astype(F32) + lead * vec_ref[0:1, :] + vec_ref[1:2, :]
        if n == 0:
            first_ref[...] = value
        unit, scale = normalize(value)
        scale_ref[span, :] = scale
        unit_ref[span, :] = unit.astype(BF16)
        normed_ref[span, :] = (unit * vec_ref[2:3, :] + vec_ref[3:4, :]).astype(BF16)
    for p, ref in enumerate(weight_refs):
        parity = c if p == 0 else 1 - c
        for j in range(nx):
            for k in range(nz):
                row = ((turned(z - k, nz) * nx + turned(x - j, nx)) * 2 + parity) * part
                weight_ref[pl.ds(pl.multiple_of(row, part), part), :] = ref[j, k]
    made = dot(normed_ref[...], weight_ref[...])
    q_ref[...] = made[:, :local]
    kv_ref[...] = made[:, local:].astype(BF16)


def enter(at, hours, tokens, packs, same, other, n_vec, part):
    nz, nx = len(tokens) - 1, len(packs) + 1
    rows, wide = tokens[0].shape
    width = wide - 128
    count = 2 * nz * rows
    local = same.shape[-1] // 3
    tall = packs[0].shape[2]
    return local_kernel(
        functools.partial(enter_kernel, nz, nx, n_vec, part),
        "enter",
        (
            shape((count, width)),
            shape((count, width)),
            shape((count, 1), F32),
            shape((count, 1), F32),
            shape((rows, width), F32),
            shape((n_vec, width), F32),
            shape((width, 3 * local)),
            shape((count, local), F32),
            shape((count, 2 * local)),
        ),
        (at, hours, *tokens, *packs, same, other),
        scalars=2,
        scratch=[pltpu.VMEM((nx, 2, nz, tall, 128), BF16)],
    )


def attend_kernel(pieces, heads, nz, at_ref, q_ref, bias_ref, qcode_ref, kcode_ref, *refs):
    kv_refs = refs[:pieces]
    out_ref, lse_ref, low_ref, send_ref = refs[pieces : pieces + 4]
    kaug, vturn, qaug, acc, stat = refs[pieces + 4 :]
    width = heads * HD
    count = q_ref.shape[0]
    rows = count // (2 * nz)
    steps = kv_refs[0].shape[0] // STEP
    low_ref[...] = (q_ref[...] + bias_ref[0:1, :]).astype(BF16) * jnp.asarray(HD ** (-0.5), BF16)
    for n in range(pieces * steps):
        block = kv_refs[n // steps]
        span_in = pl.ds((n % steps) * STEP, STEP)
        span = pl.ds(n * STEP, STEP)
        code = kcode_ref[span, :]
        for p in range(heads // 2):
            keys = block[span_in, pair_lanes(p)]
            for h in (2 * p, 2 * p + 1):
                kaug[h, span, :] = jnp.where(lane_in_head(keys.shape, h), keys, code)
        vturn[n] = jnp.transpose(block[span_in, width:])
    for p in range(heads // 2):
        part = low_ref[:, pair_lanes(p)]
        for h in (2 * p, 2 * p + 1):
            qaug[h] = jnp.where(lane_in_head(part.shape, h), part, qcode_ref[...])
    acc[...] = jnp.zeros_like(acc)
    stat[0] = jnp.full(stat.shape[1:], EXCLUDED, F32)
    stat[1] = jnp.zeros(stat.shape[1:], F32)

    def chunk(i, carry):
        for h in range(heads):
            scores = dot(kaug[h, pl.ds(i * STEP, STEP), :], qaug[h], NT)
            top = stat[0, h : h + 1, :]
            new_top = jnp.maximum(top, jnp.max(scores, axis=0, keepdims=True))
            weight = jnp.exp(scores - new_top)
            rescale = jnp.exp(top - new_top)
            stat[0, h : h + 1, :] = new_top
            stat[1, h : h + 1, :] = stat[1, h : h + 1, :] * rescale + jnp.sum(weight, axis=0, keepdims=True)
            span = slice(h * HD, (h + 1) * HD)
            acc[span, :] = acc[span, :] * rescale + dot(vturn[i, span, :], weight.astype(BF16))
        return carry

    lax.fori_loop(0, pieces * steps, chunk, 0)
    for h in range(heads):
        span = slice(h * HD, (h + 1) * HD)
        acc[span, :] = acc[span, :] / stat[1, h : h + 1, :]
    out_ref[...] = jnp.transpose(acc[...])
    lse_ref[...] = stat[0] + jnp.log(jnp.maximum(stat[1], 1e-37))
    z = at_ref[0]
    for r in range(2):
        for k in range(nz):
            span = slice((r * nz + k) * rows, (r * nz + k + 1) * rows)
            send_ref[turned(z - k, nz), r] = (out_ref[span, :] + bias_ref[1:2, :]).astype(BF16)


def attend(at, nz, q, bias, qcode, kcode, kv_pieces):
    count, width = q.shape
    heads = width // HD
    keys = kcode.shape[0]
    return local_kernel(
        functools.partial(attend_kernel, len(kv_pieces), heads, nz),
        "attend",
        (
            shape((count, width), F32),
            shape((8, count), F32),
            shape((count, width)),
            shape((nz, 2, count // (2 * nz), width)),
        ),
        (at, q, bias, qcode, kcode, *kv_pieces),
        scratch=[
            pltpu.VMEM((heads, keys, 2 * HD), BF16),
            pltpu.VMEM((keys // STEP, width, STEP), BF16),
            pltpu.VMEM((heads, count, 2 * HD), BF16),
            pltpu.VMEM((width, count), F32),
            pltpu.VMEM((2, 8, count), F32),
        ],
    )


def attend_back_kernel(
    nx, heads, nz, at_ref, q_ref, qcode_ref, kcode_ref, got_ref, full_ref, lse_ref, *refs
):
    pieces = 2 * nx
    kv_refs = refs[:pieces]
    dq_ref, dkv_refs = refs[pieces], refs[pieces + 1 : pieces + 1 + nx]
    kaug, kturn, vals, qaug, qmask, domask, acc, dout, delta = refs[pieces + 1 + nx :]
    width = heads * HD
    count = q_ref.shape[0]
    rows = count // (2 * nz)
    steps = kv_refs[0].shape[0] // STEP
    z = at_ref[0]
    for r in range(2):
        for k in range(nz):
            span = slice((r * nz + k) * rows, (r * nz + k + 1) * rows)
            dout[span, :] = got_ref[turned(z - k, nz), r]
    product = dout[...].astype(F32) * full_ref[...]
    head_rows = lax.broadcasted_iota(jnp.int32, (8, width), 0)
    head_lanes = lax.broadcasted_iota(jnp.int32, (8, width), 1) // HD
    delta[...] = lax.dot_general(
        (head_rows == head_lanes).astype(F32),
        product,
        NT,
        precision=lax.Precision.HIGHEST,
        preferred_element_type=F32,
    )
    for n in range(pieces * steps):
        block = kv_refs[n // steps]
        span_in = pl.ds((n % steps) * STEP, STEP)
        span = pl.ds(n * STEP, STEP)
        code = kcode_ref[span, :]
        for p in range(heads // 2):
            keys = block[span_in, pair_lanes(p)]
            for h in (2 * p, 2 * p + 1):
                kaug[h, span, :] = jnp.where(lane_in_head(keys.shape, h), keys, code)
        kturn[n] = jnp.transpose(block[span_in, :width])
        vals[span, :] = block[span_in, width:]
    for p in range(heads // 2):
        part = q_ref[:, pair_lanes(p)]
        dpart = dout[:, pair_lanes(p)]
        for h in (2 * p, 2 * p + 1):
            inside = lane_in_head(part.shape, h)
            qaug[h] = jnp.where(inside, part, qcode_ref[...])
            qmask[h] = jnp.where(inside, part, jnp.zeros_like(part))
            domask[h] = jnp.where(inside, dpart, jnp.zeros_like(dpart))
    acc[...] = jnp.zeros_like(acc)
    each = 2 * steps
    for j in range(nx):

        def chunk(n, carry, j=j):
            i = j * each + n
            span = pl.ds(i * STEP, STEP)
            span_out = pl.ds(n * STEP, STEP)
            for p in range(heads // 2):
                dkey = dval = None
                for h in (2 * p, 2 * p + 1):
                    scores = dot(kaug[h, span, :], qaug[h], NT)
                    prob = jnp.exp(scores - lse_ref[h : h + 1, :])
                    dprob = dot(vals[span, pair_lanes(p)], domask[h], NT)
                    dscore = (prob * (dprob - delta[h : h + 1, :])).astype(BF16)
                    add_val = dot(prob.astype(BF16), domask[h])
                    add_key = dot(dscore, qmask[h])
                    dval = add_val if dval is None else dval + add_val
                    dkey = add_key if dkey is None else dkey + add_key
                    turn = slice(h * HD, (h + 1) * HD)
                    acc[turn, :] += dot(kturn[i, turn, :], dscore)
                dkv_refs[j][span_out, pair_lanes(p)] = dkey.astype(BF16)
                dkv_refs[j][span_out, slice(width + p * 2 * HD, width + (p + 1) * 2 * HD)] = dval.astype(BF16)
            return carry

        lax.fori_loop(0, each, chunk, 0)
    dq_ref[...] = (jnp.transpose(acc[...]) * (HD ** (-0.5))).astype(BF16)


def attend_back(at, nz, q, qcode, kcode, got, full, lse, kv_pieces):
    count, width = q.shape
    heads = width // HD
    keys = kcode.shape[0]
    nx = len(kv_pieces) // 2
    return local_kernel(
        functools.partial(attend_back_kernel, nx, heads, nz),
        "attend_back",
        (shape((count, width)),) + (shape((2 * count, 2 * width)),) * nx,
        (at, q, qcode, kcode, got, full, lse, *kv_pieces),
        scratch=[
            pltpu.VMEM((heads, keys, 2 * HD), BF16),
            pltpu.VMEM((keys // STEP, width, STEP), BF16),
            pltpu.VMEM((keys, width), BF16),
            pltpu.VMEM((heads, count, 2 * HD), BF16),
            pltpu.VMEM((heads, count, 2 * HD), BF16),
            pltpu.VMEM((heads, count, 2 * HD), BF16),
            pltpu.VMEM((width, count), F32),
            pltpu.VMEM((count, width), BF16),
            pltpu.VMEM((8, count), F32),
        ],
        megabytes=56,
    )


def whole_proj_kernel(nz, nx, part, at_ref, own_ref, far_ref, out_ref):
    z, x, c, y = at_ref[0], at_ref[1], at_ref[2], at_ref[3]
    half = out_ref.shape[1] // 2
    for p, ref in enumerate((own_ref, far_ref)):
        parity = c if p == 0 else 1 - c
        for w in range(2):
            column = pl.multiple_of(turned(y - w, 2) * half, half)
            for j in range(nx):
                for k in range(nz):
                    row = ((turned(z - k, nz) * nx + turned(x - j, nx)) * 2 + parity) * part
                    out_ref[pl.ds(pl.multiple_of(row, part), part), pl.ds(column, half)] = ref[w, j, k]


def whole_proj(at, own, far):
    _, nx, nz, part, half = own.shape
    return local_kernel(
        functools.partial(whole_proj_kernel, nz, nx, part),
        "whole_proj",
        shape((2 * nx * nz * part, 2 * half)),
        (at, own, far),
    )


def project_kernel(at_ref, got_ref, far_ref, weight_ref, first_ref, vec_ref, *refs):
    attn_ref, unit_ref, scale_ref, normed_ref, middle_ref = refs
    nz, _, _, local = got_ref.shape
    c = at_ref[2]
    for block in range(2):
        base = (c if block == 0 else 1 - c) * nz
        for z in range(nz):
            lane = pl.multiple_of((base + z) * local, local)
            attn_ref[:, pl.ds(lane, local)] = got_ref[z, 0] if block == 0 else far_ref[z]
    middle = first_ref[...] + (dot(attn_ref[...], weight_ref[...], NT) + vec_ref[4:5, :])
    middle_ref[...] = middle
    unit, scale = normalize(middle)
    unit_ref[...] = unit
    scale_ref[...] = scale
    normed_ref[...] = (unit * vec_ref[5:6, :] + vec_ref[6:7, :]).astype(BF16)


def project(at, got, far, weight, first, vecs):
    rows, width = first.shape
    return local_kernel(
        project_kernel,
        "project",
        (
            shape((rows, width)),
            shape((rows, width), F32),
            shape((rows, 1), F32),
            shape((rows, width)),
            shape((rows, width), F32),
        ),
        (at, got, far, weight, first, vecs),
    )


def feed_kernel(bias_ref, own_ref, near_ref, far_ref, gz_ref, weight, *refs):
    normed_ref, act_ref, gh_ref, sum_ref, keep_n_ref, send_n_ref, keep_o_ref, send_o_ref = refs[:8]
    back, out = refs[8:]
    rows = own_ref.shape[0]
    hidden_size = act_ref.shape[1]
    normed_ref[:rows, :] = own_ref[...]
    normed_ref[rows : 2 * rows, :] = near_ref[...]
    normed_ref[2 * rows :, :] = far_ref[...]
    step = 256
    for n in range(hidden_size // step):
        up = slice(n * step, (n + 1) * step)
        down = slice(hidden_size + n * step, hidden_size + (n + 1) * step)
        value = dot(normed_ref[...], weight[:, up]) + bias_ref[:, up]
        cdf = 0.5 * (1.0 + lax.erf(value * (0.5**0.5)))
        act = (value * cdf).astype(BF16)
        slope = cdf + value * (jnp.exp(-0.5 * value * value) * ((0.5 / jnp.pi) ** 0.5))
        low = (dot(gz_ref[...], weight[:, down]) * slope).astype(BF16)
        act_ref[:, up] = act
        gh_ref[:, up] = low
        sum_ref[:, up] = jnp.sum(low.astype(F32), axis=0, keepdims=True)
        add_back = dot(low, weight[:, up], NT)
        add_out = dot(act, weight[:, down], NT)
        if n == 0:
            back[...] = add_back
            out[...] = add_out
        else:
            back[...] += add_back
            out[...] += add_out
    keep_n_ref[...] = back[: 2 * rows, :]
    send_n_ref[...] = back[2 * rows :, :].astype(BF16)
    keep_o_ref[...] = out[: 2 * rows, :]
    send_o_ref[...] = out[2 * rows :, :].astype(BF16)


def feed(bias, own, near, far, gz, weight):
    count, width = gz.shape
    hidden_size = bias.shape[1]
    half = count // 2
    return local_kernel(
        feed_kernel,
        "feed",
        (
            shape((count, width)),
            shape((count, hidden_size)),
            shape((count, hidden_size)),
            shape((1, hidden_size), F32),
            shape((half, width), F32),
            shape((half, width)),
            shape((half, width), F32),
            shape((half, width)),
        ),
        (bias, own, near, far, gz, weight),
        scalars=0,
        scratch=[pltpu.VMEM((count, width), F32), pltpu.VMEM((count, width), F32)],
        megabytes=56,
    )


def outer_kernel(normed_ref, gh_ref, gz_ref, act_ref, out_ref):
    hidden_size = gh_ref.shape[1]
    step = 256
    for base, left_ref, right_ref in ((0, normed_ref, gh_ref), (hidden_size, gz_ref, act_ref)):
        for n in range(hidden_size // step):
            made = dot(left_ref[...], right_ref[:, n * step : (n + 1) * step], TN)
            out_ref[:, base + n * step : base + (n + 1) * step] = made.astype(BF16)


def outer(normed, gh, gz, act):
    return local_kernel(
        outer_kernel, "outer", shape((normed.shape[1], 2 * gh.shape[1])), (normed, gh, gz, act), scalars=0
    )


def branch_kernel(at_ref, half_ref, near_ref, unit_ref, scale_ref, vec_ref, gz_ref, weight_ref, *refs):
    middle_ref, branch_ref, mine_ref, send_ref, sum_ref = refs
    rows = half_ref.shape[0] // 2
    nz, _, local = mine_ref.shape
    c = at_ref[2]
    grad = half_ref[:rows, :] + near_ref[...].astype(F32)
    top = gz_ref[...].astype(F32)
    unit = unit_ref[...]
    middle = top + norm_back(unit, scale_ref[...], vec_ref[5:6, :], grad)
    middle_ref[...] = middle
    low = middle.astype(BF16)
    branch_ref[...] = low
    made = dot(low, weight_ref[...]).astype(BF16)
    for h in range(2):
        for z in range(nz):
            block = made[:, (h * nz + z) * local : (h * nz + z + 1) * local]

            @pl.when(c == h)
            def _():
                mine_ref[z] = block

            @pl.when(c != h)
            def _():
                send_ref[z] = block

    sum_ref[...] = jnp.concatenate(
        [
            jnp.sum(low.astype(F32), axis=0, keepdims=True),
            jnp.sum(grad * unit, axis=0, keepdims=True),
            jnp.sum(grad, axis=0, keepdims=True),
            jnp.sum(top, axis=0, keepdims=True),
        ],
        axis=0,
    )


def branch(at, nz, half, near, unit, scale, vecs, gz, weight, before):
    rows, width = unit.shape
    local = width // (2 * nz)
    return local_kernel(
        branch_kernel,
        "branch",
        (
            shape((rows, width), F32),
            shape((rows, width)),
            shape((nz, rows, local)),
            shape((nz, rows, local)),
            shape((4, width), F32),
        ),
        (at, half, near, unit, scale, vecs, gz, weight),
        before=before,
    )


def leave_kernel(dq_ref, two_ref, near_ref, weight_ref, stack_ref, full_ref, send_ref):
    count, local = dq_ref.shape
    stack_ref[:, :local] = dq_ref[...]
    stack_ref[:, local:] = (two_ref[:count, :] + near_ref[...].astype(F32)).astype(BF16)
    full_ref[...] = dot(stack_ref[...], weight_ref[...], NT)
    send_ref[...] = full_ref[count // 2 :, :].astype(BF16)


def leave(dq, two, near, weight):
    count, local = dq.shape
    width = weight.shape[0]
    return local_kernel(
        leave_kernel,
        "leave",
        (shape((count, 3 * local)), shape((count, width), F32), shape((count // 2, width))),
        (dq, two, near, weight),
        scalars=0,
    )


def close_kernel(rows, full_ref, unit_ref, scale_ref, lead_ref, vec_ref, middle_ref, normed_ref, stack_ref, *refs):
    sum_ref, bias_ref, out_ref = refs
    count, width = full_ref.shape
    lead_row = jnp.zeros((4, width), F32)
    for n in range(count // rows):
        span = slice(n * rows, (n + 1) * rows)
        grad = full_ref[span, :]
        unit = unit_ref[span, :].astype(F32)
        back = norm_back(unit, scale_ref[span, :], vec_ref[2:3, :], grad)
        if n == 0:
            back = back + middle_ref[...]
        lead_row = lead_row + jnp.concatenate(
            [
                jnp.sum(back * lead_ref[span, :], axis=0, keepdims=True),
                jnp.sum(back, axis=0, keepdims=True),
                jnp.sum(grad * unit, axis=0, keepdims=True),
                jnp.sum(grad, axis=0, keepdims=True),
            ],
            axis=0,
        )
    sum_ref[...] = lead_row
    bias_ref[...] = jnp.sum(stack_ref[...].astype(F32), axis=0, keepdims=True)
    out_ref[...] = dot(normed_ref[...], stack_ref[...], TN).astype(BF16)


def close(rows, full, unit, scale, lead, vecs, middle, normed, stack, before):
    width = full.shape[1]
    return local_kernel(
        functools.partial(close_kernel, rows),
        "close",
        (shape((4, width), F32), shape((1, stack.shape[1]), F32), shape((width, stack.shape[1]))),
        (full, unit, scale, lead, vecs, middle, normed, stack),
        scalars=0,
        before=before,
    )


def after(block, *before):
    return lax.optimization_barrier((block,) + before)[0]


def per_device(
    tokens,
    segment_ids,
    lead_hours,
    qkv_weight,
    qv_bias,
    proj_weight,
    proj_bias,
    up_weight,
    up_bias,
    down_weight,
    down_bias,
    norm1_gain,
    norm1_bias,
    norm2_gain,
    norm2_bias,
    lead_weight,
    lead_bias,
    out_grad,
):
    grid = Grid()
    nz, nx, chips, sp = grid.nz, grid.nx, grid.chips, grid.sp
    core, y = grid.core, grid.y
    at = jnp.stack([grid.z, grid.x, core, y]).astype(jnp.int32)
    full_rows, width = tokens.shape
    rows = full_rows // 2
    part = norm1_gain.shape[0]
    each = HD // sp
    at_home = core == y

    def split(array, axis, index):
        half = array.shape[axis] // 2
        first = lax.slice_in_dim(array, 0, half, axis=axis)
        second = lax.slice_in_dim(array, half, 2 * half, axis=axis)
        return jnp.where(index == 0, first, second), jnp.where(index == 0, second, first)

    def in_order(own, other, index):
        return jnp.where(index == 0, own, other), jnp.where(index == 0, other, own)

    shard = jnp.transpose(qkv_weight.reshape(3, part, nz, -1), (2, 1, 0, 3)).reshape(nz, part, -1)
    wq_z = [pick(shard, grid.z, 0)] + [grid.zshift(pick(shard, grid.far_z(k), 0), k) for k in range(1, nz)]

    vectors = [lead_weight, lead_bias, norm1_gain, norm1_bias, proj_bias, norm2_gain, norm2_bias, down_bias]
    n_vec = len(vectors)
    n_qv, n_up = qv_bias.size // part, up_bias.size // part
    pack = jnp.concatenate(
        [
            jnp.stack(vectors),
            qv_bias.reshape(-1, part),
            up_bias.reshape(-1, part),
            segment_ids.astype(BF16).reshape(-1, part),
        ],
        axis=0,
    )
    pack_rows = pack.shape[0]
    tall = -(-pack_rows // 16) * 16
    pack = jnp.pad(pack, ((0, rows - pack_rows), (63, 128 - 64 - part)))
    own_segments = split(segment_ids, 0, y)[0]
    beside = jnp.concatenate([own_segments.astype(BF16)[:, None], pack], axis=1)
    own_tokens = jnp.concatenate([split(tokens, 0, y)[0], beside], axis=1)
    token_far = [grid.zshift(own_tokens, k) for k in range(1, nz)]
    token_z = jnp.stack([own_tokens] + token_far)
    token_c = grid.cswap(token_z)
    packs_own = jnp.stack([token_z[:, :tall, width:], token_c[:, :tall, width:]])
    packs_far = [grid.xshift(packs_own, j) for j in range(1, nx)]

    wq_z = jnp.stack(wq_z)
    wq_x = jnp.stack([wq_z] + [grid.xshift(wq_z, j) for j in range(1, nx)])
    wq_spin, wq_cross = grid.spin(wq_x), grid.cross(wq_x)
    wq_same = jnp.where(at_home, wq_x, wq_spin)
    wq_other = jnp.where(at_home, wq_spin, wq_cross)

    normed_one, unit_one, scale_one, lead, embedded, vecs, w_qkv, q_raw, kv = enter(
        at, lead_hours, [own_tokens] + token_far + [token_c], packs_far, wq_same, wq_other, n_vec, part
    )
    local = q_raw.shape[1]
    kv_far = grid.yswap(kv)
    kv_pieces = [kv, kv_far]
    for j in range(1, nx):
        kv_pieces += [grid.xshift(kv, j), grid.xshift(kv_far, j)]

    table = jnp.stack([packs_own] + packs_far)[:, :, :, n_vec:pack_rows, 64 : 64 + part].reshape(sp, -1)
    n = jnp.arange(sp)
    rel_j, rel_r, rel_k = n // (2 * nz), (n // nz) % 2, n % nz
    device = (grid.far_z(-rel_k) * nx + grid.far_x(-rel_j)) * 2 + (core + rel_r) % 2
    in_place = (jnp.arange(sp)[:, None] == device[None, :]).astype(BF16)
    table = dot(in_place, table).reshape(sp, -1, part)
    heads_local = qv_bias.shape[1]
    qv_all = jnp.transpose(table[:, :n_qv].reshape(sp, 2, heads_local, -1), (1, 2, 0, 3)).reshape(2, heads_local * HD)
    qv_far = grid.yswap(qv_all)
    qv_full = pick(jnp.where(at_home, qv_all, qv_far).reshape(2, nz, -1), grid.z, 1)
    seg_rows = table[:, n_qv + n_up :].reshape(sp * 2, rows)
    n = jnp.arange(nx * 2 * 2 * nz)
    k, r, w, j = n % nz, (n // nz) % 2, (n // (2 * nz)) % 2, n // (4 * nz)
    key_at = ((grid.far_z(-k) * nx + grid.far_x(-j)) * 2 + (core + r) % 2) * 2 + (y + w) % 2
    take = (key_at[:, None] == jnp.arange(2 * sp)[None, :]).astype(BF16)
    key_seg = dot(take, seg_rows.astype(BF16)).astype(jnp.int32).reshape(-1)
    query_seg = key_seg[: 2 * nz * rows]
    lanes = jnp.arange(2 * HD, dtype=jnp.int32) % HD
    kcode = jnp.where(key_seg[:, None] == lanes[None, :], 0.0, EXCLUDED).astype(BF16)
    qcode = (query_seg[:, None] == lanes[None, :]).astype(BF16)
    up_all = jnp.transpose(table[:, n_qv : n_qv + n_up].reshape(sp, up_bias.shape[0], -1), (1, 0, 2)).reshape(1, -1)
    up_full = split(up_all, 1, core)[0]

    up_shard, down_shard, _ = lax.optimization_barrier((up_weight, down_weight, wq_z))
    up_keep, up_send = split(up_shard, 1, core)
    down_keep, down_send = split(jnp.transpose(down_shard), 1, core)
    ff_far = grid.cswap(jnp.concatenate([up_send, down_send], axis=1))
    ff = jnp.concatenate(in_order(jnp.concatenate([up_keep, down_keep], axis=1), ff_far, core), axis=0)
    w_ff = lax.all_gather(after(ff, *token_far), ("z", "x"), axis=0, tiled=True)

    gz_own, gz_far = split(after(out_grad, kv), 0, y)
    gz_two = jnp.concatenate([gz_own, gz_far], axis=0)
    gz = jnp.concatenate([gz_two, grid.cswap(gz_two)], axis=0)

    wp = jnp.transpose(after(proj_weight, wq_spin, token_c))
    wp_z = jnp.stack([wp] + [grid.zshift(wp, k) for k in range(1, nz)])
    wp_z = after(wp_z, kv)
    wp_x = jnp.stack([wp_z] + [grid.xshift(wp_z, j) for j in range(1, nx)])
    wp_x = after(wp_x, kv_far)
    wp_own = jnp.stack([wp_x, grid.yswap(wp_x)])
    w_proj = whole_proj(at, wp_own, grid.cswap(wp_own))

    q_raw, up_full, gz = lax.optimization_barrier((q_raw, up_full, gz))
    attn_full, lse, q, attn_send = attend(at, nz, q_raw, qv_full, qcode, kcode, kv_pieces)
    attn_got = lax.all_to_all(attn_send, "z", 0, 0, tiled=True)
    attn_far = grid.cswap(attn_got[:, 1])
    attn_out, n2, s2, normed, middle = project(at, attn_got, attn_far, w_proj, embedded, vecs)
    near = grid.yswap(normed)
    far = grid.cswap(jnp.concatenate([normed, near], axis=0))
    normed_two, active, grad_hidden, up_sum, keep_n, send_n, keep_o, send_o = feed(up_full, normed, near, far, gz, w_ff)

    half_n = keep_n + grid.cswap(send_n).astype(F32)
    near_n = grid.yswap(half_n[rows:].astype(BF16))
    d_outer = outer(normed_two, grad_hidden, gz, active)
    d_ff = lax.psum_scatter(d_outer, ("z", "x"), scatter_dimension=0, tiled=True)
    grad_middle, grad_branch, mine, send, sums_two = branch(
        at, nz, half_n, near_n, n2, s2, vecs, gz[:rows], w_proj, (d_outer,)
    )
    theirs = grid.cswap(send)
    got = lax.all_to_all(jnp.stack([mine, theirs], axis=1), "z", 0, 0, tiled=True)

    back = attend_back(at, nz, q, qcode, kcode, got, attn_full, lse, kv_pieces)
    grad_q, grad_kv = back[0], back[1].astype(F32)
    for j in range(1, nx):
        grad_kv = grad_kv + grid.xshift(back[1 + j], -j).astype(F32)
    count = 2 * nz * rows
    near_kv = grid.yswap(grad_kv[count:].astype(BF16))
    grad_stack, part_full, part_send = leave(grad_q, grad_kv, near_kv, w_qkv)

    part_n1 = (part_full[: nz * rows] + grid.cswap(part_send).astype(F32)).reshape(nz, rows, width)
    low = part_n1.astype(BF16)
    n1_far = [grid.zshift(low[k], -k) for k in range(1, nz)]

    sums_one, stack_sum, d_wqkv = close(
        rows, part_full, unit_one, scale_one, lead, vecs, grad_middle, normed_one, grad_stack, (low,)
    )
    up_column = jnp.transpose(up_sum.reshape(-1, sp, each), (1, 0, 2)).reshape(1, -1)
    sums = jnp.concatenate([sums_one, sums_two, up_column], axis=0)
    sums_far = grid.cswap(sums)
    up_both = jnp.concatenate(in_order(sums[n_vec:], sums_far[n_vec:], core), axis=0)
    sums = jnp.concatenate(
        [sums[:n_vec] + sums_far[:n_vec], jnp.where(y == 0, up_both, 0.0), jnp.where(y == 0, 0.0, up_both)], axis=0
    )
    n_sums = n_vec + 4
    qv_sum = jnp.concatenate([stack_sum[0, :local], stack_sum[0, 2 * local :]]).reshape(-1, sp, each)
    n_bias = qv_sum.shape[0] * each
    qv_column = jnp.pad(jnp.transpose(qv_sum, (1, 0, 2)).reshape(sp, n_bias), ((0, 0), (0, part - n_bias)))
    columns = jnp.concatenate([jnp.transpose(sums), qv_column.reshape(-1, 1)], axis=1).astype(BF16)
    columns = jnp.pad(columns, ((0, 0), (0, 128 - columns.shape[1])))
    dw = jnp.concatenate([d_wqkv, columns], axis=1).reshape(nz, nx, 2, part, -1)
    dw_same, dw_other = pick(dw, core, 2), pick(dw, 1 - core, 2)
    from_spin = grid.spin(jnp.where(at_home, dw_other, dw_same), back=True)
    from_cross = grid.cross(dw_other)
    dw = from_spin.astype(F32) + jnp.where(at_home, dw_same, from_cross).astype(F32)
    dw_low = dw.astype(BF16)
    dw = pick(dw, grid.x, 1)
    for j in range(1, nx):
        dw = dw + grid.xshift(pick(dw_low, grid.far_x(j), 1), j).astype(F32)
    dw = lax.all_to_all(dw.astype(BF16), "z", 0, 0, tiled=True)
    g_qkv = place_qkv([dw[k] for k in range(nz)], [jnp.int32(k * local) for k in range(nz)], local)
    tails = dw[:, :, 3 * local :].astype(F32)
    sums = jnp.transpose(jnp.sum(tails[:, :, :n_sums], axis=0))
    up_rows = jnp.where(y == 0, sums[n_vec : n_vec + 2], sums[n_vec + 2 : n_vec + 4])
    g_up_bias = up_rows.reshape(-1, each)
    qv_tail = tails[:, :n_bias, n_sums].reshape(nz, 2, -1, each)
    g_qv_bias = jnp.transpose(qv_tail, (1, 0, 2, 3)).reshape(2, -1, each)

    grad_n1 = part_n1[0]
    for block in n1_far:
        grad_n1 = grad_n1 + block.astype(F32)
    input_grad = grad_middle + norm_back(unit_one[:rows].astype(F32), scale_one[:rows], vecs[2], grad_n1)
    input_grad = input_grad.astype(BF16)
    input_grad = jnp.concatenate(in_order(input_grad, grid.yswap(input_grad), y), axis=0).astype(F32)

    half_o = keep_o + grid.cswap(after(send_o, grad_branch)).astype(F32)
    block_out = half_o[:rows] + grid.yswap(half_o[rows:].astype(BF16)).astype(F32)
    block_out = (middle + (block_out + vecs[7])).astype(BF16)
    block_out = jnp.concatenate(in_order(block_out, grid.yswap(block_out), y), axis=0)
    dp = dot(grad_branch, after(attn_out, got), TN).astype(BF16).reshape(chips, 2, part, -1)
    dp = pick(dp, core, 1).astype(F32) + grid.cswap(pick(dp, 1 - core, 1)).astype(F32)
    dp_keep, dp_send = split(dp, 2, y)
    dp = dp_keep + grid.yswap(dp_send.astype(BF16)).astype(F32)
    d_proj = grid.scatter(dp.astype(BF16).reshape(nz, nx, part, -1))

    keep, send = split(after(d_ff, grad_n1), 0, core)
    low_cols, high_cols = in_order(keep, grid.cswap(send), core)
    n_hidden = grad_hidden.shape[1]
    d_up = jnp.concatenate([low_cols[:, :n_hidden], high_cols[:, :n_hidden]], axis=1).astype(F32)
    d_down = jnp.concatenate([low_cols[:, n_hidden:], high_cols[:, n_hidden:]], axis=1).astype(F32)
    return (
        block_out,
        input_grad,
        g_qkv,
        g_qv_bias,
        jnp.transpose(d_proj),
        sums[4],
        d_up,
        g_up_bias,
        jnp.transpose(d_down),
        sums[7],
        sums[2],
        sums[3],
        sums[5],
        sums[6],
        sums[0],
        sums[1],
    )


def solution(mesh):
    sp = mesh.shape["sp"]
    nz = 4
    devices = mesh.devices.reshape(nz, sp // (2 * nz), 2, mesh.shape["tp"])
    fine = jax.sharding.Mesh(devices, SP + ("tp",))
    line = P(SP)
    placed = (
        P(SP, None),
        line,
        P(),
        P(None, SP, "tp"),
        P(None, "tp", SP),
        P("tp", SP),
        line,
        P(SP, "tp"),
        P("tp", SP),
        P("tp", SP),
    ) + (line,) * 7 + (P(SP, None),)
    given = (
        P(SP, None),
        P(SP, None),
        P(None, SP, "tp"),
        P(None, "tp", SP),
        P("tp", SP),
        line,
        P(SP, "tp"),
        P("tp", SP),
        P("tp", SP),
    ) + (line,) * 7
    return jax.shard_map(per_device, mesh=fine, in_specs=placed, out_specs=given, check_vma=False)
```

```python
import functools

import jax
import jax.numpy as jnp
from jax import lax
from jax.experimental import pallas as pl
from jax.experimental.pallas import tpu as pltpu
from jax.sharding import PartitionSpec as P

HD = 64
EPSILON = 1e-05
EXCLUDED = -1e30
F32 = jnp.float32
BF16 = jnp.bfloat16
NN = (((1,), (0,)), ((), ()))
NT = (((1,), (1,)), ((), ()))
TN = (((0,), (0,)), ((), ()))


def dot(left, right, dims=NN):
    return lax.dot_general(left, right, dims, preferred_element_type=F32)


SP = ("z", "x", "core")


class Grid:
    def __init__(self):
        self.nz = lax.axis_size("z")
        self.nx = lax.axis_size("x")
        self.chips = self.nz * self.nx
        self.sp = 2 * self.chips
        me = lax.axis_index(SP)
        self.me = me
        self.core = me % 2
        self.x = (me // 2) % self.nx
        self.z = me // (2 * self.nx)
        self.y = lax.axis_index("tp")

    def _move(self, block, dz, dx, flip):
        pairs = []
        for i in range(self.sp):
            z, x, c = i // (2 * self.nx), (i // 2) % self.nx, i % 2
            to = (((z + dz) % self.nz) * self.nx + (x + dx) % self.nx) * 2 + (1 - c if flip else c)
            pairs.append((i, to))
        return lax.ppermute(block, SP, pairs)

    def zshift(self, block, k):
        return self._move(block, k, 0, False)

    def xshift(self, block, k):
        return self._move(block, 0, k, False)

    def cswap(self, block):
        return self._move(block, 0, 0, True)

    def yswap(self, block):
        return lax.ppermute(block, "tp", [(0, 1), (1, 0)])

    def _pairs(self, route):
        pairs = []
        for chip in range(self.chips):
            for (c, y), (to_c, to_y) in route:
                pairs.append(((chip * 2 + c) * 2 + y, (chip * 2 + to_c) * 2 + to_y))
        return pairs

    def spin(self, block, back=False):
        route = []
        for b in (0, 1):
            route += [((b, b), (b, 1 - b)), ((1 - b, b), (b, b))]
        if back:
            route = [(to, at) for at, to in route]
        return lax.ppermute(block, SP + ("tp",), self._pairs(route))

    def cross(self, block):
        route = [((1 - b, b), (b, 1 - b)) for b in (0, 1)]
        return lax.ppermute(block, SP + ("tp",), self._pairs(route))

    def far_z(self, k):
        return (self.z + k) % self.nz

    def far_x(self, j):
        return (self.x + j) % self.nx

    def gather(self, block):
        columns = [block] + [self.zshift(block, k) for k in range(1, self.nz)]
        return [p for b in columns for p in [b] + [self.xshift(b, j) for j in range(1, self.nx)]]

    def chip_order(self):
        order = jnp.arange(self.chips)
        return self.far_z(-(order // self.nx)) * self.nx + self.far_x(-(order % self.nx))

    def scatter(self, pieces):
        total = pick(pieces, self.x, 1).astype(F32)
        for j in range(1, self.nx):
            total = total + self.xshift(pick(pieces, self.far_x(j), 1), j).astype(F32)
        low = total.astype(pieces.dtype)
        mine = pick(total, self.z, 0)
        for k in range(1, self.nz):
            mine = mine + self.zshift(pick(low, self.far_z(k), 0), k).astype(F32)
        return mine


def pick(array, index, axis):
    return lax.dynamic_index_in_dim(array, index, axis, keepdims=False)


def normalize(values):
    center = values - jnp.mean(values, axis=-1, keepdims=True)
    spread = jnp.mean(center * center, axis=-1, keepdims=True)
    scale = lax.rsqrt(spread + EPSILON)
    return center * scale, scale


def norm_back(normed, scale, gain, grad):
    scaled = grad * gain
    mean_one = jnp.mean(scaled, axis=-1, keepdims=True)
    mean_two = jnp.mean(scaled * normed, axis=-1, keepdims=True)
    return (scaled - mean_one - normed * mean_two) * scale


def place_qkv_kernel(starts_ref, *refs):
    pieces, out_ref = refs[:-1], refs[-1]
    for i, piece in enumerate(pieces):
        size = out_ref.shape[2] // len(pieces)
        span = pl.ds(pl.multiple_of(starts_ref[i], size), size)
        for c in range(3):
            out_ref[c, :, span] = piece[:, c * size : (c + 1) * size].astype(F32)


def place_qkv(pieces, starts, columns):
    rows = pieces[0].shape[0]
    vmem = pl.BlockSpec(memory_space=pltpu.VMEM)
    return pl.pallas_call(
        place_qkv_kernel,
        out_shape=jax.ShapeDtypeStruct((3, rows, columns * len(pieces)), F32),
        in_specs=[pl.BlockSpec(memory_space=pltpu.SMEM)] + [vmem] * len(pieces),
        out_specs=vmem,
        name="place_qkv",
    )(jnp.stack(starts).astype(jnp.int32), *pieces)


def lane_in_head(shape, head):
    lanes = lax.broadcasted_iota(jnp.int32, shape, 1)
    return (lanes // HD) == (head % 2)


def pair_lanes(pair):
    return slice(pair * 2 * HD, (pair + 1) * 2 * HD)


STEP = 384
WIDE = 1536
BACK = 768
SMEM = pl.BlockSpec(memory_space=pltpu.SMEM)


def in_vmem(count):
    return [pl.BlockSpec(memory_space=pltpu.VMEM)] * count


COSTS = {"enter": 5, "attend": 14, "attend_back": 17, "whole_proj": 1, "project": 2, "branch": 2, "leave": 3, "close": 5, "outer": 5}


def local_kernel(kernel, name, out_shape, operands, scalars=1, scratch=(), flops=0, megabytes=48, before=()):
    if before:
        inner, at_end = kernel, len(operands)

        def kernel(*refs):
            inner(*refs[:at_end], *refs[at_end + len(before) :])

    single = not isinstance(out_shape, tuple)
    return pl.pallas_call(
        kernel,
        out_shape=out_shape,
        in_specs=[SMEM] * scalars + in_vmem(len(operands) - scalars) + [ANY] * len(before),
        out_specs=in_vmem(1)[0] if single else tuple(in_vmem(len(out_shape))),
        scratch_shapes=list(scratch),
        compiler_params=pltpu.CompilerParams(vmem_limit_bytes=megabytes * 1024 * 1024),
        cost_estimate=pl.CostEstimate(flops=COSTS.get(name, 0) * 1000000000, bytes_accessed=1 << 16, transcendentals=0),
        name=name,
    )(*operands, *before)


def turn_kernel(in_ref, out_ref):
    out_ref[...] = jnp.transpose(in_ref[...])


def turn(block, *before):
    return local_kernel(turn_kernel, "turn", shape(block.shape[::-1]), (block,), scalars=0, before=before)


def shape(dims, kind=BF16):
    return jax.ShapeDtypeStruct(tuple(dims), kind)


ANY = pl.BlockSpec(memory_space=pl.ANY)


def gate(block, *before):
    return pl.pallas_call(
        lambda *refs: None,
        out_shape=jax.ShapeDtypeStruct(block.shape, block.dtype),
        in_specs=[ANY] * (1 + len(before)),
        out_specs=ANY,
        input_output_aliases={0: 0},
        cost_estimate=pl.CostEstimate(flops=0, bytes_accessed=0, transcendentals=0),
        name="gate",
    )(block, *before)


def stack_kernel(count, *refs):
    for n in range(count):
        refs[-1][n] = refs[n][...]


def stack(blocks, *before):
    first = blocks[0]
    return pl.pallas_call(
        functools.partial(stack_kernel, len(blocks)),
        out_shape=jax.ShapeDtypeStruct((len(blocks),) + first.shape, first.dtype),
        in_specs=in_vmem(len(blocks)) + [ANY] * len(before),
        out_specs=in_vmem(1)[0],
        cost_estimate=pl.CostEstimate(flops=0, bytes_accessed=1 << 16, transcendentals=0),
        name="stack",
    )(*blocks, *before)


def turned(index, size):
    return lax.rem(index + size, size)


def enter_kernel(nz, nx, n_vec, part, at_ref, hour_ref, *refs):
    token_refs, refs = refs[: nz + 1], refs[nz + 1 :]
    pack_refs, refs = refs[: nx - 1], refs[nx - 1 :]
    weight_refs, refs = refs[:2], refs[2:]
    normed_ref, unit_ref, scale_ref, lead_ref, first_ref, vec_ref, weight_ref, q_ref, kv_ref = refs[:9]
    packs = refs[9]
    z, x, c = at_ref[0], at_ref[1], at_ref[2]
    rows, width = first_ref.shape
    tall = packs.shape[3]
    local = q_ref.shape[1]
    aux = slice(width, width + 128)
    for k in range(nz):
        packs[0, 0, k] = token_refs[k][:tall, aux]
        packs[0, 1, k] = token_refs[nz][k, :tall, aux]
    for j in range(1, nx):
        packs[j] = pack_refs[j - 1][...]
    for dev in range(2 * nz * nx):
        dev_z, dev_x, dev_c = dev // (2 * nx), (dev // 2) % nx, dev % 2
        block = packs[turned(x - dev_x, nx), turned(c - dev_c, 2), turned(z - dev_z, nz)]
        vec_ref[:, dev * part : (dev + 1) * part] = block[:n_vec, 64 : 64 + part].astype(F32)
    for n in range(2 * nz):
        ref = token_refs[n] if n < nz else token_refs[nz].at[n - nz]
        span = slice(n * rows, (n + 1) * rows)
        segment = ref[:, aux][:, :1].astype(F32)
        lead = jnp.zeros_like(segment)
        for i in range(hour_ref.shape[0]):
            lead = jnp.where(segment == float(i), hour_ref[i], lead)
        lead_ref[span, :] = lead
        value = ref[:, :width].astype(F32) + lead * vec_ref[0:1, :] + vec_ref[1:2, :]
        if n == 0:
            first_ref[...] = value
        unit, scale = normalize(value)
        scale_ref[span, :] = scale
        unit_ref[span, :] = unit.astype(BF16)
        normed_ref[span, :] = (unit * vec_ref[2:3, :] + vec_ref[3:4, :]).astype(BF16)
    for p, ref in enumerate(weight_refs):
        parity = c if p == 0 else 1 - c
        for j in range(nx):
            for k in range(nz):
                row = ((turned(z - k, nz) * nx + turned(x - j, nx)) * 2 + parity) * part
                weight_ref[pl.ds(pl.multiple_of(row, part), part), :] = ref[j, k]
    made = dot(normed_ref[...], weight_ref[...])
    q_ref[...] = made[:, :local]
    kv_ref[...] = made[:, local:].astype(BF16)


def enter(at, hours, tokens, packs, same, other, n_vec, part):
    nz, nx = len(tokens) - 1, len(packs) + 1
    rows, wide = tokens[0].shape
    width = wide - 128
    count = 2 * nz * rows
    local = same.shape[-1] // 3
    tall = packs[0].shape[2]
    return local_kernel(
        functools.partial(enter_kernel, nz, nx, n_vec, part),
        "enter",
        (
            shape((count, width)),
            shape((count, width)),
            shape((count, 1), F32),
            shape((count, 1), F32),
            shape((rows, width), F32),
            shape((n_vec, width), F32),
            shape((width, 3 * local)),
            shape((count, local), F32),
            shape((count, 2 * local)),
        ),
        (at, hours, *tokens, *packs, same, other),
        scalars=2,
        scratch=[pltpu.VMEM((nx, 2, nz, tall, 128), BF16)],
    )


def attend_kernel(pieces, heads, nz, at_ref, q_ref, bias_ref, qcode_ref, kcode_ref, *refs):
    kv_refs = refs[:pieces]
    out_ref, lse_ref, low_ref, send_ref = refs[pieces : pieces + 4]
    kaug, vturn, qaug, acc, stat = refs[pieces + 4 :]
    width = heads * HD
    count = q_ref.shape[0]
    rows = count // (2 * nz)
    steps = kv_refs[0].shape[0] // STEP
    low_ref[...] = (q_ref[...] + bias_ref[0:1, :]).astype(BF16) * jnp.asarray(HD ** (-0.5), BF16)
    for n in range(pieces * steps):
        block = kv_refs[n // steps]
        span_in = pl.ds((n % steps) * STEP, STEP)
        span = pl.ds(n * STEP, STEP)
        code = kcode_ref[span, :]
        for p in range(heads // 2):
            keys = block[span_in, pair_lanes(p)]
            for h in (2 * p, 2 * p + 1):
                kaug[h, span, :] = jnp.where(lane_in_head(keys.shape, h), keys, code)
        vturn[:, n * STEP : (n + 1) * STEP] = jnp.transpose(block[span_in, width:])
    for p in range(heads // 2):
        part = low_ref[:, pair_lanes(p)]
        for h in (2 * p, 2 * p + 1):
            qaug[h] = jnp.where(lane_in_head(part.shape, h), part, qcode_ref[...])
    stat[...] = jnp.ones_like(stat)
    for h in range(heads):
        span = slice(h * HD, (h + 1) * HD)
        top = total = out = None
        for n in range(kaug.shape[1] // WIDE):
            part = slice(n * WIDE, (n + 1) * WIDE)
            scores = dot(kaug[h, part, :], qaug[h], NT)
            peak = jnp.max(scores, axis=0, keepdims=True)
            new_top = peak if top is None else jnp.maximum(top, peak)
            weight = jnp.exp(scores - new_top)
            add = jnp.sum(weight, axis=0, keepdims=True)
            mixed = dot(vturn[span, part], weight.astype(BF16))
            if top is None:
                total, out = add, mixed
            else:
                rescale = jnp.exp(top - new_top)
                total, out = total * rescale + add, out * rescale + mixed
            top = new_top
        stat[0, h : h + 1, :] = top
        stat[1, h : h + 1, :] = total
        acc[span, :] = out / total
    out_ref[...] = jnp.transpose(acc[...])
    lse_ref[...] = stat[0] + jnp.log(jnp.maximum(stat[1], 1e-37))
    z = at_ref[0]
    for r in range(2):
        for k in range(nz):
            span = slice((r * nz + k) * rows, (r * nz + k + 1) * rows)
            send_ref[turned(z - k, nz), r] = (out_ref[span, :] + bias_ref[1:2, :]).astype(BF16)


def attend(at, nz, q, bias, qcode, kcode, kv_pieces):
    count, width = q.shape
    heads = width // HD
    keys = kcode.shape[0]
    return local_kernel(
        functools.partial(attend_kernel, len(kv_pieces), heads, nz),
        "attend",
        (
            shape((count, width), F32),
            shape((8, count), F32),
            shape((count, width)),
            shape((nz, 2, count // (2 * nz), width)),
        ),
        (at, q, bias, qcode, kcode, *kv_pieces),
        scratch=[
            pltpu.VMEM((heads, keys, 2 * HD), BF16),
            pltpu.VMEM((width, keys), BF16),
            pltpu.VMEM((heads, count, 2 * HD), BF16),
            pltpu.VMEM((width, count), F32),
            pltpu.VMEM((2, 8, count), F32),
        ],
    )


def attend_back_kernel(
    nx, heads, nz, at_ref, q_ref, qcode_ref, kcode_ref, got_ref, full_ref, lse_ref, *refs
):
    pieces = 2 * nx
    kv_refs = refs[:pieces]
    dq_ref, dkv_refs = refs[pieces], refs[pieces + 1 : pieces + 1 + nx]
    kaug, kturn, vals, qaug, qmask, domask, acc, dout, delta = refs[pieces + 1 + nx :]
    width = heads * HD
    count = q_ref.shape[0]
    rows = count // (2 * nz)
    steps = kv_refs[0].shape[0] // STEP
    z = at_ref[0]
    for r in range(2):
        for k in range(nz):
            span = slice((r * nz + k) * rows, (r * nz + k + 1) * rows)
            dout[span, :] = got_ref[turned(z - k, nz), r]
    product = dout[...].astype(F32) * full_ref[...]
    head_rows = lax.broadcasted_iota(jnp.int32, (8, width), 0)
    head_lanes = lax.broadcasted_iota(jnp.int32, (8, width), 1) // HD
    delta[...] = lax.dot_general(
        (head_rows == head_lanes).astype(F32),
        product,
        NT,
        precision=lax.Precision.HIGHEST,
        preferred_element_type=F32,
    )
    for n in range(pieces * steps):
        block = kv_refs[n // steps]
        span_in = pl.ds((n % steps) * STEP, STEP)
        span = pl.ds(n * STEP, STEP)
        code = kcode_ref[span, :]
        for p in range(heads // 2):
            keys = block[span_in, pair_lanes(p)]
            for h in (2 * p, 2 * p + 1):
                kaug[h, span, :] = jnp.where(lane_in_head(keys.shape, h), keys, code)
        kturn[:, n * STEP : (n + 1) * STEP] = jnp.transpose(block[span_in, :width])
        vals[span, :] = block[span_in, width:]
    for p in range(heads // 2):
        part = q_ref[:, pair_lanes(p)]
        dpart = dout[:, pair_lanes(p)]
        for h in (2 * p, 2 * p + 1):
            inside = lane_in_head(part.shape, h)
            qaug[h] = jnp.where(inside, part, qcode_ref[...])
            qmask[h] = jnp.where(inside, part, jnp.zeros_like(part))
            domask[h] = jnp.where(inside, dpart, jnp.zeros_like(dpart))
    total = [None] * heads
    for n in range(kaug.shape[1] // BACK):
        part = slice(n * BACK, (n + 1) * BACK)
        for p in range(heads // 2):
            dkey = dval = None
            for h in (2 * p, 2 * p + 1):
                scores = dot(kaug[h, part, :], qaug[h], NT)
                prob = jnp.exp(scores - lse_ref[h : h + 1, :])
                dprob = dot(vals[part, pair_lanes(p)], domask[h], NT)
                dscore = (prob * (dprob - delta[h : h + 1, :])).astype(BF16)
                add_val = dot(prob.astype(BF16), domask[h])
                add_key = dot(dscore, qmask[h])
                dval = add_val if dval is None else dval + add_val
                dkey = add_key if dkey is None else dkey + add_key
                add = dot(kturn[h * HD : (h + 1) * HD, part], dscore)
                total[h] = add if total[h] is None else total[h] + add
            each = dkv_refs[0].shape[0]
            size = min(BACK, each)
            for m in range(BACK // size):
                at_row = n * BACK + m * size
                rows_out = slice(at_row % each, at_row % each + size)
                rows_in = slice(m * size, (m + 1) * size)
                dkv_refs[at_row // each][rows_out, pair_lanes(p)] = dkey[rows_in].astype(BF16)
                lanes_out = slice(width + p * 2 * HD, width + (p + 1) * 2 * HD)
                dkv_refs[at_row // each][rows_out, lanes_out] = dval[rows_in].astype(BF16)
    for h in range(heads):
        acc[h * HD : (h + 1) * HD, :] = total[h]
    dq_ref[...] = (jnp.transpose(acc[...]) * (HD ** (-0.5))).astype(BF16)


def attend_back(at, nz, q, qcode, kcode, got, full, lse, kv_pieces):
    count, width = q.shape
    heads = width // HD
    keys = kcode.shape[0]
    nx = len(kv_pieces) // 2
    return local_kernel(
        functools.partial(attend_back_kernel, nx, heads, nz),
        "attend_back",
        (shape((count, width)),) + (shape((2 * count, 2 * width)),) * nx,
        (at, q, qcode, kcode, got, full, lse, *kv_pieces),
        scratch=[
            pltpu.VMEM((heads, keys, 2 * HD), BF16),
            pltpu.VMEM((width, keys), BF16),
            pltpu.VMEM((keys, width), BF16),
            pltpu.VMEM((heads, count, 2 * HD), BF16),
            pltpu.VMEM((heads, count, 2 * HD), BF16),
            pltpu.VMEM((heads, count, 2 * HD), BF16),
            pltpu.VMEM((width, count), F32),
            pltpu.VMEM((count, width), BF16),
            pltpu.VMEM((8, count), F32),
        ],
        megabytes=56,
    )


def whole_proj_kernel(nz, nx, part, at_ref, own_ref, far_ref, out_ref):
    z, x, c, y = at_ref[0], at_ref[1], at_ref[2], at_ref[3]
    half = out_ref.shape[1] // 2
    for p, ref in enumerate((own_ref, far_ref)):
        parity = c if p == 0 else 1 - c
        for w in range(2):
            column = pl.multiple_of(turned(y - w, 2) * half, half)
            for j in range(nx):
                for k in range(nz):
                    row = ((turned(z - k, nz) * nx + turned(x - j, nx)) * 2 + parity) * part
                    out_ref[pl.ds(pl.multiple_of(row, part), part), pl.ds(column, half)] = ref[w, j, k]


def whole_proj(at, own, far):
    _, nx, nz, part, half = own.shape
    return local_kernel(
        functools.partial(whole_proj_kernel, nz, nx, part),
        "whole_proj",
        shape((2 * nx * nz * part, 2 * half)),
        (at, own, far),
    )


def project_kernel(at_ref, got_ref, far_ref, weight_ref, first_ref, vec_ref, *refs):
    attn_ref, unit_ref, scale_ref, normed_ref, middle_ref = refs
    nz, _, _, local = got_ref.shape
    c = at_ref[2]
    for block in range(2):
        base = (c if block == 0 else 1 - c) * nz
        for z in range(nz):
            lane = pl.multiple_of((base + z) * local, local)
            attn_ref[:, pl.ds(lane, local)] = got_ref[z, 0] if block == 0 else far_ref[z]
    middle = first_ref[...] + (dot(attn_ref[...], weight_ref[...], NT) + vec_ref[4:5, :])
    middle_ref[...] = middle
    unit, scale = normalize(middle)
    unit_ref[...] = unit
    scale_ref[...] = scale
    normed_ref[...] = (unit * vec_ref[5:6, :] + vec_ref[6:7, :]).astype(BF16)


def project(at, got, far, weight, first, vecs):
    rows, width = first.shape
    return local_kernel(
        project_kernel,
        "project",
        (
            shape((rows, width)),
            shape((rows, width), F32),
            shape((rows, 1), F32),
            shape((rows, width)),
            shape((rows, width), F32),
        ),
        (at, got, far, weight, first, vecs),
    )


def feed_kernel(bias_ref, own_ref, near_ref, far_ref, gz_ref, weight, *refs):
    normed_ref, act_ref, gh_ref, sum_ref, keep_n_ref, send_n_ref, keep_o_ref, send_o_ref = refs[:8]
    back, out = refs[8:]
    rows = own_ref.shape[0]
    hidden_size = act_ref.shape[1]
    normed_ref[:rows, :] = own_ref[...]
    normed_ref[rows : 2 * rows, :] = near_ref[...]
    normed_ref[2 * rows :, :] = far_ref[...]
    step = 256
    for n in range(hidden_size // step):
        up = slice(n * step, (n + 1) * step)
        down = slice(hidden_size + n * step, hidden_size + (n + 1) * step)
        value = dot(normed_ref[...], weight[:, up]) + bias_ref[:, up]
        cdf = 0.5 * (1.0 + lax.erf(value * (0.5**0.5)))
        act = (value * cdf).astype(BF16)
        slope = cdf + value * (jnp.exp(-0.5 * value * value) * ((0.5 / jnp.pi) ** 0.5))
        low = (dot(gz_ref[...], weight[:, down]) * slope).astype(BF16)
        act_ref[:, up] = act
        gh_ref[:, up] = low
        sum_ref[:, up] = jnp.sum(low.astype(F32), axis=0, keepdims=True)
        add_back = dot(low, weight[:, up], NT)
        add_out = dot(act, weight[:, down], NT)
        if n == 0:
            back[...] = add_back
            out[...] = add_out
        else:
            back[...] += add_back
            out[...] += add_out
    keep_n_ref[...] = back[: 2 * rows, :]
    send_n_ref[...] = back[2 * rows :, :].astype(BF16)
    keep_o_ref[...] = out[: 2 * rows, :]
    send_o_ref[...] = out[2 * rows :, :].astype(BF16)


def feed(bias, own, near, far, gz, weight):
    count, width = gz.shape
    hidden_size = bias.shape[1]
    half = count // 2
    return local_kernel(
        feed_kernel,
        "feed",
        (
            shape((count, width)),
            shape((count, hidden_size)),
            shape((count, hidden_size)),
            shape((1, hidden_size), F32),
            shape((half, width), F32),
            shape((half, width)),
            shape((half, width), F32),
            shape((half, width)),
        ),
        (bias, own, near, far, gz, weight),
        scalars=0,
        scratch=[pltpu.VMEM((count, width), F32), pltpu.VMEM((count, width), F32)],
        megabytes=56,
    )


def outer_kernel(part, at_ref, normed_ref, gh_ref, gz_ref, act_ref, keep_ref, send_ref, made):
    hidden_size = gh_ref.shape[1]
    chips = keep_ref.shape[0] // part
    step = 256
    for base, left_ref, right_ref in ((0, normed_ref, gh_ref), (hidden_size, gz_ref, act_ref)):
        for n in range(hidden_size // step):
            made[...] = dot(left_ref[...], right_ref[:, n * step : (n + 1) * step], TN)
            lanes = slice(base + n * step, base + (n + 1) * step)
            for p in range(2):

                def store(ref, p=p, lanes=lanes):
                    for i in range(chips):
                        block = made[(2 * i + p) * part : (2 * i + p + 1) * part, :]
                        ref[i * part : (i + 1) * part, lanes] = block.astype(BF16)

                pl.when(at_ref[2] == p)(functools.partial(store, keep_ref))
                pl.when(at_ref[2] != p)(functools.partial(store, send_ref))


def outer(at, part, normed, gh, gz, act):
    width = normed.shape[1]
    out = shape((width // 2, 2 * gh.shape[1]))
    return local_kernel(
        functools.partial(outer_kernel, part),
        "outer",
        (out, out),
        (at, normed, gh, gz, act),
        scratch=[pltpu.VMEM((width, 256), F32)],
    )


def branch_kernel(at_ref, half_ref, near_ref, unit_ref, scale_ref, vec_ref, gz_ref, weight_ref, *refs):
    middle_ref, branch_ref, mine_ref, send_ref, sum_ref = refs
    rows = half_ref.shape[0] // 2
    nz, _, local = mine_ref.shape
    c = at_ref[2]
    grad = half_ref[:rows, :] + near_ref[...].astype(F32)
    top = gz_ref[...].astype(F32)
    unit = unit_ref[...]
    middle = top + norm_back(unit, scale_ref[...], vec_ref[5:6, :], grad)
    middle_ref[...] = middle
    low = middle.astype(BF16)
    branch_ref[...] = low
    made = dot(low, weight_ref[...]).astype(BF16)
    for h in range(2):
        for z in range(nz):
            block = made[:, (h * nz + z) * local : (h * nz + z + 1) * local]

            @pl.when(c == h)
            def _():
                mine_ref[z] = block

            @pl.when(c != h)
            def _():
                send_ref[z] = block

    sum_ref[...] = jnp.concatenate(
        [
            jnp.sum(low.astype(F32), axis=0, keepdims=True),
            jnp.sum(grad * unit, axis=0, keepdims=True),
            jnp.sum(grad, axis=0, keepdims=True),
            jnp.sum(top, axis=0, keepdims=True),
        ],
        axis=0,
    )


def branch(at, nz, half, near, unit, scale, vecs, gz, weight, before):
    rows, width = unit.shape
    local = width // (2 * nz)
    return local_kernel(
        branch_kernel,
        "branch",
        (
            shape((rows, width), F32),
            shape((rows, width)),
            shape((nz, rows, local)),
            shape((nz, rows, local)),
            shape((4, width), F32),
        ),
        (at, half, near, unit, scale, vecs, gz, weight),
        before=before,
    )


def leave_kernel(dq_ref, two_ref, near_ref, weight_ref, stack_ref, full_ref, send_ref):
    count, local = dq_ref.shape
    stack_ref[:, :local] = dq_ref[...]
    stack_ref[:, local:] = (two_ref[:count, :] + near_ref[...].astype(F32)).astype(BF16)
    full_ref[...] = dot(stack_ref[...], weight_ref[...], NT)
    send_ref[...] = full_ref[count // 2 :, :].astype(BF16)


def leave(dq, two, near, weight):
    count, local = dq.shape
    width = weight.shape[0]
    return local_kernel(
        leave_kernel,
        "leave",
        (shape((count, 3 * local)), shape((count, width), F32), shape((count // 2, width))),
        (dq, two, near, weight),
        scalars=0,
    )


def close_kernel(rows, full_ref, unit_ref, scale_ref, lead_ref, vec_ref, middle_ref, normed_ref, stack_ref, *refs):
    sum_ref, bias_ref, out_ref = refs
    count, width = full_ref.shape
    lead_row = jnp.zeros((4, width), F32)
    for n in range(count // rows):
        span = slice(n * rows, (n + 1) * rows)
        grad = full_ref[span, :]
        unit = unit_ref[span, :].astype(F32)
        back = norm_back(unit, scale_ref[span, :], vec_ref[2:3, :], grad)
        if n == 0:
            back = back + middle_ref[...]
        lead_row = lead_row + jnp.concatenate(
            [
                jnp.sum(back * lead_ref[span, :], axis=0, keepdims=True),
                jnp.sum(back, axis=0, keepdims=True),
                jnp.sum(grad * unit, axis=0, keepdims=True),
                jnp.sum(grad, axis=0, keepdims=True),
            ],
            axis=0,
        )
    sum_ref[...] = lead_row
    bias_ref[...] = jnp.sum(stack_ref[...].astype(F32), axis=0, keepdims=True)
    out_ref[...] = dot(normed_ref[...], stack_ref[...], TN).astype(BF16)


def close(rows, full, unit, scale, lead, vecs, middle, normed, stack, before):
    width = full.shape[1]
    return local_kernel(
        functools.partial(close_kernel, rows),
        "close",
        (shape((4, width), F32), shape((1, stack.shape[1]), F32), shape((width, stack.shape[1]))),
        (full, unit, scale, lead, vecs, middle, normed, stack),
        scalars=0,
        before=before,
    )


def after(block, *before):
    return lax.optimization_barrier((block,) + before)[0]


def per_device(
    tokens,
    segment_ids,
    lead_hours,
    qkv_weight,
    qv_bias,
    proj_weight,
    proj_bias,
    up_weight,
    up_bias,
    down_weight,
    down_bias,
    norm1_gain,
    norm1_bias,
    norm2_gain,
    norm2_bias,
    lead_weight,
    lead_bias,
    out_grad,
):
    grid = Grid()
    nz, nx, chips, sp = grid.nz, grid.nx, grid.chips, grid.sp
    core, y = grid.core, grid.y
    at = jnp.stack([grid.z, grid.x, core, y]).astype(jnp.int32)
    full_rows, width = tokens.shape
    rows = full_rows // 2
    part = norm1_gain.shape[0]
    each = HD // sp
    at_home = core == y

    def split(array, axis, index):
        half = array.shape[axis] // 2
        first = lax.slice_in_dim(array, 0, half, axis=axis)
        second = lax.slice_in_dim(array, half, 2 * half, axis=axis)
        return jnp.where(index == 0, first, second), jnp.where(index == 0, second, first)

    def in_order(own, other, index):
        return jnp.where(index == 0, own, other), jnp.where(index == 0, other, own)

    shard = jnp.transpose(qkv_weight.reshape(3, part, nz, -1), (2, 1, 0, 3)).reshape(nz, part, -1)
    wq_z = [pick(shard, grid.z, 0)] + [grid.zshift(pick(shard, grid.far_z(k), 0), k) for k in range(1, nz)]

    vectors = [lead_weight, lead_bias, norm1_gain, norm1_bias, proj_bias, norm2_gain, norm2_bias, down_bias]
    n_vec = len(vectors)
    n_qv, n_up = qv_bias.size // part, up_bias.size // part
    pack = jnp.concatenate(
        [
            jnp.stack(vectors),
            qv_bias.reshape(-1, part),
            up_bias.reshape(-1, part),
            segment_ids.astype(BF16).reshape(-1, part),
        ],
        axis=0,
    )
    pack_rows = pack.shape[0]
    tall = -(-pack_rows // 16) * 16
    pack = jnp.pad(pack, ((0, rows - pack_rows), (63, 128 - 64 - part)))
    own_segments = split(segment_ids, 0, y)[0]
    beside = jnp.concatenate([own_segments.astype(BF16)[:, None], pack], axis=1)
    own_tokens = jnp.concatenate([split(tokens, 0, y)[0], beside], axis=1)
    token_far = [grid.zshift(own_tokens, k) for k in range(1, nz)]
    token_z = jnp.stack([own_tokens] + token_far)
    token_c = grid.cswap(token_z)
    packs_own = jnp.stack([token_z[:, :tall, width:], token_c[:, :tall, width:]])
    packs_far = [grid.xshift(packs_own, j) for j in range(1, nx)]

    wq_z = jnp.stack(wq_z)
    wq_x = jnp.stack([wq_z] + [grid.xshift(wq_z, j) for j in range(1, nx)])
    wq_spin, wq_cross = grid.spin(wq_x), grid.cross(wq_x)
    wq_same = jnp.where(at_home, wq_x, wq_spin)
    wq_other = jnp.where(at_home, wq_spin, wq_cross)

    normed_one, unit_one, scale_one, lead, embedded, vecs, w_qkv, q_raw, kv = enter(
        at, lead_hours, [own_tokens] + token_far + [token_c], packs_far, wq_same, wq_other, n_vec, part
    )
    local = q_raw.shape[1]
    kv_far = grid.yswap(kv)
    kv_pieces = [kv, kv_far]
    for j in range(1, nx):
        kv_pieces += [grid.xshift(kv, j), grid.xshift(kv_far, j)]

    table = jnp.stack([packs_own] + packs_far)[:, :, :, n_vec:pack_rows, 64 : 64 + part].reshape(sp, -1)
    n = jnp.arange(sp)
    rel_j, rel_r, rel_k = n // (2 * nz), (n // nz) % 2, n % nz
    device = (grid.far_z(-rel_k) * nx + grid.far_x(-rel_j)) * 2 + (core + rel_r) % 2
    in_place = (jnp.arange(sp)[:, None] == device[None, :]).astype(BF16)
    table = dot(in_place, table).reshape(sp, -1, part)
    heads_local = qv_bias.shape[1]
    qv_all = jnp.transpose(table[:, :n_qv].reshape(sp, 2, heads_local, -1), (1, 2, 0, 3)).reshape(2, heads_local * HD)
    qv_far = grid.yswap(qv_all)
    qv_full = pick(jnp.where(at_home, qv_all, qv_far).reshape(2, nz, -1), grid.z, 1)
    seg_rows = table[:, n_qv + n_up :].reshape(sp * 2, rows)
    n = jnp.arange(nx * 2 * 2 * nz)
    k, r, w, j = n % nz, (n // nz) % 2, (n // (2 * nz)) % 2, n // (4 * nz)
    key_at = ((grid.far_z(-k) * nx + grid.far_x(-j)) * 2 + (core + r) % 2) * 2 + (y + w) % 2
    take = (key_at[:, None] == jnp.arange(2 * sp)[None, :]).astype(BF16)
    key_seg = dot(take, seg_rows.astype(BF16)).astype(jnp.int32).reshape(-1)
    query_seg = key_seg[: 2 * nz * rows]
    lanes = jnp.arange(2 * HD, dtype=jnp.int32) % HD
    kcode = jnp.where(key_seg[:, None] == lanes[None, :], 0.0, EXCLUDED).astype(BF16)
    qcode = (query_seg[:, None] == lanes[None, :]).astype(BF16)
    up_all = jnp.transpose(table[:, n_qv : n_qv + n_up].reshape(sp, up_bias.shape[0], -1), (1, 0, 2)).reshape(1, -1)
    up_full = split(up_all, 1, core)[0]

    up_shard, down_shard, _ = lax.optimization_barrier((up_weight, down_weight, wq_z))
    up_keep, up_send = split(up_shard, 1, core)
    down_keep, down_send = split(jnp.transpose(down_shard), 1, core)
    ff_far = grid.cswap(jnp.concatenate([up_send, down_send], axis=1))
    ff = jnp.concatenate(in_order(jnp.concatenate([up_keep, down_keep], axis=1), ff_far, core), axis=0)
    w_ff = lax.all_gather(after(ff, *token_far), ("z", "x"), axis=0, tiled=True)

    gz_own, gz_far = split(after(out_grad, kv), 0, y)
    gz_two = jnp.concatenate([gz_own, gz_far], axis=0)
    gz = jnp.concatenate([gz_two, grid.cswap(gz_two)], axis=0)

    wp = jnp.transpose(after(proj_weight, wq_spin, token_c))
    wp_z = jnp.stack([wp] + [grid.zshift(wp, k) for k in range(1, nz)])
    wp_z = after(wp_z, kv)
    wp_x = jnp.stack([wp_z] + [grid.xshift(wp_z, j) for j in range(1, nx)])
    wp_x = after(wp_x, kv_far)
    wp_own = jnp.stack([wp_x, grid.yswap(wp_x)])
    w_proj = whole_proj(at, wp_own, grid.cswap(wp_own))

    q_raw, up_full, gz = lax.optimization_barrier((q_raw, up_full, gz))
    attn_full, lse, q, attn_send = attend(at, nz, q_raw, qv_full, qcode, kcode, kv_pieces)
    attn_got = lax.all_to_all(attn_send, "z", 0, 0, tiled=True)
    attn_far = grid.cswap(attn_got[:, 1])
    attn_out, n2, s2, normed, middle = project(at, attn_got, attn_far, w_proj, embedded, vecs)
    near = grid.yswap(normed)
    far = grid.cswap(jnp.concatenate([normed, near], axis=0))
    normed_two, active, grad_hidden, up_sum, keep_n, send_n, keep_o, send_o = feed(up_full, normed, near, far, gz, w_ff)

    half_n = keep_n + grid.cswap(send_n).astype(F32)
    near_n = grid.yswap(half_n[rows:].astype(BF16))
    d_outer, d_send = outer(at, part, normed_two, grad_hidden, gz, active)
    d_both = jnp.concatenate([d_outer, grid.cswap(d_send)], axis=1)
    d_ff = lax.psum_scatter(d_both, ("z", "x"), scatter_dimension=0, tiled=True)
    grad_middle, grad_branch, mine, send, sums_two = branch(
        at, nz, half_n, near_n, n2, s2, vecs, gz[:rows], w_proj, (d_outer,)
    )
    theirs = grid.cswap(send)
    got = lax.all_to_all(jnp.stack([mine, theirs], axis=1), "z", 0, 0, tiled=True)

    back = attend_back(at, nz, q, qcode, kcode, got, attn_full, lse, kv_pieces)
    grad_q, grad_kv = back[0], back[1].astype(F32)
    for j in range(1, nx):
        grad_kv = grad_kv + grid.xshift(back[1 + j], -j).astype(F32)
    count = 2 * nz * rows
    near_kv = grid.yswap(grad_kv[count:].astype(BF16))
    grad_stack, part_full, part_send = leave(grad_q, grad_kv, near_kv, w_qkv)

    part_n1 = (part_full[: nz * rows] + grid.cswap(part_send).astype(F32)).reshape(nz, rows, width)
    low = part_n1.astype(BF16)
    n1_far = [grid.zshift(low[k], -k) for k in range(1, nz)]

    sums_one, stack_sum, d_wqkv = close(
        rows, part_full, unit_one, scale_one, lead, vecs, grad_middle, normed_one, grad_stack, (low,)
    )
    up_column = jnp.transpose(up_sum.reshape(-1, sp, each), (1, 0, 2)).reshape(1, -1)
    sums = jnp.concatenate([sums_one, sums_two, up_column], axis=0)
    sums_far = grid.cswap(sums)
    up_both = jnp.concatenate(in_order(sums[n_vec:], sums_far[n_vec:], core), axis=0)
    sums = jnp.concatenate(
        [sums[:n_vec] + sums_far[:n_vec], jnp.where(y == 0, up_both, 0.0), jnp.where(y == 0, 0.0, up_both)], axis=0
    )
    n_sums = n_vec + 4
    qv_sum = jnp.concatenate([stack_sum[0, :local], stack_sum[0, 2 * local :]]).reshape(-1, sp, each)
    n_bias = qv_sum.shape[0] * each
    qv_column = jnp.pad(jnp.transpose(qv_sum, (1, 0, 2)).reshape(sp, n_bias), ((0, 0), (0, part - n_bias)))
    columns = jnp.concatenate([jnp.transpose(sums), qv_column.reshape(-1, 1)], axis=1).astype(BF16)
    columns = jnp.pad(columns, ((0, 0), (0, 128 - columns.shape[1])))
    dw = jnp.concatenate([d_wqkv, columns], axis=1).reshape(nz, nx, 2, part, -1)
    dw_same, dw_other = pick(dw, core, 2), pick(dw, 1 - core, 2)
    from_spin = grid.spin(jnp.where(at_home, dw_other, dw_same), back=True)
    from_cross = grid.cross(dw_other)
    dw = from_spin.astype(F32) + jnp.where(at_home, dw_same, from_cross).astype(F32)
    dw_low = dw.astype(BF16)
    dw = pick(dw, grid.x, 1)
    for j in range(1, nx):
        dw = dw + grid.xshift(pick(dw_low, grid.far_x(j), 1), j).astype(F32)
    dw = lax.all_to_all(dw.astype(BF16), "z", 0, 0, tiled=True)
    g_qkv = place_qkv([dw[k] for k in range(nz)], [jnp.int32(k * local) for k in range(nz)], local)
    tails = dw[:, :, 3 * local :].astype(F32)
    sums = jnp.transpose(jnp.sum(tails[:, :, :n_sums], axis=0))
    up_rows = jnp.where(y == 0, sums[n_vec : n_vec + 2], sums[n_vec + 2 : n_vec + 4])
    g_up_bias = up_rows.reshape(-1, each)
    qv_tail = tails[:, :n_bias, n_sums].reshape(nz, 2, -1, each)
    g_qv_bias = jnp.transpose(qv_tail, (1, 0, 2, 3)).reshape(2, -1, each)

    grad_n1 = part_n1[0]
    for block in n1_far:
        grad_n1 = grad_n1 + block.astype(F32)
    input_grad = grad_middle + norm_back(unit_one[:rows].astype(F32), scale_one[:rows], vecs[2], grad_n1)
    input_grad = input_grad.astype(BF16)
    input_grad = jnp.concatenate(in_order(input_grad, grid.yswap(input_grad), y), axis=0).astype(F32)

    half_o = keep_o + grid.cswap(after(send_o, grad_branch)).astype(F32)
    block_out = half_o[:rows] + grid.yswap(half_o[rows:].astype(BF16)).astype(F32)
    block_out = (middle + (block_out + vecs[7])).astype(BF16)
    block_out = jnp.concatenate(in_order(block_out, grid.yswap(block_out), y), axis=0)
    dp = dot(grad_branch, after(attn_out, got), TN).astype(BF16).reshape(chips, 2, part, -1)
    dp = pick(dp, core, 1).astype(F32) + grid.cswap(pick(dp, 1 - core, 1)).astype(F32)
    dp_keep, dp_send = split(dp, 2, y)
    dp = dp_keep + grid.yswap(dp_send.astype(BF16)).astype(F32)
    d_proj = grid.scatter(dp.astype(BF16).reshape(nz, nx, part, -1))

    n_cols = 2 * grad_hidden.shape[1]
    low_cols, high_cols = in_order(d_ff[:, :n_cols], d_ff[:, n_cols:], core)
    n_hidden = grad_hidden.shape[1]
    d_up = jnp.concatenate([low_cols[:, :n_hidden], high_cols[:, :n_hidden]], axis=1).astype(F32)
    d_down = jnp.concatenate([low_cols[:, n_hidden:], high_cols[:, n_hidden:]], axis=1).astype(F32)
    return (
        block_out,
        input_grad,
        g_qkv,
        g_qv_bias,
        jnp.transpose(d_proj),
        sums[4],
        d_up,
        g_up_bias,
        jnp.transpose(d_down),
        sums[7],
        sums[2],
        sums[3],
        sums[5],
        sums[6],
        sums[0],
        sums[1],
    )


def solution(mesh):
    sp = mesh.shape["sp"]
    nz = 4
    devices = mesh.devices.reshape(nz, sp // (2 * nz), 2, mesh.shape["tp"])
    fine = jax.sharding.Mesh(devices, SP + ("tp",))
    line = P(SP)
    placed = (
        P(SP, None),
        line,
        P(),
        P(None, SP, "tp"),
        P(None, "tp", SP),
        P("tp", SP),
        line,
        P(SP, "tp"),
        P("tp", SP),
        P("tp", SP),
    ) + (line,) * 7 + (P(SP, None),)
    given = (
        P(SP, None),
        P(SP, None),
        P(None, SP, "tp"),
        P(None, "tp", SP),
        P("tp", SP),
        line,
        P(SP, "tp"),
        P("tp", SP),
        P("tp", SP),
    ) + (line,) * 7
    return jax.shard_map(per_device, mesh=fine, in_specs=placed, out_specs=given, check_vma=False)
```

```python
import functools

import jax
import jax.numpy as jnp
from jax import lax
from jax.experimental import pallas as pl
from jax.experimental.pallas import tpu as pltpu
from jax.sharding import PartitionSpec as P

HD = 64
EPSILON = 1e-05
EXCLUDED = -1e30
F32 = jnp.float32
BF16 = jnp.bfloat16
NN = (((1,), (0,)), ((), ()))
NT = (((1,), (1,)), ((), ()))
TN = (((0,), (0,)), ((), ()))


def dot(left, right, dims=NN):
    return lax.dot_general(left, right, dims, preferred_element_type=F32)


SP = ("z", "x", "core")


class Grid:
    def __init__(self):
        self.nz = lax.axis_size("z")
        self.nx = lax.axis_size("x")
        self.chips = self.nz * self.nx
        self.sp = 2 * self.chips
        me = lax.axis_index(SP)
        self.me = me
        self.core = me % 2
        self.x = (me // 2) % self.nx
        self.z = me // (2 * self.nx)
        self.y = lax.axis_index("tp")

    def _move(self, block, dz, dx, flip):
        pairs = []
        for i in range(self.sp):
            z, x, c = i // (2 * self.nx), (i // 2) % self.nx, i % 2
            to = (((z + dz) % self.nz) * self.nx + (x + dx) % self.nx) * 2 + (1 - c if flip else c)
            pairs.append((i, to))
        return lax.ppermute(block, SP, pairs)

    def zshift(self, block, k):
        return self._move(block, k, 0, False)

    def xshift(self, block, k):
        return self._move(block, 0, k, False)

    def cswap(self, block):
        return self._move(block, 0, 0, True)

    def yswap(self, block):
        return lax.ppermute(block, "tp", [(0, 1), (1, 0)])

    def _pairs(self, route):
        pairs = []
        for chip in range(self.chips):
            for (c, y), (to_c, to_y) in route:
                pairs.append(((chip * 2 + c) * 2 + y, (chip * 2 + to_c) * 2 + to_y))
        return pairs

    def spin(self, block, back=False):
        route = []
        for b in (0, 1):
            route += [((b, b), (b, 1 - b)), ((1 - b, b), (b, b))]
        if back:
            route = [(to, at) for at, to in route]
        return lax.ppermute(block, SP + ("tp",), self._pairs(route))

    def cross(self, block):
        route = [((1 - b, b), (b, 1 - b)) for b in (0, 1)]
        return lax.ppermute(block, SP + ("tp",), self._pairs(route))

    def far_z(self, k):
        return (self.z + k) % self.nz

    def far_x(self, j):
        return (self.x + j) % self.nx

    def gather(self, block):
        columns = [block] + [self.zshift(block, k) for k in range(1, self.nz)]
        return [p for b in columns for p in [b] + [self.xshift(b, j) for j in range(1, self.nx)]]

    def chip_order(self):
        order = jnp.arange(self.chips)
        return self.far_z(-(order // self.nx)) * self.nx + self.far_x(-(order % self.nx))

    def scatter(self, pieces):
        total = pick(pieces, self.x, 1).astype(F32)
        for j in range(1, self.nx):
            total = total + self.xshift(pick(pieces, self.far_x(j), 1), j).astype(F32)
        low = total.astype(pieces.dtype)
        mine = pick(total, self.z, 0)
        for k in range(1, self.nz):
            mine = mine + self.zshift(pick(low, self.far_z(k), 0), k).astype(F32)
        return mine


def pick(array, index, axis):
    return lax.dynamic_index_in_dim(array, index, axis, keepdims=False)


def normalize(values):
    center = values - jnp.mean(values, axis=-1, keepdims=True)
    spread = jnp.mean(center * center, axis=-1, keepdims=True)
    scale = lax.rsqrt(spread + EPSILON)
    return center * scale, scale


def norm_back(normed, scale, gain, grad):
    scaled = grad * gain
    mean_one = jnp.mean(scaled, axis=-1, keepdims=True)
    mean_two = jnp.mean(scaled * normed, axis=-1, keepdims=True)
    return (scaled - mean_one - normed * mean_two) * scale


def place_qkv_kernel(starts_ref, *refs):
    pieces, out_ref = refs[:-1], refs[-1]
    for i, piece in enumerate(pieces):
        size = out_ref.shape[2] // len(pieces)
        span = pl.ds(pl.multiple_of(starts_ref[i], size), size)
        for c in range(3):
            out_ref[c, :, span] = piece[:, c * size : (c + 1) * size].astype(F32)


def place_qkv(pieces, starts, columns):
    rows = pieces[0].shape[0]
    vmem = pl.BlockSpec(memory_space=pltpu.VMEM)
    return pl.pallas_call(
        place_qkv_kernel,
        out_shape=jax.ShapeDtypeStruct((3, rows, columns * len(pieces)), F32),
        in_specs=[pl.BlockSpec(memory_space=pltpu.SMEM)] + [vmem] * len(pieces),
        out_specs=vmem,
        name="place_qkv",
    )(jnp.stack(starts).astype(jnp.int32), *pieces)


def lane_in_head(shape, head):
    lanes = lax.broadcasted_iota(jnp.int32, shape, 1)
    return (lanes // HD) == (head % 2)


def pair_lanes(pair):
    return slice(pair * 2 * HD, (pair + 1) * 2 * HD)


STEP = 384
WIDE = 1536
BACK = 768
SMEM = pl.BlockSpec(memory_space=pltpu.SMEM)


def in_vmem(count):
    return [pl.BlockSpec(memory_space=pltpu.VMEM)] * count


COSTS = {"enter": 5, "attend": 14, "attend_back": 17, "whole_proj": 1, "project": 2, "branch": 2, "leave": 3, "close": 5, "outer": 5}


def local_kernel(kernel, name, out_shape, operands, scalars=1, scratch=(), flops=0, megabytes=48, before=()):
    if before:
        inner, at_end = kernel, len(operands)

        def kernel(*refs):
            inner(*refs[:at_end], *refs[at_end + len(before) :])

    single = not isinstance(out_shape, tuple)
    return pl.pallas_call(
        kernel,
        out_shape=out_shape,
        in_specs=[SMEM] * scalars + in_vmem(len(operands) - scalars) + [ANY] * len(before),
        out_specs=in_vmem(1)[0] if single else tuple(in_vmem(len(out_shape))),
        scratch_shapes=list(scratch),
        compiler_params=pltpu.CompilerParams(vmem_limit_bytes=megabytes * 1024 * 1024),
        cost_estimate=pl.CostEstimate(flops=COSTS.get(name, 0) * 1000000000, bytes_accessed=1 << 16, transcendentals=0),
        name=name,
    )(*operands, *before)


def turn_kernel(in_ref, out_ref):
    out_ref[...] = jnp.transpose(in_ref[...])


def turn(block, *before):
    return local_kernel(turn_kernel, "turn", shape(block.shape[::-1]), (block,), scalars=0, before=before)


def shape(dims, kind=BF16):
    return jax.ShapeDtypeStruct(tuple(dims), kind)


ANY = pl.BlockSpec(memory_space=pl.ANY)


def gate(block, *before):
    return pl.pallas_call(
        lambda *refs: None,
        out_shape=jax.ShapeDtypeStruct(block.shape, block.dtype),
        in_specs=[ANY] * (1 + len(before)),
        out_specs=ANY,
        input_output_aliases={0: 0},
        cost_estimate=pl.CostEstimate(flops=0, bytes_accessed=0, transcendentals=0),
        name="gate",
    )(block, *before)


def stack_kernel(count, *refs):
    for n in range(count):
        refs[-1][n] = refs[n][...]


def stack(blocks, *before):
    first = blocks[0]
    return pl.pallas_call(
        functools.partial(stack_kernel, len(blocks)),
        out_shape=jax.ShapeDtypeStruct((len(blocks),) + first.shape, first.dtype),
        in_specs=in_vmem(len(blocks)) + [ANY] * len(before),
        out_specs=in_vmem(1)[0],
        cost_estimate=pl.CostEstimate(flops=0, bytes_accessed=1 << 16, transcendentals=0),
        name="stack",
    )(*blocks, *before)


def turned(index, size):
    return lax.rem(index + size, size)


def enter_kernel(nz, nx, n_vec, part, at_ref, hour_ref, *refs):
    token_refs, refs = refs[: nz + 1], refs[nz + 1 :]
    pack_refs, refs = refs[: nx - 1], refs[nx - 1 :]
    weight_refs, refs = refs[:2], refs[2:]
    normed_ref, unit_ref, scale_ref, lead_ref, first_ref, vec_ref, weight_ref, q_ref, kv_ref = refs[:9]
    packs = refs[9]
    z, x, c = at_ref[0], at_ref[1], at_ref[2]
    rows, width = first_ref.shape
    tall = packs.shape[3]
    local = q_ref.shape[1]
    aux = slice(width, width + 128)
    for k in range(nz):
        packs[0, 0, k] = token_refs[k][:tall, aux]
        packs[0, 1, k] = token_refs[nz][k, :tall, aux]
    for j in range(1, nx):
        packs[j] = pack_refs[j - 1][...]
    for dev in range(2 * nz * nx):
        dev_z, dev_x, dev_c = dev // (2 * nx), (dev // 2) % nx, dev % 2
        block = packs[turned(x - dev_x, nx), turned(c - dev_c, 2), turned(z - dev_z, nz)]
        vec_ref[:, dev * part : (dev + 1) * part] = block[:n_vec, 64 : 64 + part].astype(F32)
    for n in range(2 * nz):
        ref = token_refs[n] if n < nz else token_refs[nz].at[n - nz]
        span = slice(n * rows, (n + 1) * rows)
        segment = ref[:, aux][:, :1].astype(F32)
        lead = jnp.zeros_like(segment)
        for i in range(hour_ref.shape[0]):
            lead = jnp.where(segment == float(i), hour_ref[i], lead)
        lead_ref[span, :] = lead
        value = ref[:, :width].astype(F32) + lead * vec_ref[0:1, :] + vec_ref[1:2, :]
        if n == 0:
            first_ref[...] = value
        unit, scale = normalize(value)
        scale_ref[span, :] = scale
        unit_ref[span, :] = unit.astype(BF16)
        normed_ref[span, :] = (unit * vec_ref[2:3, :] + vec_ref[3:4, :]).astype(BF16)
    for p, ref in enumerate(weight_refs):
        parity = c if p == 0 else 1 - c
        for j in range(nx):
            for k in range(nz):
                row = ((turned(z - k, nz) * nx + turned(x - j, nx)) * 2 + parity) * part
                weight_ref[pl.ds(pl.multiple_of(row, part), part), :] = ref[j, k]
    made = dot(normed_ref[...], weight_ref[...])
    q_ref[...] = made[:, :local]
    kv_ref[...] = made[:, local:].astype(BF16)


def enter(at, hours, tokens, packs, same, other, n_vec, part):
    nz, nx = len(tokens) - 1, len(packs) + 1
    rows, wide = tokens[0].shape
    width = wide - 128
    count = 2 * nz * rows
    local = same.shape[-1] // 3
    tall = packs[0].shape[2]
    return local_kernel(
        functools.partial(enter_kernel, nz, nx, n_vec, part),
        "enter",
        (
            shape((count, width)),
            shape((count, width)),
            shape((count, 1), F32),
            shape((count, 1), F32),
            shape((rows, width), F32),
            shape((n_vec, width), F32),
            shape((width, 3 * local)),
            shape((count, local), F32),
            shape((count, 2 * local)),
        ),
        (at, hours, *tokens, *packs, same, other),
        scalars=2,
        scratch=[pltpu.VMEM((nx, 2, nz, tall, 128), BF16)],
    )


def attend_kernel(pieces, heads, nz, at_ref, q_ref, bias_ref, qcode_ref, kcode_ref, *refs):
    kv_refs = refs[:pieces]
    out_ref, lse_ref, low_ref, send_ref = refs[pieces : pieces + 4]
    kaug, vturn, qaug, acc, stat = refs[pieces + 4 :]
    width = heads * HD
    count = q_ref.shape[0]
    rows = count // (2 * nz)
    steps = kv_refs[0].shape[0] // STEP
    low_ref[...] = (q_ref[...] + bias_ref[0:1, :]).astype(BF16) * jnp.asarray(HD ** (-0.5), BF16)
    for n in range(pieces * steps):
        block = kv_refs[n // steps]
        span_in = pl.ds((n % steps) * STEP, STEP)
        span = pl.ds(n * STEP, STEP)
        code = kcode_ref[span, :]
        for p in range(heads // 2):
            keys = block[span_in, pair_lanes(p)]
            for h in (2 * p, 2 * p + 1):
                kaug[h, span, :] = jnp.where(lane_in_head(keys.shape, h), keys, code)
        vturn[:, n * STEP : (n + 1) * STEP] = jnp.transpose(block[span_in, width:])
    for p in range(heads // 2):
        part = low_ref[:, pair_lanes(p)]
        for h in (2 * p, 2 * p + 1):
            qaug[h] = jnp.where(lane_in_head(part.shape, h), part, qcode_ref[...])
    stat[...] = jnp.ones_like(stat)
    for h in range(heads):
        span = slice(h * HD, (h + 1) * HD)
        top = total = out = None
        for n in range(kaug.shape[1] // WIDE):
            part = slice(n * WIDE, (n + 1) * WIDE)
            scores = dot(kaug[h, part, :], qaug[h], NT)
            peak = jnp.max(scores, axis=0, keepdims=True)
            new_top = peak if top is None else jnp.maximum(top, peak)
            weight = jnp.exp(scores - new_top)
            add = jnp.sum(weight, axis=0, keepdims=True)
            mixed = dot(vturn[span, part], weight.astype(BF16))
            if top is None:
                total, out = add, mixed
            else:
                rescale = jnp.exp(top - new_top)
                total, out = total * rescale + add, out * rescale + mixed
            top = new_top
        stat[0, h : h + 1, :] = top
        stat[1, h : h + 1, :] = total
        acc[span, :] = out / total
    out_ref[...] = jnp.transpose(acc[...])
    lse_ref[...] = stat[0] + jnp.log(jnp.maximum(stat[1], 1e-37))
    z = at_ref[0]
    for r in range(2):
        for k in range(nz):
            span = slice((r * nz + k) * rows, (r * nz + k + 1) * rows)
            send_ref[turned(z - k, nz), r] = (out_ref[span, :] + bias_ref[1:2, :]).astype(BF16)


def attend(at, nz, q, bias, qcode, kcode, kv_pieces):
    count, width = q.shape
    heads = width // HD
    keys = kcode.shape[0]
    return local_kernel(
        functools.partial(attend_kernel, len(kv_pieces), heads, nz),
        "attend",
        (
            shape((count, width), F32),
            shape((8, count), F32),
            shape((count, width)),
            shape((nz, 2, count // (2 * nz), width)),
        ),
        (at, q, bias, qcode, kcode, *kv_pieces),
        scratch=[
            pltpu.VMEM((heads, keys, 2 * HD), BF16),
            pltpu.VMEM((width, keys), BF16),
            pltpu.VMEM((heads, count, 2 * HD), BF16),
            pltpu.VMEM((width, count), F32),
            pltpu.VMEM((2, 8, count), F32),
        ],
    )


def attend_back_kernel(
    nx, heads, nz, at_ref, q_ref, qcode_ref, kcode_ref, got_ref, full_ref, lse_ref, *refs
):
    pieces = 2 * nx
    kv_refs = refs[:pieces]
    dq_ref, dkv_refs = refs[pieces], refs[pieces + 1 : pieces + 1 + nx]
    kaug, kturn, vals, qaug, qmask, domask, acc, dout, delta = refs[pieces + 1 + nx :]
    width = heads * HD
    count = q_ref.shape[0]
    rows = count // (2 * nz)
    steps = kv_refs[0].shape[0] // STEP
    z = at_ref[0]
    for r in range(2):
        for k in range(nz):
            span = slice((r * nz + k) * rows, (r * nz + k + 1) * rows)
            dout[span, :] = got_ref[turned(z - k, nz), r]
    product = dout[...].astype(F32) * full_ref[...]
    head_rows = lax.broadcasted_iota(jnp.int32, (8, width), 0)
    head_lanes = lax.broadcasted_iota(jnp.int32, (8, width), 1) // HD
    delta[...] = lax.dot_general(
        (head_rows == head_lanes).astype(F32),
        product,
        NT,
        precision=lax.Precision.HIGHEST,
        preferred_element_type=F32,
    )
    for n in range(pieces * steps):
        block = kv_refs[n // steps]
        span_in = pl.ds((n % steps) * STEP, STEP)
        span = pl.ds(n * STEP, STEP)
        code = kcode_ref[span, :]
        for p in range(heads // 2):
            keys = block[span_in, pair_lanes(p)]
            for h in (2 * p, 2 * p + 1):
                kaug[h, span, :] = jnp.where(lane_in_head(keys.shape, h), keys, code)
        kturn[:, n * STEP : (n + 1) * STEP] = jnp.transpose(block[span_in, :width])
        vals[span, :] = block[span_in, width:]
    for p in range(heads // 2):
        part = q_ref[:, pair_lanes(p)]
        dpart = dout[:, pair_lanes(p)]
        for h in (2 * p, 2 * p + 1):
            inside = lane_in_head(part.shape, h)
            qaug[h] = jnp.where(inside, part, qcode_ref[...])
            qmask[h] = jnp.where(inside, part, jnp.zeros_like(part))
            domask[h] = jnp.where(inside, dpart, jnp.zeros_like(dpart))
    total = [None] * heads
    for n in range(kaug.shape[1] // BACK):
        part = slice(n * BACK, (n + 1) * BACK)
        for p in range(heads // 2):
            dkey = dval = None
            for h in (2 * p, 2 * p + 1):
                scores = dot(kaug[h, part, :], qaug[h], NT)
                prob = jnp.exp(scores - lse_ref[h : h + 1, :])
                dprob = dot(vals[part, pair_lanes(p)], domask[h], NT)
                dscore = (prob * (dprob - delta[h : h + 1, :])).astype(BF16)
                add_val = dot(prob.astype(BF16), domask[h])
                add_key = dot(dscore, qmask[h])
                dval = add_val if dval is None else dval + add_val
                dkey = add_key if dkey is None else dkey + add_key
                add = dot(kturn[h * HD : (h + 1) * HD, part], dscore)
                total[h] = add if total[h] is None else total[h] + add
            each = dkv_refs[0].shape[0]
            size = min(BACK, each)
            for m in range(BACK // size):
                at_row = n * BACK + m * size
                rows_out = slice(at_row % each, at_row % each + size)
                rows_in = slice(m * size, (m + 1) * size)
                dkv_refs[at_row // each][rows_out, pair_lanes(p)] = dkey[rows_in].astype(BF16)
                lanes_out = slice(width + p * 2 * HD, width + (p + 1) * 2 * HD)
                dkv_refs[at_row // each][rows_out, lanes_out] = dval[rows_in].astype(BF16)
    for h in range(heads):
        acc[h * HD : (h + 1) * HD, :] = total[h]
    dq_ref[...] = (jnp.transpose(acc[...]) * (HD ** (-0.5))).astype(BF16)


def attend_back(at, nz, q, qcode, kcode, got, full, lse, kv_pieces):
    count, width = q.shape
    heads = width // HD
    keys = kcode.shape[0]
    nx = len(kv_pieces) // 2
    return local_kernel(
        functools.partial(attend_back_kernel, nx, heads, nz),
        "attend_back",
        (shape((count, width)),) + (shape((2 * count, 2 * width)),) * nx,
        (at, q, qcode, kcode, got, full, lse, *kv_pieces),
        scratch=[
            pltpu.VMEM((heads, keys, 2 * HD), BF16),
            pltpu.VMEM((width, keys), BF16),
            pltpu.VMEM((keys, width), BF16),
            pltpu.VMEM((heads, count, 2 * HD), BF16),
            pltpu.VMEM((heads, count, 2 * HD), BF16),
            pltpu.VMEM((heads, count, 2 * HD), BF16),
            pltpu.VMEM((width, count), F32),
            pltpu.VMEM((count, width), BF16),
            pltpu.VMEM((8, count), F32),
        ],
        megabytes=56,
    )


def whole_proj_kernel(nz, nx, part, at_ref, own_ref, far_ref, out_ref):
    z, x, c, y = at_ref[0], at_ref[1], at_ref[2], at_ref[3]
    half = out_ref.shape[1] // 2
    for p, ref in enumerate((own_ref, far_ref)):
        parity = c if p == 0 else 1 - c
        for w in range(2):
            column = pl.multiple_of(turned(y - w, 2) * half, half)
            for j in range(nx):
                for k in range(nz):
                    row = ((turned(z - k, nz) * nx + turned(x - j, nx)) * 2 + parity) * part
                    out_ref[pl.ds(pl.multiple_of(row, part), part), pl.ds(column, half)] = ref[w, j, k]


def whole_proj(at, own, far):
    _, nx, nz, part, half = own.shape
    return local_kernel(
        functools.partial(whole_proj_kernel, nz, nx, part),
        "whole_proj",
        shape((2 * nx * nz * part, 2 * half)),
        (at, own, far),
    )


def project_kernel(at_ref, got_ref, far_ref, weight_ref, first_ref, vec_ref, *refs):
    attn_ref, unit_ref, scale_ref, normed_ref, middle_ref = refs
    nz, _, _, local = got_ref.shape
    c = at_ref[2]
    for block in range(2):
        base = (c if block == 0 else 1 - c) * nz
        for z in range(nz):
            lane = pl.multiple_of((base + z) * local, local)
            attn_ref[:, pl.ds(lane, local)] = got_ref[z, 0] if block == 0 else far_ref[z]
    middle = first_ref[...] + (dot(attn_ref[...], weight_ref[...], NT) + vec_ref[4:5, :])
    middle_ref[...] = middle
    unit, scale = normalize(middle)
    unit_ref[...] = unit
    scale_ref[...] = scale
    normed_ref[...] = (unit * vec_ref[5:6, :] + vec_ref[6:7, :]).astype(BF16)


def project(at, got, far, weight, first, vecs):
    rows, width = first.shape
    return local_kernel(
        project_kernel,
        "project",
        (
            shape((rows, width)),
            shape((rows, width), F32),
            shape((rows, 1), F32),
            shape((rows, width)),
            shape((rows, width), F32),
        ),
        (at, got, far, weight, first, vecs),
    )


def feed_kernel(bias_ref, own_ref, near_ref, far_ref, gz_ref, weight, *refs):
    normed_ref, act_ref, gh_ref, sum_ref, keep_n_ref, send_n_ref, keep_o_ref, send_o_ref = refs
    rows = own_ref.shape[0]
    hidden_size = act_ref.shape[1]
    normed_ref[:rows, :] = own_ref[...]
    normed_ref[rows : 2 * rows, :] = near_ref[...]
    normed_ref[2 * rows :, :] = far_ref[...]
    step = 1024
    for n in range(hidden_size // step):
        up = slice(n * step, (n + 1) * step)
        down = slice(hidden_size + n * step, hidden_size + (n + 1) * step)
        value = dot(normed_ref[...], weight[:, up]) + bias_ref[:, up]
        cdf = 0.5 * (1.0 + lax.erf(value * (0.5**0.5)))
        act = (value * cdf).astype(BF16)
        slope = cdf + value * (jnp.exp(-0.5 * value * value) * ((0.5 / jnp.pi) ** 0.5))
        low = (dot(gz_ref[...], weight[:, down]) * slope).astype(BF16)
        act_ref[:, up] = act
        gh_ref[:, up] = low
        sum_ref[:, up] = jnp.sum(low.astype(F32), axis=0, keepdims=True)
        add_back = dot(low, weight[:, up], NT)
        add_out = dot(act, weight[:, down], NT)
        back = add_back if n == 0 else back + add_back
        out = add_out if n == 0 else out + add_out
    keep_n_ref[...] = back[: 2 * rows]
    send_n_ref[...] = back[2 * rows :].astype(BF16)
    keep_o_ref[...] = out[: 2 * rows]
    send_o_ref[...] = out[2 * rows :].astype(BF16)


def feed(bias, own, near, far, gz, weight):
    count, width = gz.shape
    hidden_size = bias.shape[1]
    half = count // 2
    return local_kernel(
        feed_kernel,
        "feed",
        (
            shape((count, width)),
            shape((count, hidden_size)),
            shape((count, hidden_size)),
            shape((1, hidden_size), F32),
            shape((half, width), F32),
            shape((half, width)),
            shape((half, width), F32),
            shape((half, width)),
        ),
        (bias, own, near, far, gz, weight),
        scalars=0,
        megabytes=56,
    )


def outer_kernel(part, at_ref, normed_ref, gh_ref, gz_ref, act_ref, keep_ref, send_ref, made):
    hidden_size = gh_ref.shape[1]
    chips = keep_ref.shape[0] // part
    step = 512
    for base, left_ref, right_ref in ((0, normed_ref, gh_ref), (hidden_size, gz_ref, act_ref)):
        for n in range(hidden_size // step):
            made[...] = dot(left_ref[...], right_ref[:, n * step : (n + 1) * step], TN)
            lanes = slice(base + n * step, base + (n + 1) * step)
            for p in range(2):

                def store(ref, p=p, lanes=lanes):
                    for i in range(chips):
                        block = made[(2 * i + p) * part : (2 * i + p + 1) * part, :]
                        ref[i * part : (i + 1) * part, lanes] = block.astype(BF16)

                pl.when(at_ref[2] == p)(functools.partial(store, keep_ref))
                pl.when(at_ref[2] != p)(functools.partial(store, send_ref))


def outer(at, part, normed, gh, gz, act):
    width = normed.shape[1]
    out = shape((width // 2, 2 * gh.shape[1]))
    return local_kernel(
        functools.partial(outer_kernel, part),
        "outer",
        (out, out),
        (at, normed, gh, gz, act),
        scratch=[pltpu.VMEM((width, 512), F32)],
    )


def branch_kernel(at_ref, half_ref, near_ref, unit_ref, scale_ref, vec_ref, gz_ref, weight_ref, *refs):
    middle_ref, branch_ref, mine_ref, send_ref, sum_ref = refs
    rows = half_ref.shape[0] // 2
    nz, _, local = mine_ref.shape
    c = at_ref[2]
    grad = half_ref[:rows, :] + near_ref[...].astype(F32)
    top = gz_ref[...].astype(F32)
    unit = unit_ref[...]
    middle = top + norm_back(unit, scale_ref[...], vec_ref[5:6, :], grad)
    middle_ref[...] = middle
    low = middle.astype(BF16)
    branch_ref[...] = low
    made = dot(low, weight_ref[...]).astype(BF16)
    for h in range(2):
        for z in range(nz):
            block = made[:, (h * nz + z) * local : (h * nz + z + 1) * local]

            @pl.when(c == h)
            def _():
                mine_ref[z] = block

            @pl.when(c != h)
            def _():
                send_ref[z] = block

    sum_ref[...] = jnp.concatenate(
        [
            jnp.sum(low.astype(F32), axis=0, keepdims=True),
            jnp.sum(grad * unit, axis=0, keepdims=True),
            jnp.sum(grad, axis=0, keepdims=True),
            jnp.sum(top, axis=0, keepdims=True),
        ],
        axis=0,
    )


def branch(at, nz, half, near, unit, scale, vecs, gz, weight, before):
    rows, width = unit.shape
    local = width // (2 * nz)
    return local_kernel(
        branch_kernel,
        "branch",
        (
            shape((rows, width), F32),
            shape((rows, width)),
            shape((nz, rows, local)),
            shape((nz, rows, local)),
            shape((4, width), F32),
        ),
        (at, half, near, unit, scale, vecs, gz, weight),
        before=before,
    )


def leave_kernel(dq_ref, two_ref, near_ref, weight_ref, stack_ref, full_ref, send_ref):
    count, local = dq_ref.shape
    stack_ref[:, :local] = dq_ref[...]
    stack_ref[:, local:] = (two_ref[:count, :] + near_ref[...].astype(F32)).astype(BF16)
    full_ref[...] = dot(stack_ref[...], weight_ref[...], NT)
    send_ref[...] = full_ref[count // 2 :, :].astype(BF16)


def leave(dq, two, near, weight):
    count, local = dq.shape
    width = weight.shape[0]
    return local_kernel(
        leave_kernel,
        "leave",
        (shape((count, 3 * local)), shape((count, width), F32), shape((count // 2, width))),
        (dq, two, near, weight),
        scalars=0,
    )


def close_kernel(rows, full_ref, unit_ref, scale_ref, lead_ref, vec_ref, middle_ref, normed_ref, stack_ref, *refs):
    sum_ref, bias_ref, out_ref = refs
    count, width = full_ref.shape
    lead_row = jnp.zeros((4, width), F32)
    for n in range(count // rows):
        span = slice(n * rows, (n + 1) * rows)
        grad = full_ref[span, :]
        unit = unit_ref[span, :].astype(F32)
        back = norm_back(unit, scale_ref[span, :], vec_ref[2:3, :], grad)
        if n == 0:
            back = back + middle_ref[...]
        lead_row = lead_row + jnp.concatenate(
            [
                jnp.sum(back * lead_ref[span, :], axis=0, keepdims=True),
                jnp.sum(back, axis=0, keepdims=True),
                jnp.sum(grad * unit, axis=0, keepdims=True),
                jnp.sum(grad, axis=0, keepdims=True),
            ],
            axis=0,
        )
    sum_ref[...] = lead_row
    bias_ref[...] = jnp.sum(stack_ref[...].astype(F32), axis=0, keepdims=True)
    out_ref[...] = dot(normed_ref[...], stack_ref[...], TN).astype(BF16)


def close(rows, full, unit, scale, lead, vecs, middle, normed, stack, before):
    width = full.shape[1]
    return local_kernel(
        functools.partial(close_kernel, rows),
        "close",
        (shape((4, width), F32), shape((1, stack.shape[1]), F32), shape((width, stack.shape[1]))),
        (full, unit, scale, lead, vecs, middle, normed, stack),
        scalars=0,
        before=before,
    )


def after(block, *before):
    return lax.optimization_barrier((block,) + before)[0]


def per_device(
    tokens,
    segment_ids,
    lead_hours,
    qkv_weight,
    qv_bias,
    proj_weight,
    proj_bias,
    up_weight,
    up_bias,
    down_weight,
    down_bias,
    norm1_gain,
    norm1_bias,
    norm2_gain,
    norm2_bias,
    lead_weight,
    lead_bias,
    out_grad,
):
    grid = Grid()
    nz, nx, chips, sp = grid.nz, grid.nx, grid.chips, grid.sp
    core, y = grid.core, grid.y
    at = jnp.stack([grid.z, grid.x, core, y]).astype(jnp.int32)
    full_rows, width = tokens.shape
    rows = full_rows // 2
    part = norm1_gain.shape[0]
    each = HD // sp
    at_home = core == y

    def split(array, axis, index):
        half = array.shape[axis] // 2
        first = lax.slice_in_dim(array, 0, half, axis=axis)
        second = lax.slice_in_dim(array, half, 2 * half, axis=axis)
        return jnp.where(index == 0, first, second), jnp.where(index == 0, second, first)

    def in_order(own, other, index):
        return jnp.where(index == 0, own, other), jnp.where(index == 0, other, own)

    shard = jnp.transpose(qkv_weight.reshape(3, part, nz, -1), (2, 1, 0, 3)).reshape(nz, part, -1)
    wq_z = [pick(shard, grid.z, 0)] + [grid.zshift(pick(shard, grid.far_z(k), 0), k) for k in range(1, nz)]

    vectors = [lead_weight, lead_bias, norm1_gain, norm1_bias, proj_bias, norm2_gain, norm2_bias, down_bias]
    n_vec = len(vectors)
    n_qv, n_up = qv_bias.size // part, up_bias.size // part
    pack = jnp.concatenate(
        [
            jnp.stack(vectors),
            qv_bias.reshape(-1, part),
            up_bias.reshape(-1, part),
            segment_ids.astype(BF16).reshape(-1, part),
        ],
        axis=0,
    )
    pack_rows = pack.shape[0]
    tall = -(-pack_rows // 16) * 16
    pack = jnp.pad(pack, ((0, rows - pack_rows), (63, 128 - 64 - part)))
    own_segments = split(segment_ids, 0, y)[0]
    beside = jnp.concatenate([own_segments.astype(BF16)[:, None], pack], axis=1)
    own_tokens = jnp.concatenate([split(tokens, 0, y)[0], beside], axis=1)
    token_far = [grid.zshift(own_tokens, k) for k in range(1, nz)]
    token_z = jnp.stack([own_tokens] + token_far)
    token_c = grid.cswap(token_z)
    packs_own = jnp.stack([token_z[:, :tall, width:], token_c[:, :tall, width:]])
    packs_far = [grid.xshift(packs_own, j) for j in range(1, nx)]

    wq_z = jnp.stack(wq_z)
    wq_x = jnp.stack([wq_z] + [grid.xshift(wq_z, j) for j in range(1, nx)])
    wq_spin, wq_cross = grid.spin(wq_x), grid.cross(wq_x)
    wq_same = jnp.where(at_home, wq_x, wq_spin)
    wq_other = jnp.where(at_home, wq_spin, wq_cross)

    normed_one, unit_one, scale_one, lead, embedded, vecs, w_qkv, q_raw, kv = enter(
        at, lead_hours, [own_tokens] + token_far + [token_c], packs_far, wq_same, wq_other, n_vec, part
    )
    local = q_raw.shape[1]
    kv_far = grid.yswap(kv)
    kv_pieces = [kv, kv_far]
    for j in range(1, nx):
        kv_pieces += [grid.xshift(kv, j), grid.xshift(kv_far, j)]

    table = jnp.stack([packs_own] + packs_far)[:, :, :, n_vec:pack_rows, 64 : 64 + part].reshape(sp, -1)
    n = jnp.arange(sp)
    rel_j, rel_r, rel_k = n // (2 * nz), (n // nz) % 2, n % nz
    device = (grid.far_z(-rel_k) * nx + grid.far_x(-rel_j)) * 2 + (core + rel_r) % 2
    in_place = (jnp.arange(sp)[:, None] == device[None, :]).astype(BF16)
    table = dot(in_place, table).reshape(sp, -1, part)
    heads_local = qv_bias.shape[1]
    qv_all = jnp.transpose(table[:, :n_qv].reshape(sp, 2, heads_local, -1), (1, 2, 0, 3)).reshape(2, heads_local * HD)
    qv_far = grid.yswap(qv_all)
    qv_full = pick(jnp.where(at_home, qv_all, qv_far).reshape(2, nz, -1), grid.z, 1)
    seg_rows = table[:, n_qv + n_up :].reshape(sp * 2, rows)
    n = jnp.arange(nx * 2 * 2 * nz)
    k, r, w, j = n % nz, (n // nz) % 2, (n // (2 * nz)) % 2, n // (4 * nz)
    key_at = ((grid.far_z(-k) * nx + grid.far_x(-j)) * 2 + (core + r) % 2) * 2 + (y + w) % 2
    take = (key_at[:, None] == jnp.arange(2 * sp)[None, :]).astype(BF16)
    key_seg = dot(take, seg_rows.astype(BF16)).astype(jnp.int32).reshape(-1)
    query_seg = key_seg[: 2 * nz * rows]
    lanes = jnp.arange(2 * HD, dtype=jnp.int32) % HD
    kcode = jnp.where(key_seg[:, None] == lanes[None, :], 0.0, EXCLUDED).astype(BF16)
    qcode = (query_seg[:, None] == lanes[None, :]).astype(BF16)
    up_all = jnp.transpose(table[:, n_qv : n_qv + n_up].reshape(sp, up_bias.shape[0], -1), (1, 0, 2)).reshape(1, -1)
    up_full = split(up_all, 1, core)[0]

    up_shard, down_shard, _ = lax.optimization_barrier((up_weight, down_weight, wq_z))
    up_keep, up_send = split(up_shard, 1, core)
    down_keep, down_send = split(jnp.transpose(down_shard), 1, core)
    ff_far = grid.cswap(jnp.concatenate([up_send, down_send], axis=1))
    ff = jnp.concatenate(in_order(jnp.concatenate([up_keep, down_keep], axis=1), ff_far, core), axis=0)
    w_ff = lax.all_gather(after(ff, *token_far), ("z", "x"), axis=0, tiled=True)

    gz_own, gz_far = split(after(out_grad, kv), 0, y)
    gz_two = jnp.concatenate([gz_own, gz_far], axis=0)
    gz = jnp.concatenate([gz_two, grid.cswap(gz_two)], axis=0)

    wp = jnp.transpose(after(proj_weight, wq_spin, token_c))
    wp_z = jnp.stack([wp] + [grid.zshift(wp, k) for k in range(1, nz)])
    wp_z = after(wp_z, kv)
    wp_x = jnp.stack([wp_z] + [grid.xshift(wp_z, j) for j in range(1, nx)])
    wp_x = after(wp_x, kv_far)
    wp_own = jnp.stack([wp_x, grid.yswap(wp_x)])
    w_proj = whole_proj(at, wp_own, grid.cswap(wp_own))

    q_raw, up_full, gz = lax.optimization_barrier((q_raw, up_full, gz))
    attn_full, lse, q, attn_send = attend(at, nz, q_raw, qv_full, qcode, kcode, kv_pieces)
    attn_got = lax.all_to_all(attn_send, "z", 0, 0, tiled=True)
    attn_far = grid.cswap(attn_got[:, 1])
    attn_out, n2, s2, normed, middle = project(at, attn_got, attn_far, w_proj, embedded, vecs)
    near = grid.yswap(normed)
    far = grid.cswap(jnp.concatenate([normed, near], axis=0))
    normed_two, active, grad_hidden, up_sum, keep_n, send_n, keep_o, send_o = feed(up_full, normed, near, far, gz, w_ff)

    half_n = keep_n + grid.cswap(send_n).astype(F32)
    near_n = grid.yswap(half_n[rows:].astype(BF16))
    d_outer, d_send = outer(at, part, normed_two, grad_hidden, gz, active)
    d_both = jnp.concatenate([d_outer, grid.cswap(d_send)], axis=1)
    d_ff = lax.psum_scatter(d_both, ("z", "x"), scatter_dimension=0, tiled=True)
    grad_middle, grad_branch, mine, send, sums_two = branch(
        at, nz, half_n, near_n, n2, s2, vecs, gz[:rows], w_proj, (d_outer,)
    )
    theirs = grid.cswap(send)
    got = lax.all_to_all(jnp.stack([mine, theirs], axis=1), "z", 0, 0, tiled=True)

    back = attend_back(at, nz, q, qcode, kcode, got, attn_full, lse, kv_pieces)
    grad_q, grad_kv = back[0], back[1].astype(F32)
    for j in range(1, nx):
        grad_kv = grad_kv + grid.xshift(back[1 + j], -j).astype(F32)
    count = 2 * nz * rows
    near_kv = grid.yswap(grad_kv[count:].astype(BF16))
    grad_stack, part_full, part_send = leave(grad_q, grad_kv, near_kv, w_qkv)

    part_n1 = (part_full[: nz * rows] + grid.cswap(part_send).astype(F32)).reshape(nz, rows, width)
    low = part_n1.astype(BF16)
    n1_far = [grid.zshift(low[k], -k) for k in range(1, nz)]

    sums_one, stack_sum, d_wqkv = close(
        rows, part_full, unit_one, scale_one, lead, vecs, grad_middle, normed_one, grad_stack, (low,)
    )
    up_column = jnp.transpose(up_sum.reshape(-1, sp, each), (1, 0, 2)).reshape(1, -1)
    sums = jnp.concatenate([sums_one, sums_two, up_column], axis=0)
    sums_far = grid.cswap(sums)
    up_both = jnp.concatenate(in_order(sums[n_vec:], sums_far[n_vec:], core), axis=0)
    sums = jnp.concatenate(
        [sums[:n_vec] + sums_far[:n_vec], jnp.where(y == 0, up_both, 0.0), jnp.where(y == 0, 0.0, up_both)], axis=0
    )
    n_sums = n_vec + 4
    qv_sum = jnp.concatenate([stack_sum[0, :local], stack_sum[0, 2 * local :]]).reshape(-1, sp, each)
    n_bias = qv_sum.shape[0] * each
    qv_column = jnp.pad(jnp.transpose(qv_sum, (1, 0, 2)).reshape(sp, n_bias), ((0, 0), (0, part - n_bias)))
    columns = jnp.concatenate([jnp.transpose(sums), qv_column.reshape(-1, 1)], axis=1).astype(BF16)
    columns = jnp.pad(columns, ((0, 0), (0, 128 - columns.shape[1])))
    dw = jnp.concatenate([d_wqkv, columns], axis=1).reshape(nz, nx, 2, part, -1)
    dw_same, dw_other = pick(dw, core, 2), pick(dw, 1 - core, 2)
    from_spin = grid.spin(jnp.where(at_home, dw_other, dw_same), back=True)
    from_cross = grid.cross(dw_other)
    dw = from_spin.astype(F32) + jnp.where(at_home, dw_same, from_cross).astype(F32)
    dw_low = dw.astype(BF16)
    dw = pick(dw, grid.x, 1)
    for j in range(1, nx):
        dw = dw + grid.xshift(pick(dw_low, grid.far_x(j), 1), j).astype(F32)
    dw = lax.all_to_all(dw.astype(BF16), "z", 0, 0, tiled=True)
    g_qkv = place_qkv([dw[k] for k in range(nz)], [jnp.int32(k * local) for k in range(nz)], local)
    tails = dw[:, :, 3 * local :].astype(F32)
    sums = jnp.transpose(jnp.sum(tails[:, :, :n_sums], axis=0))
    up_rows = jnp.where(y == 0, sums[n_vec : n_vec + 2], sums[n_vec + 2 : n_vec + 4])
    g_up_bias = up_rows.reshape(-1, each)
    qv_tail = tails[:, :n_bias, n_sums].reshape(nz, 2, -1, each)
    g_qv_bias = jnp.transpose(qv_tail, (1, 0, 2, 3)).reshape(2, -1, each)

    grad_n1 = part_n1[0]
    for block in n1_far:
        grad_n1 = grad_n1 + block.astype(F32)
    input_grad = grad_middle + norm_back(unit_one[:rows].astype(F32), scale_one[:rows], vecs[2], grad_n1)
    input_grad = input_grad.astype(BF16)
    input_grad = jnp.concatenate(in_order(input_grad, grid.yswap(input_grad), y), axis=0).astype(F32)

    half_o = keep_o + grid.cswap(after(send_o, grad_branch)).astype(F32)
    block_out = half_o[:rows] + grid.yswap(half_o[rows:].astype(BF16)).astype(F32)
    block_out = (middle + (block_out + vecs[7])).astype(BF16)
    block_out = jnp.concatenate(in_order(block_out, grid.yswap(block_out), y), axis=0)
    dp = dot(grad_branch, after(attn_out, got), TN).astype(BF16).reshape(chips, 2, part, -1)
    dp = pick(dp, core, 1).astype(F32) + grid.cswap(pick(dp, 1 - core, 1)).astype(F32)
    dp_keep, dp_send = split(dp, 2, y)
    dp = dp_keep + grid.yswap(dp_send.astype(BF16)).astype(F32)
    d_proj = grid.scatter(dp.astype(BF16).reshape(nz, nx, part, -1))

    n_cols = 2 * grad_hidden.shape[1]
    low_cols, high_cols = in_order(d_ff[:, :n_cols], d_ff[:, n_cols:], core)
    n_hidden = grad_hidden.shape[1]
    d_up = jnp.concatenate([low_cols[:, :n_hidden], high_cols[:, :n_hidden]], axis=1).astype(F32)
    d_down = jnp.concatenate([low_cols[:, n_hidden:], high_cols[:, n_hidden:]], axis=1).astype(F32)
    return (
        block_out,
        input_grad,
        g_qkv,
        g_qv_bias,
        jnp.transpose(d_proj),
        sums[4],
        d_up,
        g_up_bias,
        jnp.transpose(d_down),
        sums[7],
        sums[2],
        sums[3],
        sums[5],
        sums[6],
        sums[0],
        sums[1],
    )


def solution(mesh):
    sp = mesh.shape["sp"]
    nz = 4
    devices = mesh.devices.reshape(nz, sp // (2 * nz), 2, mesh.shape["tp"])
    fine = jax.sharding.Mesh(devices, SP + ("tp",))
    line = P(SP)
    placed = (
        P(SP, None),
        line,
        P(),
        P(None, SP, "tp"),
        P(None, "tp", SP),
        P("tp", SP),
        line,
        P(SP, "tp"),
        P("tp", SP),
        P("tp", SP),
    ) + (line,) * 7 + (P(SP, None),)
    given = (
        P(SP, None),
        P(SP, None),
        P(None, SP, "tp"),
        P(None, "tp", SP),
        P("tp", SP),
        line,
        P(SP, "tp"),
        P("tp", SP),
        P("tp", SP),
    ) + (line,) * 7
    return jax.shard_map(per_device, mesh=fine, in_specs=placed, out_specs=given, check_vma=False)
```

```python
import functools

import jax
import jax.numpy as jnp
from jax import lax
from jax.experimental import pallas as pl
from jax.experimental.pallas import tpu as pltpu
from jax.sharding import PartitionSpec as P

HD = 64
EPSILON = 1e-05
EXCLUDED = -1e30
F32 = jnp.float32
BF16 = jnp.bfloat16
NN = (((1,), (0,)), ((), ()))
NT = (((1,), (1,)), ((), ()))
TN = (((0,), (0,)), ((), ()))


def dot(left, right, dims=NN):
    return lax.dot_general(left, right, dims, preferred_element_type=F32)


SP = ("z", "x", "core")


class Grid:
    def __init__(self):
        self.nz = lax.axis_size("z")
        self.nx = lax.axis_size("x")
        self.chips = self.nz * self.nx
        self.sp = 2 * self.chips
        me = lax.axis_index(SP)
        self.me = me
        self.core = me % 2
        self.x = (me // 2) % self.nx
        self.z = me // (2 * self.nx)
        self.y = lax.axis_index("tp")

    def _move(self, block, dz, dx, flip):
        pairs = []
        for i in range(self.sp):
            z, x, c = i // (2 * self.nx), (i // 2) % self.nx, i % 2
            to = (((z + dz) % self.nz) * self.nx + (x + dx) % self.nx) * 2 + (1 - c if flip else c)
            pairs.append((i, to))
        return lax.ppermute(block, SP, pairs)

    def zshift(self, block, k):
        return self._move(block, k, 0, False)

    def xshift(self, block, k):
        return self._move(block, 0, k, False)

    def cswap(self, block):
        return self._move(block, 0, 0, True)

    def yswap(self, block):
        return lax.ppermute(block, "tp", [(0, 1), (1, 0)])

    def _pairs(self, route):
        pairs = []
        for chip in range(self.chips):
            for (c, y), (to_c, to_y) in route:
                pairs.append(((chip * 2 + c) * 2 + y, (chip * 2 + to_c) * 2 + to_y))
        return pairs

    def spin(self, block, back=False):
        route = []
        for b in (0, 1):
            route += [((b, b), (b, 1 - b)), ((1 - b, b), (b, b))]
        if back:
            route = [(to, at) for at, to in route]
        return lax.ppermute(block, SP + ("tp",), self._pairs(route))

    def cross(self, block):
        route = [((1 - b, b), (b, 1 - b)) for b in (0, 1)]
        return lax.ppermute(block, SP + ("tp",), self._pairs(route))

    def far_z(self, k):
        return (self.z + k) % self.nz

    def far_x(self, j):
        return (self.x + j) % self.nx

    def gather(self, block):
        columns = [block] + [self.zshift(block, k) for k in range(1, self.nz)]
        return [p for b in columns for p in [b] + [self.xshift(b, j) for j in range(1, self.nx)]]

    def chip_order(self):
        order = jnp.arange(self.chips)
        return self.far_z(-(order // self.nx)) * self.nx + self.far_x(-(order % self.nx))

    def scatter(self, pieces):
        total = pick(pieces, self.x, 1).astype(F32)
        for j in range(1, self.nx):
            total = total + self.xshift(pick(pieces, self.far_x(j), 1), j).astype(F32)
        low = total.astype(pieces.dtype)
        mine = pick(total, self.z, 0)
        for k in range(1, self.nz):
            mine = mine + self.zshift(pick(low, self.far_z(k), 0), k).astype(F32)
        return mine


def pick(array, index, axis):
    return lax.dynamic_index_in_dim(array, index, axis, keepdims=False)


def normalize(values):
    center = values - jnp.mean(values, axis=-1, keepdims=True)
    spread = jnp.mean(center * center, axis=-1, keepdims=True)
    scale = lax.rsqrt(spread + EPSILON)
    return center * scale, scale


def norm_back(normed, scale, gain, grad):
    scaled = grad * gain
    mean_one = jnp.mean(scaled, axis=-1, keepdims=True)
    mean_two = jnp.mean(scaled * normed, axis=-1, keepdims=True)
    return (scaled - mean_one - normed * mean_two) * scale


def place_qkv_kernel(starts_ref, *refs):
    pieces, out_ref = refs[:-1], refs[-1]
    for i, piece in enumerate(pieces):
        size = out_ref.shape[2] // len(pieces)
        span = pl.ds(pl.multiple_of(starts_ref[i], size), size)
        for c in range(3):
            out_ref[c, :, span] = piece[:, c * size : (c + 1) * size].astype(F32)


def place_qkv(pieces, starts, columns):
    rows = pieces[0].shape[0]
    vmem = pl.BlockSpec(memory_space=pltpu.VMEM)
    return pl.pallas_call(
        place_qkv_kernel,
        out_shape=jax.ShapeDtypeStruct((3, rows, columns * len(pieces)), F32),
        in_specs=[pl.BlockSpec(memory_space=pltpu.SMEM)] + [vmem] * len(pieces),
        out_specs=vmem,
        name="place_qkv",
    )(jnp.stack(starts).astype(jnp.int32), *pieces)


def lane_in_head(shape, head):
    lanes = lax.broadcasted_iota(jnp.int32, shape, 1)
    return (lanes // HD) == (head % 2)


def pair_lanes(pair):
    return slice(pair * 2 * HD, (pair + 1) * 2 * HD)


STEP = 384
WIDE = 1536
BACK = 768
SMEM = pl.BlockSpec(memory_space=pltpu.SMEM)


def in_vmem(count):
    return [pl.BlockSpec(memory_space=pltpu.VMEM)] * count


COSTS = {"enter": 5, "attend": 14, "attend_back": 17, "whole_proj": 1, "project": 2, "branch": 2, "leave": 3, "close": 5, "outer": 5}


def local_kernel(kernel, name, out_shape, operands, scalars=1, scratch=(), flops=0, megabytes=48, before=()):
    if before:
        inner, at_end = kernel, len(operands)

        def kernel(*refs):
            inner(*refs[:at_end], *refs[at_end + len(before) :])

    single = not isinstance(out_shape, tuple)
    return pl.pallas_call(
        kernel,
        out_shape=out_shape,
        in_specs=[SMEM] * scalars + in_vmem(len(operands) - scalars) + [ANY] * len(before),
        out_specs=in_vmem(1)[0] if single else tuple(in_vmem(len(out_shape))),
        scratch_shapes=list(scratch),
        compiler_params=pltpu.CompilerParams(vmem_limit_bytes=megabytes * 1024 * 1024),
        cost_estimate=pl.CostEstimate(flops=COSTS.get(name, 0) * 1000000000, bytes_accessed=1 << 16, transcendentals=0),
        name=name,
    )(*operands, *before)


def turn_kernel(in_ref, out_ref):
    out_ref[...] = jnp.transpose(in_ref[...])


def turn(block, *before):
    return local_kernel(turn_kernel, "turn", shape(block.shape[::-1]), (block,), scalars=0, before=before)


def shape(dims, kind=BF16):
    return jax.ShapeDtypeStruct(tuple(dims), kind)


ANY = pl.BlockSpec(memory_space=pl.ANY)


def gate(block, *before):
    return pl.pallas_call(
        lambda *refs: None,
        out_shape=jax.ShapeDtypeStruct(block.shape, block.dtype),
        in_specs=[ANY] * (1 + len(before)),
        out_specs=ANY,
        input_output_aliases={0: 0},
        cost_estimate=pl.CostEstimate(flops=0, bytes_accessed=0, transcendentals=0),
        name="gate",
    )(block, *before)


def stack_kernel(count, *refs):
    for n in range(count):
        refs[-1][n] = refs[n][...]


def stack(blocks, *before):
    first = blocks[0]
    return pl.pallas_call(
        functools.partial(stack_kernel, len(blocks)),
        out_shape=jax.ShapeDtypeStruct((len(blocks),) + first.shape, first.dtype),
        in_specs=in_vmem(len(blocks)) + [ANY] * len(before),
        out_specs=in_vmem(1)[0],
        cost_estimate=pl.CostEstimate(flops=0, bytes_accessed=1 << 16, transcendentals=0),
        name="stack",
    )(*blocks, *before)


def turned(index, size):
    return lax.rem(index + size, size)


def enter_kernel(nz, nx, n_vec, part, at_ref, hour_ref, *refs):
    token_refs, refs = refs[: nz + 1], refs[nz + 1 :]
    pack_refs, refs = refs[: nx - 1], refs[nx - 1 :]
    weight_refs, refs = refs[:2], refs[2:]
    normed_ref, unit_ref, scale_ref, lead_ref, first_ref, vec_ref, weight_ref, q_ref, kv_ref = refs[:9]
    packs = refs[9]
    z, x, c = at_ref[0], at_ref[1], at_ref[2]
    rows, width = first_ref.shape
    tall = packs.shape[3]
    local = q_ref.shape[1]
    aux = slice(width, width + 128)
    for k in range(nz):
        packs[0, 0, k] = token_refs[k][:tall, aux]
        packs[0, 1, k] = token_refs[nz][k, :tall, aux]
    for j in range(1, nx):
        packs[j] = pack_refs[j - 1][...]
    for dev in range(2 * nz * nx):
        dev_z, dev_x, dev_c = dev // (2 * nx), (dev // 2) % nx, dev % 2
        block = packs[turned(x - dev_x, nx), turned(c - dev_c, 2), turned(z - dev_z, nz)]
        vec_ref[:, dev * part : (dev + 1) * part] = block[:n_vec, 64 : 64 + part].astype(F32)
    for n in range(2 * nz):
        ref = token_refs[n] if n < nz else token_refs[nz].at[n - nz]
        span = slice(n * rows, (n + 1) * rows)
        segment = ref[:, aux][:, :1].astype(F32)
        lead = jnp.zeros_like(segment)
        for i in range(hour_ref.shape[0]):
            lead = jnp.where(segment == float(i), hour_ref[i], lead)
        lead_ref[span, :] = lead
        value = ref[:, :width].astype(F32) + lead * vec_ref[0:1, :] + vec_ref[1:2, :]
        if n == 0:
            first_ref[...] = value
        unit, scale = normalize(value)
        scale_ref[span, :] = scale
        unit_ref[span, :] = unit.astype(BF16)
        normed_ref[span, :] = (unit * vec_ref[2:3, :] + vec_ref[3:4, :]).astype(BF16)
    for p, ref in enumerate(weight_refs):
        parity = c if p == 0 else 1 - c
        for j in range(nx):
            for k in range(nz):
                row = ((turned(z - k, nz) * nx + turned(x - j, nx)) * 2 + parity) * part
                weight_ref[pl.ds(pl.multiple_of(row, part), part), :] = ref[j, k]
    made = dot(normed_ref[...], weight_ref[...])
    q_ref[...] = made[:, :local]
    kv_ref[...] = made[:, local:].astype(BF16)


def enter(at, hours, tokens, packs, same, other, n_vec, part):
    nz, nx = len(tokens) - 1, len(packs) + 1
    rows, wide = tokens[0].shape
    width = wide - 128
    count = 2 * nz * rows
    local = same.shape[-1] // 3
    tall = packs[0].shape[2]
    return local_kernel(
        functools.partial(enter_kernel, nz, nx, n_vec, part),
        "enter",
        (
            shape((count, width)),
            shape((count, width)),
            shape((count, 1), F32),
            shape((count, 1), F32),
            shape((rows, width), F32),
            shape((n_vec, width), F32),
            shape((width, 3 * local)),
            shape((count, local), F32),
            shape((count, 2 * local)),
        ),
        (at, hours, *tokens, *packs, same, other),
        scalars=2,
        scratch=[pltpu.VMEM((nx, 2, nz, tall, 128), BF16)],
    )


def attend_kernel(pieces, heads, nz, at_ref, q_ref, bias_ref, qcode_ref, kcode_ref, *refs):
    kv_refs = refs[:pieces]
    out_ref, lse_ref, low_ref, send_ref = refs[pieces : pieces + 4]
    kaug, vturn, qaug, acc, stat = refs[pieces + 4 :]
    width = heads * HD
    count = q_ref.shape[0]
    rows = count // (2 * nz)
    steps = kv_refs[0].shape[0] // STEP
    low_ref[...] = (q_ref[...] + bias_ref[0:1, :]).astype(BF16) * jnp.asarray(HD ** (-0.5), BF16)
    for n in range(pieces * steps):
        block = kv_refs[n // steps]
        span_in = pl.ds((n % steps) * STEP, STEP)
        span = pl.ds(n * STEP, STEP)
        code = kcode_ref[span, :]
        for p in range(heads // 2):
            keys = block[span_in, pair_lanes(p)]
            for h in (2 * p, 2 * p + 1):
                kaug[h, span, :] = jnp.where(lane_in_head(keys.shape, h), keys, code)
        vturn[:, n * STEP : (n + 1) * STEP] = jnp.transpose(block[span_in, width:])
    for p in range(heads // 2):
        part = low_ref[:, pair_lanes(p)]
        for h in (2 * p, 2 * p + 1):
            qaug[h] = jnp.where(lane_in_head(part.shape, h), part, qcode_ref[...])
    stat[...] = jnp.ones_like(stat)
    for h in range(heads):
        span = slice(h * HD, (h + 1) * HD)
        top = total = out = None
        for n in range(kaug.shape[1] // WIDE):
            part = slice(n * WIDE, (n + 1) * WIDE)
            scores = dot(kaug[h, part, :], qaug[h], NT)
            peak = jnp.max(scores, axis=0, keepdims=True)
            new_top = peak if top is None else jnp.maximum(top, peak)
            weight = jnp.exp(scores - new_top)
            add = jnp.sum(weight, axis=0, keepdims=True)
            mixed = dot(vturn[span, part], weight.astype(BF16))
            if top is None:
                total, out = add, mixed
            else:
                rescale = jnp.exp(top - new_top)
                total, out = total * rescale + add, out * rescale + mixed
            top = new_top
        stat[0, h : h + 1, :] = top
        stat[1, h : h + 1, :] = total
        acc[span, :] = out / total
    out_ref[...] = jnp.transpose(acc[...])
    lse_ref[...] = stat[0] + jnp.log(jnp.maximum(stat[1], 1e-37))
    z = at_ref[0]
    for r in range(2):
        for k in range(nz):
            span = slice((r * nz + k) * rows, (r * nz + k + 1) * rows)
            send_ref[turned(z - k, nz), r] = (out_ref[span, :] + bias_ref[1:2, :]).astype(BF16)


def attend(at, nz, q, bias, qcode, kcode, kv_pieces):
    count, width = q.shape
    heads = width // HD
    keys = kcode.shape[0]
    return local_kernel(
        functools.partial(attend_kernel, len(kv_pieces), heads, nz),
        "attend",
        (
            shape((count, width), F32),
            shape((8, count), F32),
            shape((count, width)),
            shape((nz, 2, count // (2 * nz), width)),
        ),
        (at, q, bias, qcode, kcode, *kv_pieces),
        scratch=[
            pltpu.VMEM((heads, keys, 2 * HD), BF16),
            pltpu.VMEM((width, keys), BF16),
            pltpu.VMEM((heads, count, 2 * HD), BF16),
            pltpu.VMEM((width, count), F32),
            pltpu.VMEM((2, 8, count), F32),
        ],
    )


def attend_back_kernel(
    nx, heads, nz, at_ref, q_ref, qcode_ref, kcode_ref, got_ref, full_ref, lse_ref, *refs
):
    pieces = 2 * nx
    kv_refs = refs[:pieces]
    dq_ref, dkv_refs = refs[pieces], refs[pieces + 1 : pieces + 1 + nx]
    kaug, kturn, vals, qaug, qmask, domask, acc, dout, delta = refs[pieces + 1 + nx :]
    width = heads * HD
    count = q_ref.shape[0]
    rows = count // (2 * nz)
    steps = kv_refs[0].shape[0] // STEP
    z = at_ref[0]
    for r in range(2):
        for k in range(nz):
            span = slice((r * nz + k) * rows, (r * nz + k + 1) * rows)
            dout[span, :] = got_ref[turned(z - k, nz), r]
    product = dout[...].astype(F32) * full_ref[...]
    head_rows = lax.broadcasted_iota(jnp.int32, (8, width), 0)
    head_lanes = lax.broadcasted_iota(jnp.int32, (8, width), 1) // HD
    delta[...] = lax.dot_general(
        (head_rows == head_lanes).astype(F32),
        product,
        NT,
        precision=lax.Precision.HIGHEST,
        preferred_element_type=F32,
    )
    for n in range(pieces * steps):
        block = kv_refs[n // steps]
        span_in = pl.ds((n % steps) * STEP, STEP)
        span = pl.ds(n * STEP, STEP)
        code = kcode_ref[span, :]
        for p in range(heads // 2):
            keys = block[span_in, pair_lanes(p)]
            for h in (2 * p, 2 * p + 1):
                kaug[h, span, :] = jnp.where(lane_in_head(keys.shape, h), keys, code)
        kturn[:, n * STEP : (n + 1) * STEP] = jnp.transpose(block[span_in, :width])
        vals[span, :] = block[span_in, width:]
    for p in range(heads // 2):
        part = q_ref[:, pair_lanes(p)]
        dpart = dout[:, pair_lanes(p)]
        for h in (2 * p, 2 * p + 1):
            inside = lane_in_head(part.shape, h)
            qaug[h] = jnp.where(inside, part, qcode_ref[...])
            qmask[h] = jnp.where(inside, part, jnp.zeros_like(part))
            domask[h] = jnp.where(inside, dpart, jnp.zeros_like(dpart))
    total = [None] * heads
    for n in range(kaug.shape[1] // BACK):
        part = slice(n * BACK, (n + 1) * BACK)
        for p in range(heads // 2):
            dkey = dval = None
            for h in (2 * p, 2 * p + 1):
                scores = dot(kaug[h, part, :], qaug[h], NT)
                prob = jnp.exp(scores - lse_ref[h : h + 1, :])
                dprob = dot(vals[part, pair_lanes(p)], domask[h], NT)
                dscore = (prob * (dprob - delta[h : h + 1, :])).astype(BF16)
                add_val = dot(prob.astype(BF16), domask[h])
                add_key = dot(dscore, qmask[h])
                dval = add_val if dval is None else dval + add_val
                dkey = add_key if dkey is None else dkey + add_key
                add = dot(kturn[h * HD : (h + 1) * HD, part], dscore)
                total[h] = add if total[h] is None else total[h] + add
            each = dkv_refs[0].shape[0]
            size = min(BACK, each)
            for m in range(BACK // size):
                at_row = n * BACK + m * size
                rows_out = slice(at_row % each, at_row % each + size)
                rows_in = slice(m * size, (m + 1) * size)
                dkv_refs[at_row // each][rows_out, pair_lanes(p)] = dkey[rows_in].astype(BF16)
                lanes_out = slice(width + p * 2 * HD, width + (p + 1) * 2 * HD)
                dkv_refs[at_row // each][rows_out, lanes_out] = dval[rows_in].astype(BF16)
    for h in range(heads):
        acc[h * HD : (h + 1) * HD, :] = total[h]
    dq_ref[...] = (jnp.transpose(acc[...]) * (HD ** (-0.5))).astype(BF16)


def attend_back(at, nz, q, qcode, kcode, got, full, lse, kv_pieces):
    count, width = q.shape
    heads = width // HD
    keys = kcode.shape[0]
    nx = len(kv_pieces) // 2
    return local_kernel(
        functools.partial(attend_back_kernel, nx, heads, nz),
        "attend_back",
        (shape((count, width)),) + (shape((2 * count, 2 * width)),) * nx,
        (at, q, qcode, kcode, got, full, lse, *kv_pieces),
        scratch=[
            pltpu.VMEM((heads, keys, 2 * HD), BF16),
            pltpu.VMEM((width, keys), BF16),
            pltpu.VMEM((keys, width), BF16),
            pltpu.VMEM((heads, count, 2 * HD), BF16),
            pltpu.VMEM((heads, count, 2 * HD), BF16),
            pltpu.VMEM((heads, count, 2 * HD), BF16),
            pltpu.VMEM((width, count), F32),
            pltpu.VMEM((count, width), BF16),
            pltpu.VMEM((8, count), F32),
        ],
        megabytes=56,
    )


def whole_proj_kernel(nz, nx, part, at_ref, own_ref, far_ref, out_ref):
    z, x, c, y = at_ref[0], at_ref[1], at_ref[2], at_ref[3]
    half = out_ref.shape[1] // 2
    for p, ref in enumerate((own_ref, far_ref)):
        parity = c if p == 0 else 1 - c
        for w in range(2):
            column = pl.multiple_of(turned(y - w, 2) * half, half)
            for j in range(nx):
                for k in range(nz):
                    row = ((turned(z - k, nz) * nx + turned(x - j, nx)) * 2 + parity) * part
                    out_ref[pl.ds(pl.multiple_of(row, part), part), pl.ds(column, half)] = ref[w, j, k]


def whole_proj(at, own, far):
    _, nx, nz, part, half = own.shape
    return local_kernel(
        functools.partial(whole_proj_kernel, nz, nx, part),
        "whole_proj",
        shape((2 * nx * nz * part, 2 * half)),
        (at, own, far),
    )


def project_kernel(at_ref, got_ref, far_ref, weight_ref, first_ref, vec_ref, *refs):
    attn_ref, unit_ref, scale_ref, normed_ref, middle_ref = refs
    nz, _, _, local = got_ref.shape
    c = at_ref[2]
    for block in range(2):
        base = (c if block == 0 else 1 - c) * nz
        for z in range(nz):
            lane = pl.multiple_of((base + z) * local, local)
            attn_ref[:, pl.ds(lane, local)] = got_ref[z, 0] if block == 0 else far_ref[z]
    middle = first_ref[...] + (dot(attn_ref[...], weight_ref[...], NT) + vec_ref[4:5, :])
    middle_ref[...] = middle
    unit, scale = normalize(middle)
    unit_ref[...] = unit
    scale_ref[...] = scale
    normed_ref[...] = (unit * vec_ref[5:6, :] + vec_ref[6:7, :]).astype(BF16)


def project(at, got, far, weight, first, vecs):
    rows, width = first.shape
    return local_kernel(
        project_kernel,
        "project",
        (
            shape((rows, width)),
            shape((rows, width), F32),
            shape((rows, 1), F32),
            shape((rows, width)),
            shape((rows, width), F32),
        ),
        (at, got, far, weight, first, vecs),
    )


def feed_kernel(bias_ref, own_ref, near_ref, far_ref, gz_ref, weight, *refs):
    normed_ref, act_ref, gh_ref, sum_ref, keep_n_ref, send_n_ref, keep_o_ref, send_o_ref = refs
    rows = own_ref.shape[0]
    hidden_size = act_ref.shape[1]
    normed_ref[:rows, :] = own_ref[...]
    normed_ref[rows : 2 * rows, :] = near_ref[...]
    normed_ref[2 * rows :, :] = far_ref[...]
    step = 1024
    for n in range(hidden_size // step):
        up = slice(n * step, (n + 1) * step)
        down = slice(hidden_size + n * step, hidden_size + (n + 1) * step)
        value = dot(normed_ref[...], weight[:, up]) + bias_ref[:, up]
        cdf = 0.5 * (1.0 + lax.erf(value * (0.5**0.5)))
        act = (value * cdf).astype(BF16)
        slope = cdf + value * (jnp.exp(-0.5 * value * value) * ((0.5 / jnp.pi) ** 0.5))
        low = (dot(gz_ref[...], weight[:, down]) * slope).astype(BF16)
        act_ref[:, up] = act
        gh_ref[:, up] = low
        sum_ref[:, up] = jnp.sum(low.astype(F32), axis=0, keepdims=True)
        add_back = dot(low, weight[:, up], NT)
        add_out = dot(act, weight[:, down], NT)
        back = add_back if n == 0 else back + add_back
        out = add_out if n == 0 else out + add_out
    keep_n_ref[...] = back[: 2 * rows]
    send_n_ref[...] = back[2 * rows :].astype(BF16)
    keep_o_ref[...] = out[: 2 * rows]
    send_o_ref[...] = out[2 * rows :].astype(BF16)


def feed(bias, own, near, far, gz, weight):
    count, width = gz.shape
    hidden_size = bias.shape[1]
    half = count // 2
    return local_kernel(
        feed_kernel,
        "feed",
        (
            shape((count, width)),
            shape((count, hidden_size)),
            shape((count, hidden_size)),
            shape((1, hidden_size), F32),
            shape((half, width), F32),
            shape((half, width)),
            shape((half, width), F32),
            shape((half, width)),
        ),
        (bias, own, near, far, gz, weight),
        scalars=0,
        megabytes=56,
    )


def outer_kernel(part, at_ref, normed_ref, gh_ref, gz_ref, act_ref, keep_ref, send_ref, made):
    hidden_size = gh_ref.shape[1]
    chips = keep_ref.shape[0] // part
    step = 1024
    for base, left_ref, right_ref in ((0, normed_ref, gh_ref), (hidden_size, gz_ref, act_ref)):
        for n in range(hidden_size // step):
            made[...] = dot(left_ref[...], right_ref[:, n * step : (n + 1) * step], TN)
            lanes = slice(base + n * step, base + (n + 1) * step)
            for p in range(2):

                def store(ref, p=p, lanes=lanes):
                    for i in range(chips):
                        block = made[(2 * i + p) * part : (2 * i + p + 1) * part, :]
                        ref[i * part : (i + 1) * part, lanes] = block.astype(BF16)

                pl.when(at_ref[2] == p)(functools.partial(store, keep_ref))
                pl.when(at_ref[2] != p)(functools.partial(store, send_ref))


def outer(at, part, normed, gh, gz, act):
    width = normed.shape[1]
    out = shape((width // 2, 2 * gh.shape[1]))
    return local_kernel(
        functools.partial(outer_kernel, part),
        "outer",
        (out, out),
        (at, normed, gh, gz, act),
        scratch=[pltpu.VMEM((width, 1024), F32)],
    )


def branch_kernel(at_ref, half_ref, near_ref, unit_ref, scale_ref, vec_ref, gz_ref, weight_ref, *refs):
    middle_ref, branch_ref, mine_ref, send_ref, sum_ref = refs
    rows = half_ref.shape[0] // 2
    nz, _, local = mine_ref.shape
    c = at_ref[2]
    grad = half_ref[:rows, :] + near_ref[...].astype(F32)
    top = gz_ref[...].astype(F32)
    unit = unit_ref[...]
    middle = top + norm_back(unit, scale_ref[...], vec_ref[5:6, :], grad)
    middle_ref[...] = middle
    low = middle.astype(BF16)
    branch_ref[...] = low
    made = dot(low, weight_ref[...]).astype(BF16)
    for h in range(2):
        for z in range(nz):
            block = made[:, (h * nz + z) * local : (h * nz + z + 1) * local]

            @pl.when(c == h)
            def _():
                mine_ref[z] = block

            @pl.when(c != h)
            def _():
                send_ref[z] = block

    sum_ref[...] = jnp.concatenate(
        [
            jnp.sum(low.astype(F32), axis=0, keepdims=True),
            jnp.sum(grad * unit, axis=0, keepdims=True),
            jnp.sum(grad, axis=0, keepdims=True),
            jnp.sum(top, axis=0, keepdims=True),
        ],
        axis=0,
    )


def branch(at, nz, half, near, unit, scale, vecs, gz, weight, before):
    rows, width = unit.shape
    local = width // (2 * nz)
    return local_kernel(
        branch_kernel,
        "branch",
        (
            shape((rows, width), F32),
            shape((rows, width)),
            shape((nz, rows, local)),
            shape((nz, rows, local)),
            shape((4, width), F32),
        ),
        (at, half, near, unit, scale, vecs, gz, weight),
        before=before,
    )


def leave_kernel(dq_ref, two_ref, near_ref, weight_ref, stack_ref, full_ref, send_ref):
    count, local = dq_ref.shape
    stack_ref[:, :local] = dq_ref[...]
    stack_ref[:, local:] = (two_ref[:count, :] + near_ref[...].astype(F32)).astype(BF16)
    full_ref[...] = dot(stack_ref[...], weight_ref[...], NT)
    send_ref[...] = full_ref[count // 2 :, :].astype(BF16)


def leave(dq, two, near, weight):
    count, local = dq.shape
    width = weight.shape[0]
    return local_kernel(
        leave_kernel,
        "leave",
        (shape((count, 3 * local)), shape((count, width), F32), shape((count // 2, width))),
        (dq, two, near, weight),
        scalars=0,
    )


def close_kernel(rows, full_ref, unit_ref, scale_ref, lead_ref, vec_ref, middle_ref, normed_ref, stack_ref, *refs):
    sum_ref, bias_ref, out_ref = refs
    count, width = full_ref.shape
    for n in range(count // rows):
        span = slice(n * rows, (n + 1) * rows)
        grad = full_ref[span, :]
        unit = unit_ref[span, :].astype(F32)
        back = norm_back(unit, scale_ref[span, :], vec_ref[2:3, :], grad)
        if n == 0:
            back = back + middle_ref[...]
        parts = (back * lead_ref[span, :], back, grad * unit, grad)
        added = [jnp.sum(block, axis=0, keepdims=True) for block in parts]
        total = added if n == 0 else [x + y for x, y in zip(total, added)]
    for n, row in enumerate(total):
        sum_ref[n : n + 1, :] = row
    bias_ref[...] = jnp.sum(stack_ref[...].astype(F32), axis=0, keepdims=True)
    out_ref[...] = dot(normed_ref[...], stack_ref[...], TN).astype(BF16)


def close(rows, full, unit, scale, lead, vecs, middle, normed, stack, before):
    width = full.shape[1]
    return local_kernel(
        functools.partial(close_kernel, rows),
        "close",
        (shape((4, width), F32), shape((1, stack.shape[1]), F32), shape((width, stack.shape[1]))),
        (full, unit, scale, lead, vecs, middle, normed, stack),
        scalars=0,
        before=before,
    )


def after(block, *before):
    return lax.optimization_barrier((block,) + before)[0]


def per_device(
    tokens,
    segment_ids,
    lead_hours,
    qkv_weight,
    qv_bias,
    proj_weight,
    proj_bias,
    up_weight,
    up_bias,
    down_weight,
    down_bias,
    norm1_gain,
    norm1_bias,
    norm2_gain,
    norm2_bias,
    lead_weight,
    lead_bias,
    out_grad,
):
    grid = Grid()
    nz, nx, chips, sp = grid.nz, grid.nx, grid.chips, grid.sp
    core, y = grid.core, grid.y
    at = jnp.stack([grid.z, grid.x, core, y]).astype(jnp.int32)
    full_rows, width = tokens.shape
    rows = full_rows // 2
    part = norm1_gain.shape[0]
    each = HD // sp
    at_home = core == y

    def split(array, axis, index):
        half = array.shape[axis] // 2
        first = lax.slice_in_dim(array, 0, half, axis=axis)
        second = lax.slice_in_dim(array, half, 2 * half, axis=axis)
        return jnp.where(index == 0, first, second), jnp.where(index == 0, second, first)

    def in_order(own, other, index):
        return jnp.where(index == 0, own, other), jnp.where(index == 0, other, own)

    shard = jnp.transpose(qkv_weight.reshape(3, part, nz, -1), (2, 1, 0, 3)).reshape(nz, part, -1)
    wq_z = [pick(shard, grid.z, 0)] + [grid.zshift(pick(shard, grid.far_z(k), 0), k) for k in range(1, nz)]

    vectors = [lead_weight, lead_bias, norm1_gain, norm1_bias, proj_bias, norm2_gain, norm2_bias, down_bias]
    n_vec = len(vectors)
    n_qv, n_up = qv_bias.size // part, up_bias.size // part
    pack = jnp.concatenate(
        [
            jnp.stack(vectors),
            qv_bias.reshape(-1, part),
            up_bias.reshape(-1, part),
            segment_ids.astype(BF16).reshape(-1, part),
        ],
        axis=0,
    )
    pack_rows = pack.shape[0]
    tall = -(-pack_rows // 16) * 16
    pack = jnp.pad(pack, ((0, rows - pack_rows), (63, 128 - 64 - part)))
    own_segments = split(segment_ids, 0, y)[0]
    beside = jnp.concatenate([own_segments.astype(BF16)[:, None], pack], axis=1)
    own_tokens = jnp.concatenate([split(tokens, 0, y)[0], beside], axis=1)
    token_far = [grid.zshift(own_tokens, k) for k in range(1, nz)]
    token_z = jnp.stack([own_tokens] + token_far)
    token_c = grid.cswap(token_z)
    packs_own = jnp.stack([token_z[:, :tall, width:], token_c[:, :tall, width:]])
    packs_far = [grid.xshift(packs_own, j) for j in range(1, nx)]

    wq_z = jnp.stack(wq_z)
    wq_x = jnp.stack([wq_z] + [grid.xshift(wq_z, j) for j in range(1, nx)])
    wq_spin, wq_cross = grid.spin(wq_x), grid.cross(wq_x)
    wq_same = jnp.where(at_home, wq_x, wq_spin)
    wq_other = jnp.where(at_home, wq_spin, wq_cross)

    normed_one, unit_one, scale_one, lead, embedded, vecs, w_qkv, q_raw, kv = enter(
        at, lead_hours, [own_tokens] + token_far + [token_c], packs_far, wq_same, wq_other, n_vec, part
    )
    local = q_raw.shape[1]
    kv_far = grid.yswap(kv)
    kv_pieces = [kv, kv_far]
    for j in range(1, nx):
        kv_pieces += [grid.xshift(kv, j), grid.xshift(kv_far, j)]

    table = jnp.stack([packs_own] + packs_far)[:, :, :, n_vec:pack_rows, 64 : 64 + part].reshape(sp, -1)
    n = jnp.arange(sp)
    rel_j, rel_r, rel_k = n // (2 * nz), (n // nz) % 2, n % nz
    device = (grid.far_z(-rel_k) * nx + grid.far_x(-rel_j)) * 2 + (core + rel_r) % 2
    in_place = (jnp.arange(sp)[:, None] == device[None, :]).astype(BF16)
    table = dot(in_place, table).reshape(sp, -1, part)
    heads_local = qv_bias.shape[1]
    qv_all = jnp.transpose(table[:, :n_qv].reshape(sp, 2, heads_local, -1), (1, 2, 0, 3)).reshape(2, heads_local * HD)
    qv_far = grid.yswap(qv_all)
    qv_full = pick(jnp.where(at_home, qv_all, qv_far).reshape(2, nz, -1), grid.z, 1)
    seg_rows = table[:, n_qv + n_up :].reshape(sp * 2, rows)
    n = jnp.arange(nx * 2 * 2 * nz)
    k, r, w, j = n % nz, (n // nz) % 2, (n // (2 * nz)) % 2, n // (4 * nz)
    key_at = ((grid.far_z(-k) * nx + grid.far_x(-j)) * 2 + (core + r) % 2) * 2 + (y + w) % 2
    take = (key_at[:, None] == jnp.arange(2 * sp)[None, :]).astype(BF16)
    key_seg = dot(take, seg_rows.astype(BF16)).astype(jnp.int32).reshape(-1)
    query_seg = key_seg[: 2 * nz * rows]
    lanes = jnp.arange(2 * HD, dtype=jnp.int32) % HD
    kcode = jnp.where(key_seg[:, None] == lanes[None, :], 0.0, EXCLUDED).astype(BF16)
    qcode = (query_seg[:, None] == lanes[None, :]).astype(BF16)
    up_all = jnp.transpose(table[:, n_qv : n_qv + n_up].reshape(sp, up_bias.shape[0], -1), (1, 0, 2)).reshape(1, -1)
    up_full = split(up_all, 1, core)[0]

    up_shard, down_shard, _ = lax.optimization_barrier((up_weight, down_weight, wq_z))
    up_keep, up_send = split(up_shard, 1, core)
    down_keep, down_send = split(jnp.transpose(down_shard), 1, core)
    ff_far = grid.cswap(jnp.concatenate([up_send, down_send], axis=1))
    ff = jnp.concatenate(in_order(jnp.concatenate([up_keep, down_keep], axis=1), ff_far, core), axis=0)
    w_ff = lax.all_gather(after(ff, *token_far), ("z", "x"), axis=0, tiled=True)

    gz_own, gz_far = split(after(out_grad, kv), 0, y)
    gz_two = jnp.concatenate([gz_own, gz_far], axis=0)
    gz = jnp.concatenate([gz_two, grid.cswap(gz_two)], axis=0)

    wp = jnp.transpose(after(proj_weight, wq_spin, token_c))
    wp_z = jnp.stack([wp] + [grid.zshift(wp, k) for k in range(1, nz)])
    wp_z = after(wp_z, kv)
    wp_x = jnp.stack([wp_z] + [grid.xshift(wp_z, j) for j in range(1, nx)])
    wp_x = after(wp_x, kv_far)
    wp_own = jnp.stack([wp_x, grid.yswap(wp_x)])
    w_proj = whole_proj(at, wp_own, grid.cswap(wp_own))

    q_raw, up_full, gz = lax.optimization_barrier((q_raw, up_full, gz))
    attn_full, lse, q, attn_send = attend(at, nz, q_raw, qv_full, qcode, kcode, kv_pieces)
    attn_got = lax.all_to_all(attn_send, "z", 0, 0, tiled=True)
    attn_far = grid.cswap(attn_got[:, 1])
    attn_out, n2, s2, normed, middle = project(at, attn_got, attn_far, w_proj, embedded, vecs)
    near = grid.yswap(normed)
    far = grid.cswap(jnp.concatenate([normed, near], axis=0))
    normed_two, active, grad_hidden, up_sum, keep_n, send_n, keep_o, send_o = feed(up_full, normed, near, far, gz, w_ff)

    half_n = keep_n + grid.cswap(send_n).astype(F32)
    near_n = grid.yswap(half_n[rows:].astype(BF16))
    d_outer, d_send = outer(at, part, normed_two, grad_hidden, gz, active)
    d_both = jnp.concatenate([d_outer, grid.cswap(d_send)], axis=1)
    d_ff = lax.psum_scatter(d_both, ("z", "x"), scatter_dimension=0, tiled=True)
    grad_middle, grad_branch, mine, send, sums_two = branch(
        at, nz, half_n, near_n, n2, s2, vecs, gz[:rows], w_proj, (d_outer,)
    )
    theirs = grid.cswap(send)
    got = lax.all_to_all(jnp.stack([mine, theirs], axis=1), "z", 0, 0, tiled=True)

    back = attend_back(at, nz, q, qcode, kcode, got, attn_full, lse, kv_pieces)
    grad_q, grad_kv = back[0], back[1].astype(F32)
    for j in range(1, nx):
        grad_kv = grad_kv + grid.xshift(back[1 + j], -j).astype(F32)
    count = 2 * nz * rows
    near_kv = grid.yswap(grad_kv[count:].astype(BF16))
    grad_stack, part_full, part_send = leave(grad_q, grad_kv, near_kv, w_qkv)

    part_n1 = (part_full[: nz * rows] + grid.cswap(part_send).astype(F32)).reshape(nz, rows, width)
    low = part_n1.astype(BF16)
    n1_far = [grid.zshift(low[k], -k) for k in range(1, nz)]

    sums_one, stack_sum, d_wqkv = close(
        rows, part_full, unit_one, scale_one, lead, vecs, grad_middle, normed_one, grad_stack, (low,)
    )
    up_column = jnp.transpose(up_sum.reshape(-1, sp, each), (1, 0, 2)).reshape(1, -1)
    sums = jnp.concatenate([sums_one, sums_two, up_column], axis=0)
    sums_far = grid.cswap(sums)
    up_both = jnp.concatenate(in_order(sums[n_vec:], sums_far[n_vec:], core), axis=0)
    sums = jnp.concatenate(
        [sums[:n_vec] + sums_far[:n_vec], jnp.where(y == 0, up_both, 0.0), jnp.where(y == 0, 0.0, up_both)], axis=0
    )
    n_sums = n_vec + 4
    qv_sum = jnp.concatenate([stack_sum[0, :local], stack_sum[0, 2 * local :]]).reshape(-1, sp, each)
    n_bias = qv_sum.shape[0] * each
    qv_column = jnp.pad(jnp.transpose(qv_sum, (1, 0, 2)).reshape(sp, n_bias), ((0, 0), (0, part - n_bias)))
    columns = jnp.concatenate([jnp.transpose(sums), qv_column.reshape(-1, 1)], axis=1).astype(BF16)
    columns = jnp.pad(columns, ((0, 0), (0, 128 - columns.shape[1])))
    dw = jnp.concatenate([d_wqkv, columns], axis=1).reshape(nz, nx, 2, part, -1)
    dw_same, dw_other = pick(dw, core, 2), pick(dw, 1 - core, 2)
    from_spin = grid.spin(jnp.where(at_home, dw_other, dw_same), back=True)
    from_cross = grid.cross(dw_other)
    dw = from_spin.astype(F32) + jnp.where(at_home, dw_same, from_cross).astype(F32)
    dw_low = dw.astype(BF16)
    dw = pick(dw, grid.x, 1)
    for j in range(1, nx):
        dw = dw + grid.xshift(pick(dw_low, grid.far_x(j), 1), j).astype(F32)
    dw = lax.all_to_all(dw.astype(BF16), "z", 0, 0, tiled=True)
    g_qkv = place_qkv([dw[k] for k in range(nz)], [jnp.int32(k * local) for k in range(nz)], local)
    tails = dw[:, :, 3 * local :].astype(F32)
    sums = jnp.transpose(jnp.sum(tails[:, :, :n_sums], axis=0))
    up_rows = jnp.where(y == 0, sums[n_vec : n_vec + 2], sums[n_vec + 2 : n_vec + 4])
    g_up_bias = up_rows.reshape(-1, each)
    qv_tail = tails[:, :n_bias, n_sums].reshape(nz, 2, -1, each)
    g_qv_bias = jnp.transpose(qv_tail, (1, 0, 2, 3)).reshape(2, -1, each)

    grad_n1 = part_n1[0]
    for block in n1_far:
        grad_n1 = grad_n1 + block.astype(F32)
    input_grad = grad_middle + norm_back(unit_one[:rows].astype(F32), scale_one[:rows], vecs[2], grad_n1)
    input_grad = input_grad.astype(BF16)
    input_grad = jnp.concatenate(in_order(input_grad, grid.yswap(input_grad), y), axis=0).astype(F32)

    half_o = keep_o + grid.cswap(after(send_o, grad_branch)).astype(F32)
    block_out = half_o[:rows] + grid.yswap(half_o[rows:].astype(BF16)).astype(F32)
    block_out = (middle + (block_out + vecs[7])).astype(BF16)
    block_out = jnp.concatenate(in_order(block_out, grid.yswap(block_out), y), axis=0)
    dp = dot(grad_branch, after(attn_out, got), TN).astype(BF16).reshape(chips, 2, part, -1)
    dp = pick(dp, core, 1).astype(F32) + grid.cswap(pick(dp, 1 - core, 1)).astype(F32)
    dp_keep, dp_send = split(dp, 2, y)
    dp = dp_keep + grid.yswap(dp_send.astype(BF16)).astype(F32)
    d_proj = grid.scatter(dp.astype(BF16).reshape(nz, nx, part, -1))

    n_cols = 2 * grad_hidden.shape[1]
    low_cols, high_cols = in_order(d_ff[:, :n_cols], d_ff[:, n_cols:], core)
    n_hidden = grad_hidden.shape[1]
    d_up = jnp.concatenate([low_cols[:, :n_hidden], high_cols[:, :n_hidden]], axis=1).astype(F32)
    d_down = jnp.concatenate([low_cols[:, n_hidden:], high_cols[:, n_hidden:]], axis=1).astype(F32)
    return (
        block_out,
        input_grad,
        g_qkv,
        g_qv_bias,
        jnp.transpose(d_proj),
        sums[4],
        d_up,
        g_up_bias,
        jnp.transpose(d_down),
        sums[7],
        sums[2],
        sums[3],
        sums[5],
        sums[6],
        sums[0],
        sums[1],
    )


def solution(mesh):
    sp = mesh.shape["sp"]
    nz = 4
    devices = mesh.devices.reshape(nz, sp // (2 * nz), 2, mesh.shape["tp"])
    fine = jax.sharding.Mesh(devices, SP + ("tp",))
    line = P(SP)
    placed = (
        P(SP, None),
        line,
        P(),
        P(None, SP, "tp"),
        P(None, "tp", SP),
        P("tp", SP),
        line,
        P(SP, "tp"),
        P("tp", SP),
        P("tp", SP),
    ) + (line,) * 7 + (P(SP, None),)
    given = (
        P(SP, None),
        P(SP, None),
        P(None, SP, "tp"),
        P(None, "tp", SP),
        P("tp", SP),
        line,
        P(SP, "tp"),
        P("tp", SP),
        P("tp", SP),
    ) + (line,) * 7
    return jax.shard_map(per_device, mesh=fine, in_specs=placed, out_specs=given, check_vma=False)
```
